32 devices in a mesh: dp: 8 (over z, x), blk: 4 (over y, core).
Axes of the slice: x: 2, y: 2, z: 4, core: 2. Of those that a mesh axis runs over, the one named last changes fastest.
Arguments:
- tokens: bfloat16 [2, 8, 512, 768], P(None, 'dp', 'blk'), may hold values from -6 to 6
- timesteps: int32 [2, 8], P(None, 'dp'), may hold values from 0 to 999
- routes: int32 [2, 8, 512, 2], P(None, 'dp', 'blk'), may hold values from 0 to 3, all different within a row; in each aligned block of 128 rows (0 to 127, 128 to 255, ..., all dimensions but the last counted through in order) at most 68 rows name the same one
- ada_weight: bfloat16 [768, 4608], P('dp', 'blk'), may hold values from -0.3125 to 0.3125
- qkv_weight: bfloat16 [768, 2304], P('dp', 'blk'), may hold values from -0.21875 to 0.21875
- out_weight: bfloat16 [768, 768], P('dp', 'blk'), may hold values from -0.3125 to 0.3125
- router_weight: bfloat16 [768, 4], P('dp', 'blk'), may hold values from -0.109375 to 0.109375
- shared_in_weight: bfloat16 [768, 3072], P('dp', 'blk'), may hold values from -0.21875 to 0.21875
- shared_out_weight: bfloat16 [3072, 768], P('blk', 'dp'), may hold values from -0.109375 to 0.109375
- expert_in_weight: bfloat16 [4, 768, 3072], P('blk', 'dp'), may hold values from -0.21875 to 0.21875
- expert_out_weight: bfloat16 [4, 3072, 768], P('blk', None, 'dp'), may hold values from -0.109375 to 0.109375
- cotangent: bfloat16 [2, 8, 512, 768], P(None, 'dp', 'blk'), may hold values from -6 to 6
Outputs:
- block_out: bfloat16 [2, 8, 512, 768], P(None, 'dp', 'blk')
- tokens_grad: float32 [2, 8, 512, 768], P(None, 'dp', 'blk')
- ada_grad: float32 [768, 4608], P('dp', 'blk')
- qkv_grad: float32 [768, 2304], P('dp', 'blk')
- out_grad: float32 [768, 768], P('dp', 'blk')
- router_grad: float32 [768, 4], P('dp', 'blk')
- shared_in_grad: float32 [768, 3072], P('dp', 'blk')
- shared_out_grad: float32 [3072, 768], P('blk', 'dp')
- expert_in_grad: float32 [4, 768, 3072], P('blk', 'dp')
- expert_out_grad: float32 [4, 3072, 768], P('blk', None, 'dp')
The draws below stay inside these ranges and needn't reach their ends.
Inputs may be any that keep to these rules, and one draw needn't show every extreme that they name: `routes`: each row names 2 different experts. In every aligned block of 128 rows (the patches of one device in one micro-batch) no expert is named more than 68 times, and in every draw some block names some expert exactly 68 times.
All inputs are finite; a program needn't handle non-finite values.
Results may differ from the reference program's by a relative error of at most 0.017.
Values may be sent and summed in bfloat16 or wider, within the bound.
No kernel may reach another device: no remote copies, remote signals or barrier semaphores. Data moves between devices by JAX's collectives and lax.ppermute only.
A program may use at most 256 MiB of HBM per device.

```python
import functools
import math
import jax
import jax.numpy as jnp
import numpy as np
from jax import lax

D = 768
HEADS = 12
HEAD_DIM = 64
FF = 3072
LEN_DEV = 128
MICRO = 2
TOP = 2
EXPERTS = 4
SEQ = 512
ITEMS = 8
CAP = 68
N_BLK = 4


def place_ends(values, key, least, high):
    place = [jax.random.randint(jax.random.fold_in(key, axis), (), 0, length) for axis, length in enumerate(values.shape)]
    longest = values.shape.index(max(values.shape))
    next_to = place[:longest] + [(place[longest] + 1) % values.shape[longest]] + place[longest + 1:]
    return values.at[tuple(place)].set(least).at[tuple(next_to)].set(high)


def raised(values, stream_key, source, target, shards_of, factor):
    def block_of(axis_at):
        return (jnp.arange(values.shape[axis_at]) // (values.shape[axis_at] // shards_of)).reshape((-1,) + (1,) * (values.ndim - 1 - axis_at))

    near = jax.random.permutation(stream_key, shards_of)[block_of(target)]
    second = (block_of(target) + shards_of // 2) % shards_of
    return jnp.where((block_of(source) == near) | (block_of(source) == second), factor * values, values)


def steps_of(key, shape, cuts, smallest, top_value):
    gain, own = 1.0, jax.random.fold_in(key, 6)
    for dim, shards_of in cuts:
        heights = jnp.exp(jax.random.uniform(jax.random.fold_in(own, dim), (shards_of,), jnp.float32, smallest / len(cuts), top_value / len(cuts)))
        gain = gain * jnp.repeat(heights, shape[dim] // shards_of).reshape([-1 if axis == dim else 1 for axis in range(len(shape))])
    return gain


def routed_block(own_key, own, number, rows, amount, top, most, skew):
    order = jax.random.permutation(own_key, amount)
    packed, usual = portions_of(amount, rows * top, most, skew, True), portions_of(amount, rows * top, most, skew, False)
    places = jnp.arange(amount)

    def named(lengths, offset_by):
        used = int((lengths > 0).sum())
        fixed = max(1, used // 4)
        shifted = fixed + (places - fixed + offset_by * (used - fixed)) % max(1, amount - fixed)
        return jnp.zeros((amount,), jnp.int32).at[order[jnp.where(places < fixed, places, shifted)]].set(jnp.asarray(lengths, jnp.int32))

    lengths = jnp.where(number % 4 == 0, named(packed, number // 4), named(usual, number - number // 4 - 1))
    mixed = jax.random.permutation(jax.random.fold_in(own, 3), amount)
    source_of, taker = mixed[0:amount // 2 * 2:2], mixed[1:amount // 2 * 2:2]
    slack = jnp.minimum(lengths[source_of] - 1, most - lengths[taker]) // 2
    slack = jnp.where((source_of == order[0]) | (taker == order[0]) | (lengths[taker] == 0), 0, jnp.maximum(slack, 0))
    shifted = jax.random.randint(jax.random.fold_in(own, 4), (amount // 2,), 0, 1 << 20) % (slack + 1)
    lengths = lengths.at[source_of].add(-shifted).at[taker].add(shifted)
    members = jnp.searchsorted(jnp.cumsum(lengths), jnp.arange(rows * top), side="right").astype(jnp.int32)
    listing = members.reshape(top, rows).T
    listing = listing[jax.random.permutation(jax.random.fold_in(own, 1), rows)]
    offset_by = jax.random.randint(jax.random.fold_in(own, 2), (rows, 1), 0, top)
    return jnp.take_along_axis(listing, (jnp.arange(top)[None, :] + offset_by) % top, axis=1)


def portions_of(amount, total, reach, slope, full):
    portions = [(1 << 20) // math.isqrt(standing ** slope) + 1 for standing in range(1, amount + 1)]
    largest = reach if full else min(reach, max(-(-total // amount), total * portions[0] // sum(portions)))
    least = 1 if total - largest >= amount - 1 else 0
    counts, spare = [largest] + [least] * (amount - 1), total - largest - least * (amount - 1)
    while spare > 0:
        free = [i for i in range(1, amount) if counts[i] < largest] or [i for i in range(1, amount) if counts[i] < reach]
        mass, budget = sum([portions[i] for i in free]), spare
        for i in free:
            addition = min(reach - counts[i], max(1, budget * portions[i] // mass), spare)
            counts[i] = counts[i] + addition
            spare = spare - addition
    return np.array(counts)


def bell_draw(key, extent, deviation, bound, cuts=(), held_as=jnp.bfloat16):
    entries = jax.random.normal(key, extent, jnp.float32) * deviation
    if len(cuts) > 0:
        entries = steps_of(key, extent, cuts, -0.22, 0.18) * entries
    return jnp.clip(entries, min=-bound, max=bound).astype(held_as)


def bell_draw_with(rng, dims, deviation, most, cuts, heavy, kind=jnp.bfloat16):
    entries = deviation * jax.random.normal(rng, dims, jnp.float32)
    if cuts:
        entries = entries * steps_of(rng, dims, cuts, -0.22, 0.18)
    return jnp.clip(raised(entries, jax.random.fold_in(rng, 3), *heavy), -most, most).astype(kind)


def setup_inputs(seed: int = 0) -> dict:
    arg_keys = jax.random.split(jax.random.key(seed), 13)
    tokens = bell_draw(arg_keys[0], (MICRO, ITEMS, SEQ, D), 1.0, 6.0, ((1, 8), (2, 4)))
    timesteps = place_ends(jax.random.randint(arg_keys[1], (MICRO, ITEMS), 0, 1000), jax.random.fold_in(arg_keys[1], 1), 0, 999).astype(jnp.int32)
    routes_keys = jax.random.split(jax.random.fold_in(arg_keys[2], 1), MICRO * ITEMS * SEQ // LEN_DEV)
    routes_turns = jax.random.permutation(jax.random.fold_in(arg_keys[2], 3), MICRO * ITEMS * SEQ // LEN_DEV)
    routes = jax.vmap(lambda own, number: routed_block(jax.random.fold_in(arg_keys[2], 2), own, number, LEN_DEV, EXPERTS, TOP, CAP, 1))(routes_keys, routes_turns).reshape((MICRO, ITEMS, SEQ, TOP))
    ada_weight = bell_draw(arg_keys[3], (D, 6 * D), (D // 2) ** -0.5, 0.3125, ((0, 8), (1, 4)))
    qkv_weight = bell_draw(arg_keys[4], (D, 3 * D), D ** -0.5, 0.21875, ((0, 8), (1, 4)))
    out_weight = bell_draw(arg_keys[5], (D, D), (D // 2) ** -0.5, 0.3125, ((0, 8), (1, 4)))
    router_weight = bell_draw(arg_keys[6], (D, EXPERTS), (4 * D) ** -0.5, 0.109375, ((0, 8), (1, 4)))
    shared_in_weight = bell_draw(arg_keys[7], (D, FF), D ** -0.5, 0.21875, ((0, 8), (1, 4)))
    shared_out_weight = bell_draw(arg_keys[8], (FF, D), FF ** -0.5, 0.109375, ((0, 4), (1, 8)))
    expert_in_weight = bell_draw(arg_keys[9], (EXPERTS, D, FF), D ** -0.5, 0.21875, ((0, 4), (1, 8)))
    expert_out_weight = bell_draw(arg_keys[10], (EXPERTS, FF, D), FF ** -0.5, 0.109375, ((0, 4), (2, 8)))
    cotangent = bell_draw_with(arg_keys[11], (MICRO, ITEMS, SEQ, D), 1.0, 6.0, ((1, 8), (2, 4)), (1, 3, 8, 2.0))
    return {"tokens": tokens, "timesteps": timesteps, "routes": routes, "ada_weight": ada_weight, "qkv_weight": qkv_weight, "out_weight": out_weight, "router_weight": router_weight, "shared_in_weight": shared_in_weight, "shared_out_weight": shared_out_weight, "expert_in_weight": expert_in_weight, "expert_out_weight": expert_out_weight, "cotangent": cotangent}


@jax.custom_vjp
def low(v):
    return lax.optimization_barrier(v.astype(jnp.bfloat16)).astype(jnp.float32)

@jax.custom_vjp
def low_back(v):
    return v

def low_keep(v):
    return (low(v), None)

def low_pass(kept, grad):
    return (grad,)

def back_keep(v):
    return (v, None)

def back_low(kept, grad):
    return (low(grad),)
low.defvjp(low_keep, low_pass)
low_back.defvjp(back_keep, back_low)
eps_norm = 1e-06
highest = lax.Precision.HIGHEST

def matmul(left, right):
    return jnp.dot(left, right, precision=highest)

def modulate(row_values, row_shift, row_scale):
    row_mean = lax.optimization_barrier(jnp.mean(row_values, axis=-1, keepdims=True))
    centered = row_values - row_mean
    row_var = lax.optimization_barrier(jnp.mean(centered * centered, axis=-1, keepdims=True))
    return centered * lax.rsqrt(row_var + eps_norm) * (1.0 + row_scale) + row_shift

def timestep_features(step_index, feature_width):
    half_width = feature_width // 2
    frequency = jnp.exp(-math.log(10000.0) * jnp.arange(half_width, dtype=jnp.float32) / half_width)
    angles = step_index.astype(jnp.float32) * frequency
    return jnp.concatenate([jnp.cos(angles), jnp.sin(angles)])

def gelu_tanh(values_in):
    return jax.nn.gelu(values_in, approximate=True)

def slot_tables(routing, experts, capacity):
    flat_ids = routing.reshape(-1)
    pair_count = flat_ids.shape[0]
    onehot = (flat_ids[:, None] == jnp.arange(experts, dtype=jnp.int32)[None, :]).astype(jnp.int32)
    before = jnp.cumsum(onehot, axis=0) - onehot
    position = lax.optimization_barrier(jnp.sum(before * onehot, axis=1))
    slot_index = flat_ids * capacity + position
    sources = jnp.full((experts * capacity,), pair_count, jnp.int32).at[slot_index].set(jnp.arange(pair_count, dtype=jnp.int32))
    filled = sources < pair_count
    return (slot_index, jnp.minimum(sources, pair_count - 1), filled)

def take_rows(matrix, index_rows):
    return matrix[index_rows]

def to_float(array):
    return array.astype(jnp.float32)

def reference(tokens, timesteps, routes, ada_weight, qkv_weight, out_weight, router_weight, shared_in_weight, shared_out_weight, expert_in_weight, expert_out_weight, cotangent):
    capacity = CAP
    items_all = MICRO * ITEMS
    score_scale = 1.0 / math.sqrt(HEAD_DIM)
    tokens_f = tokens.astype(jnp.float32).reshape(items_all, SEQ, D)
    steps_flat = timesteps.reshape(items_all).astype(jnp.int32)
    routes_flat = routes.reshape(items_all, SEQ, TOP).astype(jnp.int32)
    table_fn = functools.partial(slot_tables, experts=EXPERTS, capacity=capacity)
    slot_maps, source_maps, filled_maps = jax.vmap(jax.vmap(table_fn))(routes_flat.reshape(items_all, N_BLK, LEN_DEV, TOP))

    def forward(tokens_all, ada, qkv, out_w, router, shared_in, shared_out, expert_in, expert_out):

        def one_item(operands):
            row_values, step_index, routing, slot_map, source_map, filled_map = operands
            cond_act = low(jax.nn.silu(timestep_features(step_index, D)))
            modulation = matmul(cond_act[None, :], ada)[0]
            shift_one, scale_one, gate_one, shift_two, scale_two, gate_two = jnp.split(modulation, 6)
            normed_one = low(modulate(row_values, shift_one, scale_one))
            projected = low_back(low(matmul(normed_one, qkv)))
            queries, keys_all, values_all = jnp.split(projected, 3, axis=1)
            queries = queries.reshape(SEQ, HEADS, HEAD_DIM)
            keys_all = keys_all.reshape(SEQ, HEADS, HEAD_DIM)
            values_all = values_all.reshape(SEQ, HEADS, HEAD_DIM)
            scores = low_back(jnp.einsum('qhd,khd->hqk', queries, keys_all, precision=highest) * score_scale)
            probs = low(jax.nn.softmax(scores, axis=-1))
            mixed_heads = low_back(low(jnp.einsum('hqk,khd->qhd', probs, values_all, precision=highest).reshape(SEQ, D)))
            attended = low_back(matmul(mixed_heads, out_w))
            residual = row_values + gate_one * attended
            normed_two = low(modulate(residual, shift_two, scale_two))
            logits = low_back(matmul(normed_two, router))
            gate_probs = jax.nn.softmax(jnp.take_along_axis(logits, routing, axis=1), axis=-1)
            shared_pre = low_back(matmul(normed_two, shared_in))
            shared_val = low_back(matmul(low(gelu_tanh(shared_pre)), shared_out))
            blocks = normed_two.reshape(N_BLK, LEN_DEV, D)
            gathered = jax.vmap(take_rows)(blocks, source_map // TOP)
            buffers = jnp.where(filled_map[:, :, None], gathered, 0.0).reshape(N_BLK, EXPERTS, capacity, D)
            expert_pre = low_back(jnp.einsum('becd,edf->becf', buffers, expert_in, precision=highest))
            expert_act = low(gelu_tanh(expert_pre))
            expert_val = low_back(low(jnp.einsum('becf,efd->becd', expert_act, expert_out, precision=highest)))
            expert_val = expert_val.reshape(N_BLK, EXPERTS * capacity, D)
            routed = jax.vmap(take_rows)(expert_val, slot_map).reshape(SEQ, TOP, D)
            mixture = shared_val + lax.optimization_barrier(jnp.sum(gate_probs[:, :, None] * routed, axis=1))
            return residual + gate_two * mixture
        return lax.map(jax.checkpoint(one_item), (tokens_all, steps_flat, routes_flat, slot_maps, source_maps, filled_maps))
    weights_f = jax.tree.map(to_float, (ada_weight, qkv_weight, out_weight, router_weight, shared_in_weight, shared_out_weight, expert_in_weight, expert_out_weight))
    outputs, pullback = jax.vjp(forward, tokens_f, weights_f[0], weights_f[1], weights_f[2], weights_f[3], weights_f[4], weights_f[5], weights_f[6], weights_f[7])
    grads = pullback(cotangent.astype(jnp.float32).reshape(items_all, SEQ, D))
    block_out = outputs.reshape(MICRO, ITEMS, SEQ, D).astype(jnp.bfloat16)
    tokens_grad = grads[0].reshape(MICRO, ITEMS, SEQ, D)
    return (block_out, tokens_grad, grads[1], grads[2], grads[3], grads[4], grads[5], grads[6], grads[7], grads[8])
```

```python
import functools
import math

import jax
import jax.numpy as jnp
from jax import lax
from jax.experimental import pallas as pl
from jax.experimental.pallas import tpu as pltpu
from jax.sharding import PartitionSpec as P

D = 768
HEADS = 12
HEAD_DIM = 64
TOP = 2
LANES = 128
F32 = jnp.float32
BF16 = jnp.bfloat16
NN = (((1,), (0,)), ((), ()))
NT = (((1,), (1,)), ((), ()))
TN = (((0,), (0,)), ((), ()))
EPS_NORM = 1e-06
GELU_C = math.sqrt(2.0 / math.pi)
GELU_A = 0.044715
VMEM_LIMIT = 60 * 1024 * 1024


def mm(left, right, dims=NN):
    return lax.dot_general(left, right, dims, preferred_element_type=F32)


def call(kernel, out_shape, name, **kwargs):
    return pl.pallas_call(
        kernel,
        out_shape=out_shape,
        name=name,
        compiler_params=pltpu.CompilerParams(vmem_limit_bytes=VMEM_LIMIT),
        **kwargs,
    )


def smem():
    return pl.BlockSpec(memory_space=pltpu.SMEM)


def vmem():
    return pl.BlockSpec(memory_space=pltpu.VMEM)


def shaped(shape, dtype):
    return jax.ShapeDtypeStruct(shape, dtype)


class Moves:
    def __init__(self, mesh):
        self.n_dp, self.n_blk = mesh.shape["dp"], mesh.shape["blk"]
        self.ring = 4 if self.n_dp == 8 else 0
        self.rows = D // self.n_dp if self.ring else D
        self.slots = 8 if self.ring else 1

    def info(self):
        dp, blk = lax.axis_index("dp"), lax.axis_index("blk")
        if self.ring:
            z, x = dp // 2, dp % 2
            offs = [
                (2 * ((z + self.ring - step) % self.ring) + (x ^ flip)) * self.rows
                for flip in range(2)
                for step in range(self.ring)
            ]
        else:
            offs = [jnp.zeros((), jnp.int32)]
        blocks = [blk ^ rel for rel in range(self.n_blk)]
        return jnp.stack(offs + blocks).astype(jnp.int32)

    def rotate(self, array, steps=1):
        pairs = [(d, (d + 2 * steps) % self.n_dp) for d in range(self.n_dp)]
        return lax.ppermute(array, "dp", pairs)

    def swap(self, array):
        return lax.ppermute(array, "dp", [(d, d ^ 1) for d in range(self.n_dp)])

    def flip(self, array, bit):
        return lax.ppermute(array, "blk", [(b, b ^ bit) for b in range(self.n_blk)])

    def round(self, array):
        steps = [array]
        for _ in range(self.ring - 1):
            steps.append(self.rotate(steps[-1]))
        return steps

    def whole(self, shard):
        return lax.all_gather(shard, "dp", axis=0, tiled=True)[None]

    def fold_ring(self, parts):
        travelling = parts[1].astype(BF16)
        for step in range(2, self.ring + 1):
            arrived = self.rotate(travelling).astype(F32)
            total = parts[step % self.ring] + arrived
            travelling = total.astype(BF16)
        return total

    def fold_whole(self, part):
        return lax.psum_scatter(part[0], "dp", scatter_dimension=0, tiled=True).astype(F32)


def add(left, right):
    return left.astype(F32) + right.astype(F32)


def normed(rows):
    mean = jnp.mean(rows, axis=-1, keepdims=True)
    centered = rows - mean
    var = jnp.mean(centered * centered, axis=-1, keepdims=True)
    inverse = lax.rsqrt(var + EPS_NORM)
    return centered * inverse, inverse


def norm_back(hat, inverse, grad_hat):
    mean_grad = jnp.mean(grad_hat, axis=-1, keepdims=True)
    mean_both = jnp.mean(grad_hat * hat, axis=-1, keepdims=True)
    return inverse * (grad_hat - mean_grad - hat * mean_both)


def column_sum(rows):
    return jnp.sum(rows, axis=0, keepdims=True)


def assemble_kernel(moves, widths, info, *refs):
    n_in = len(refs) - len(widths)
    ins, outs = refs[:n_in], refs[n_in:]
    n_blk, slots, rows = moves.n_blk, moves.slots, moves.rows
    per = n_blk // n_in
    for rel in range(n_blk):
        block = info[slots + rel]
        source = ins[rel // per]
        for j in range(slots):
            first = pl.multiple_of(info[j], rows)
            start = 0
            for out, width in zip(outs, widths):
                out[block, pl.ds(first, rows), :] = source[rel % per, j, :, start : start + width]
                start += width


def qkv_kernel(micro, n_blk, tokens, mod, weight, normed_out, out, wide):
    length = tokens.shape[0] // micro
    for m in range(micro):
        rows = slice(m * length, (m + 1) * length)
        hat, _ = normed(tokens[rows, :].astype(F32))
        values = hat * (1.0 + mod[m, 1:2, :]) + mod[m, 0:1, :]
        normed_out[rows, :] = values.astype(BF16)
    rows = normed_out[...]
    width = weight.shape[2]
    for b in range(n_blk):
        wide[:, b * width : (b + 1) * width] = mm(rows, weight[b]).astype(BF16)
    part = D // n_blk
    for h in range(n_blk):
        for i in range(3):
            out[h, :, i * part : (i + 1) * part] = wide[:, i * D + h * part : i * D + (h + 1) * part]


def head_rows(ref, start):
    block = ref[:, :, start : start + HEAD_DIM]
    return block.reshape(block.shape[0] * block.shape[1], HEAD_DIM)


def softmax_rows(query, key):
    scores = mm(query, key, NT) * (1.0 / math.sqrt(HEAD_DIM))
    raised = jnp.exp(scores - jnp.max(scores, axis=-1, keepdims=True))
    return raised / jnp.sum(raised, axis=-1, keepdims=True)


def attend_kernel(projected, out):
    part = out.shape[2]
    sources, length = out.shape[0], out.shape[1]
    for start in range(0, part, HEAD_DIM):
        query, key, value = (head_rows(projected, i * part + start) for i in range(3))
        probs = softmax_rows(query, key).astype(BF16)
        mixed = mm(probs, value).astype(BF16)
        out[:, :, start : start + HEAD_DIM] = mixed.reshape(sources, length, HEAD_DIM)


def attend_back_kernel(projected, grad_mixed, out):
    part = grad_mixed.shape[2]
    sources, length = out.shape[0], out.shape[1]
    scale = 1.0 / math.sqrt(HEAD_DIM)
    for start in range(0, part, HEAD_DIM):
        query, key, value = (head_rows(projected, i * part + start) for i in range(3))
        grad = head_rows(grad_mixed, start)
        probs = softmax_rows(query, key)
        grad_probs = mm(grad, value, NT)
        inner = jnp.sum(probs * grad_probs, axis=-1, keepdims=True)
        grad_scores = (probs * (grad_probs - inner)).astype(BF16)
        grads = (
            mm(grad_scores, key) * scale,
            mm(grad_scores, query, TN) * scale,
            mm(probs.astype(BF16), grad, TN),
        )
        for i, part_grad in enumerate(grads):
            out[:, :, i * part + start : i * part + start + HEAD_DIM] = part_grad.astype(
                BF16
            ).reshape(sources, length, HEAD_DIM)


def pick(routes, k, count):
    lanes = lax.broadcasted_iota(jnp.int32, (routes.shape[0], count), 1)
    return lanes == routes[:, k : k + 1]


def residual_kernel(
    micro, n_blk, mixed_in, tokens, mod, out_weight, router, cotangent, routes, slots_t,
    mixed, attended, residual, normed_two, grad_shared, probs, send,
):
    part = D // n_blk
    for h in range(n_blk):
        mixed[:, h * part : (h + 1) * part] = mixed_in[h]
    all_mixed = mixed[...]
    for b in range(n_blk):
        attended[:, b * part : (b + 1) * part] = mm(all_mixed, out_weight[b])
    length = tokens.shape[0] // micro
    for m in range(micro):
        rows = slice(m * length, (m + 1) * length)
        stream = tokens[rows, :].astype(F32) + mod[m, 2:3, :] * attended[rows, :]
        residual[rows, :] = stream
        hat, _ = normed(stream)
        normed_two[rows, :] = (hat * (1.0 + mod[m, 4:5, :]) + mod[m, 3:4, :]).astype(BF16)
    rows_two = normed_two[...]
    logits = mm(rows_two, router[...], NT)
    chosen = [
        jnp.sum(jnp.where(pick(routes, k, LANES), logits, 0.0), axis=-1, keepdims=True)
        for k in range(TOP)
    ]
    top = functools.reduce(jnp.maximum, chosen)
    raised = [jnp.exp(value - top) for value in chosen]
    total = functools.reduce(jnp.add, raised)
    gates = [value / total for value in raised]
    for k in range(TOP):
        probs[:, k : k + 1] = gates[k]
    grad_mix = jnp.concatenate(
        [
            cotangent[m * length : (m + 1) * length, :].astype(F32) * mod[m, 5:6, :]
            for m in range(micro)
        ]
    )
    grad_shared[...] = grad_mix.astype(BF16)
    experts, _, room, _ = send.shape
    index = lax.broadcasted_iota(jnp.int32, (experts * room, micro * length), 0)
    holds = [(index == slots_t[k : k + 1, :]).astype(BF16) for k in range(TOP)]
    sent = mm(functools.reduce(jnp.add, holds), rows_two).astype(BF16)
    send[:, 0] = sent.reshape(experts, room, D)
    pairs = [(gates[k] * grad_mix).astype(BF16) for k in range(TOP)]
    sent = functools.reduce(jnp.add, [mm(holds[k], pairs[k]) for k in range(TOP)]).astype(BF16)
    send[:, 1] = sent.reshape(experts, room, D)


def expert_kernel(moves, maps, first, last, tile, info, rows_ref, grads_ref, *refs):
    refs = list(refs)
    acc = [] if first else [refs.pop(0), refs.pop(0)]
    weights = [refs.pop(0) for _ in maps]
    if last:
        both = refs.pop(0)
    else:
        totals = [refs.pop(0), refs.pop(0)]
    outs = [refs.pop(0) for _ in maps]
    w_in, w_out, g_in, g_out = refs[:4]
    if last:
        totals = refs[4:6]
    step = pl.program_id(0)
    rows = rows_ref[...].reshape(-1, D)
    grads = grads_ref[...].reshape(-1, D)

    @pl.when(step == 0)
    def _():
        for i in range(2):
            totals[i][...] = jnp.zeros_like(totals[i]) if first else acc[i][...]

    for ref, slots in zip(weights, maps):
        for k, j in enumerate(slots):
            at = pl.ds(pl.multiple_of(info[j], moves.rows), moves.rows)
            w_in[at, :] = ref[k, :, :tile]
            w_out[at, :] = ref[k, :, tile:]
    pre = mm(rows, w_in[...])
    squared = pre * pre
    bend = jnp.tanh(GELU_C * pre * (1.0 + GELU_A * squared))
    half = 0.5 * (1.0 + bend)
    act = (pre * half).astype(BF16)
    slope = half + 0.5 * pre * (1.0 - bend * bend) * (GELU_C * (1.0 + 3.0 * GELU_A * squared))
    totals[0][...] += mm(act, w_out[...], NT)
    grad_pre = (mm(grads, w_out[...]) * slope).astype(BF16)
    totals[1][...] += mm(grad_pre, w_in[...], NT)
    g_in[...] = mm(rows, grad_pre, TN).astype(BF16)
    g_out[...] = mm(grads, act, TN).astype(BF16)
    for ref, slots in zip(outs, maps):
        for k, j in enumerate(slots):
            at = pl.ds(pl.multiple_of(info[j], moves.rows), moves.rows)
            ref[k, :, :tile] = g_in[at, :]
            ref[k, :, tile:] = g_out[at, :]
    if last:

        @pl.when(step == pl.num_programs(0) - 1)
        def _():
            for i in range(2):
                both[:, i] = totals[i][...].astype(BF16).reshape(both.shape[0], *both.shape[2:])


def expert_part(moves, info, rows, grads, acc, weights, maps, tile, out_both, name):
    first, last = acc is None, out_both is not None
    steps = weights[0].shape[2] // (2 * tile)
    count = math.prod(rows[0].shape[i] for i in rows[2])
    kernel = functools.partial(expert_kernel, moves, maps, first, last, tile)
    w_specs = [
        pl.BlockSpec((w.shape[0], w.shape[1], 2 * tile), lambda j: (0, 0, j)) for w in weights
    ]
    in_specs = [smem(), rows[1], grads[1]]
    operands = [info, rows[0], grads[0]]
    flat = pl.BlockSpec((count, D), lambda j: (0, 0))
    if not first:
        in_specs += [flat, flat]
        operands += list(acc)
    out_specs, out_shape = [], []
    scratch = [pltpu.VMEM((D, tile), BF16) for _ in range(4)]
    if last:
        out_specs.append(pl.BlockSpec(out_both, lambda j: (0,) * len(out_both)))
        out_shape.append(shaped(out_both, BF16))
        scratch += [pltpu.VMEM((count, D), F32) for _ in range(2)]
    else:
        out_specs += [flat, flat]
        out_shape += [shaped((count, D), F32)] * 2
    results = call(
        kernel,
        out_shape + [shaped(w.shape, BF16) for w in weights],
        name,
        grid=(steps,),
        in_specs=in_specs + w_specs,
        out_specs=out_specs + w_specs,
        scratch_shapes=scratch,
        cost_estimate=pl.CostEstimate(
            flops=12 * count * D * tile * steps,
            bytes_accessed=16 * D * tile * steps,
            transcendentals=count * tile * steps,
        ),
    )(*operands, *weights)
    if last:
        return results[0], results[1:]
    return results[:2], results[2:]


def middle_kernel(
    micro, n_blk, moves, info, back, routes, slots, probs, shared_val, shared_grad, residual, attended, mixed, normed_two,
    mod, out_weight, router, cotangent,
    block_out, grad_residual, grad_mod, grad_router, out_keep, out_send, grad_mixed, grad_attended, scratch,
):
    part = D // n_blk
    length = residual.shape[0] // micro
    experts, _, room, _ = back.shape
    values = back[:, 0].reshape(experts * room, D)
    grads = back[:, 1].reshape(experts * room, D)
    index = lax.broadcasted_iota(jnp.int32, (micro * length, experts * room), 1)
    holds = [(index == slots[:, k : k + 1]).astype(BF16) for k in range(TOP)]
    routed = [mm(holds[k], values) for k in range(TOP)]
    gates = [probs[:, k : k + 1] for k in range(TOP)]
    mixture = shared_val[...] + functools.reduce(
        jnp.add, [gates[k] * routed[k] for k in range(TOP)]
    )
    given = cotangent[...].astype(F32)
    grad_gates = []
    grad_mix = []
    for m in range(micro):
        rows = slice(m * length, (m + 1) * length)
        gate = mod[m, 5:6, :]
        block_out[rows, :] = (residual[rows, :] + gate * mixture[rows]).astype(BF16)
        grad_mod[m, 3:4, :] = column_sum(given[rows] * mixture[rows])
        grad_mix.append(given[rows] * gate)
    grad_mix = jnp.concatenate(grad_mix)
    grad_gates = [jnp.sum(grad_mix * routed[k], axis=-1, keepdims=True) for k in range(TOP)]
    inner = functools.reduce(jnp.add, [gates[k] * grad_gates[k] for k in range(TOP)])
    grad_logits = functools.reduce(
        jnp.add,
        [
            jnp.where(pick(routes, k, LANES), gates[k] * (grad_gates[k] - inner), 0.0)
            for k in range(TOP)
        ],
    ).astype(BF16)
    grad_router[...] = mm(grad_logits, normed_two[...], TN)
    grad_two = (
        shared_grad[...]
        + mm(functools.reduce(jnp.add, holds), grads)
        + mm(grad_logits, router[...])
    )
    for m in range(micro):
        rows = slice(m * length, (m + 1) * length)
        hat, inverse = normed(residual[rows, :])
        own = grad_two[rows]
        grad_mod[m, 1:2, :] = column_sum(own)
        grad_mod[m, 2:3, :] = column_sum(own * hat)
        total = given[rows] + norm_back(hat, inverse, own * (1.0 + mod[m, 4:5, :]))
        grad_residual[rows, :] = total
        grad_mod[m, 0:1, :] = column_sum(total * attended[rows, :])
        grad_attended[rows, :] = (total * mod[m, 2:3, :]).astype(BF16)
    all_mixed = mixed[...]
    back_mixed = functools.reduce(
        jnp.add,
        [
            mm(grad_attended[:, b * part : (b + 1) * part], out_weight[b], NT)
            for b in range(n_blk)
        ],
    ).astype(BF16)
    for h in range(n_blk):
        grad_mixed[h] = back_mixed[:, h * part : (h + 1) * part]
    for b in range(n_blk):
        scratch[b] = mm(all_mixed, grad_attended[:, b * part : (b + 1) * part], TN).astype(BF16)
    emit(moves, info, n_blk, lambda block: scratch.at[block], out_keep, out_send)


def emit(moves, info, n_blk, source, keep, send):
    for rel in range(n_blk):
        target = send if rel % 2 else keep
        held = source(info[moves.slots + rel])
        for j in range(moves.slots):
            first = pl.multiple_of(info[j], moves.rows)
            target[rel // 2, j] = held[pl.ds(first, moves.rows), :]


def qkv_grad_kernel(n_blk, moves, info, arrived, normed_one, keep, send, wide, blocks, held):
    part = D // n_blk
    for h in range(n_blk):
        for i in range(3):
            wide[:, i * D + h * part : i * D + (h + 1) * part] = arrived[h, :, i * part : (i + 1) * part]
    width = blocks.shape[2]
    for b in range(n_blk):
        blocks[b] = wide[:, b * width : (b + 1) * width]
    rows = normed_one[...]

    def source(block):
        held[...] = mm(rows, blocks[block], TN).astype(BF16)
        return held

    emit(moves, info, n_blk, source, keep, send)


def tokens_grad_kernel(micro, n_blk, blocks, weight, tokens, mod, grad_residual, out, grad_mod):
    width = blocks.shape[2]
    grad_one = functools.reduce(
        jnp.add, [mm(blocks[b], weight[b], NT) for b in range(n_blk)]
    )
    length = tokens.shape[0] // micro
    for m in range(micro):
        rows = slice(m * length, (m + 1) * length)
        hat, inverse = normed(tokens[rows, :].astype(F32))
        own = grad_one[rows]
        grad_mod[m, 0:1, :] = column_sum(own)
        grad_mod[m, 1:2, :] = column_sum(own * hat)
        out[rows, :] = grad_residual[rows, :] + norm_back(hat, inverse, own * (1.0 + mod[m, 1:2, :]))


def by_tile(left, right, tile):
    rows, columns = left.shape
    pair = jnp.stack([left.reshape(rows, -1, tile), right.reshape(rows, -1, tile)], axis=2)
    return pair.reshape(rows, 2 * columns)


def from_tiles(packed, tile):
    rows, columns = packed.shape
    pair = packed.reshape(rows, -1, 2, tile)
    return pair[:, :, 0].reshape(rows, -1), pair[:, :, 1].reshape(rows, -1)


def slots_of(routes, experts, room):
    count = routes.shape[0]
    hot = routes[:, :, None] == jnp.arange(experts, dtype=jnp.int32)
    named = jnp.sum(hot.astype(BF16), axis=1)
    before = jnp.arange(count)[:, None] > jnp.arange(count)[None, :]
    rank = mm(before.astype(BF16), named)
    ranks = jnp.sum(jnp.where(hot, rank[:, None, :], 0.0), axis=2).astype(jnp.int32)
    return routes * room + ranks


def on_device(moves, tokens, timesteps, routes, ada, qkv, out_w, router, shared_in, shared_out, expert_in, expert_out, cotangent):
    micro, _, length, _ = tokens.shape
    count = micro * length
    n_dp, n_blk = moves.n_dp, moves.n_blk
    experts = n_blk
    capacity = length * TOP // experts + max(2, length // 32)
    room = -(-micro * capacity // 16) * 16
    shard = D // n_dp
    info = moves.info()
    dp_at = lax.axis_index("dp")

    tokens_2d = tokens.reshape(count, D)
    given = cotangent.reshape(count, D)
    routes_2d = routes.reshape(count, TOP)

    pack_a = jnp.concatenate([qkv, out_w], axis=1)
    tile = shared_in.shape[1]
    pack_b = by_tile(shared_in, shared_out.T, tile)
    ff = expert_in.shape[2]
    chunk = ff // 4
    e_out = expert_out[0].T
    packs_e = [
        by_tile(expert_in[0][:, c : c + chunk], e_out[:, c : c + chunk], tile)
        for c in range(0, ff, chunk)
    ]

    steps_all = lax.all_gather(timesteps[:, 0], "dp", axis=0)
    half = D // 2
    column = dp_at * shard + jnp.arange(shard)
    frequency = jnp.exp(-math.log(10000.0) * (column % half).astype(F32) / half)
    angles = steps_all[:, :, None].astype(F32) * frequency
    cond = jnp.where(column < half, jnp.cos(angles), jnp.sin(angles))
    cond = jax.nn.silu(cond).astype(BF16)
    partial_mod = jnp.einsum("dmr,rc->dmc", cond, ada, preferred_element_type=F32)
    wide = ada.shape[1]
    payload = jnp.concatenate(
        [
            partial_mod.reshape(n_dp, micro * wide),
            jnp.broadcast_to(router[:, 0].astype(F32)[None], (n_dp, shard)),
        ],
        axis=1,
    )
    payload = jnp.broadcast_to(payload[:, None], (n_dp, n_blk, payload.shape[1]))
    payload = payload.reshape(n_dp * n_blk, -1)
    arrived = lax.all_to_all(payload, ("dp", "blk"), 0, 0, tiled=True).reshape(n_dp, n_blk, -1)
    mod = jnp.sum(arrived[:, :, : micro * wide], axis=0).reshape(n_blk, micro, wide)
    mod = mod.transpose(1, 0, 2).reshape(micro, 6, D)
    router_t = arrived[:, :, micro * wide :].transpose(1, 0, 2).reshape(n_blk, D).astype(BF16)
    router_t = jnp.pad(router_t, ((0, LANES - n_blk), (0, 0)))

    if moves.ring:
        held = jnp.stack([moves.rotate(pack_a, s) if s else pack_a for s in range(moves.ring)])
        held = jnp.concatenate([held, moves.swap(held)])
    else:
        held = moves.whole(pack_a)
    held = held[None]
    bit = 2
    while bit < n_blk:
        held = jnp.concatenate([held, moves.flip(held, bit)])
        bit *= 2
    width_q, width_o = qkv.shape[1], out_w.shape[1]
    held = [held, moves.flip(held, 1)]
    order = [0, 2, 1, 3]
    blocks_info = jnp.concatenate(
        [info[: moves.slots], info[moves.slots :][jnp.array(order)]]
    )
    qkv_w, out_full = call(
        functools.partial(assemble_kernel, moves, (width_q, width_o)),
        [shaped((n_blk, D, width_q), BF16), shaped((n_blk, D, width_o), BF16)],
        "assemble",
        in_specs=[smem(), vmem(), vmem()],
    )(blocks_info, *held)

    if moves.ring:
        weights_e = []
        for pack in packs_e:
            own = moves.round(pack[None])
            weights_e.append(own + [moves.swap(a) for a in own])
        maps_e = [[j] for j in range(moves.slots)]
        both = jnp.stack([pack_b, moves.swap(pack_b)])
        own_b = moves.round(both)
        maps_b = [[s, moves.ring + s] for s in range(moves.ring)]
    else:
        weights_e = [[moves.whole(pack)] for pack in packs_e]
        maps_e = [[0]]
        own_b = [moves.whole(pack_b)]
        maps_b = [[0]]
    far_b = [moves.flip(a, 2) for a in own_b]
    weights_b = [own_b, [moves.flip(a, 1) for a in own_b], far_b, [moves.flip(a, 1) for a in far_b]]

    normed_one, projected = call(
        functools.partial(qkv_kernel, micro, n_blk),
        [shaped((count, D), BF16), shaped((n_blk, count, 3 * D // n_blk), BF16)],
        "qkv",
        scratch_shapes=[pltpu.VMEM((count, 3 * D), BF16)],
    )(tokens_2d, mod, qkv_w)
    projected = lax.all_to_all(projected, "blk", 0, 0, tiled=True)
    part = D // n_blk

    def by_micro(columns):
        return pl.BlockSpec((n_blk, length, columns), lambda m: (0, m, 0))

    mixed_out = call(
        attend_kernel,
        shaped((n_blk, count, part), BF16),
        "attend",
        grid=(micro,),
        in_specs=[by_micro(3 * part)],
        out_specs=by_micro(part),
    )(projected)
    mixed_in = lax.all_to_all(mixed_out, "blk", 0, 0, tiled=True)

    slots = slots_of(routes_2d, experts, room)
    mixed, attended, residual, normed_two, grad_shared, probs, send = call(
        functools.partial(residual_kernel, micro, n_blk),
        [
            shaped((count, D), BF16),
            shaped((count, D), F32),
            shaped((count, D), F32),
            shaped((count, D), BF16),
            shaped((count, D), BF16),
            shaped((count, TOP), F32),
            shaped((experts, 2, room, D), BF16),
        ],
        "residual",
    )(mixed_in, tokens_2d, mod, out_full, router_t, given, routes_2d, slots.T)

    to_expert = lax.all_to_all(send, "blk", 0, 0, tiled=True)
    plain = pl.BlockSpec((count, D), lambda j: (0, 0))
    acc, grads_b = None, []
    for rel in range(n_blk):
        acc, got = expert_part(
            moves, info, (normed_two, plain, (0,)), (grad_shared, plain, (0,)), acc, weights_b[rel], maps_b, tile, None, "shared"
        )
        grads_b.append(got)
    shared_val, shared_grad = acc
    specs = [pl.BlockSpec((experts, None, room, D), lambda j, i=i: (0, i, 0, 0)) for i in range(2)]
    acc, grads_e = None, []
    for c, weights in enumerate(weights_e):
        last = c == len(weights_e) - 1
        acc, got = expert_part(
            moves, info, (to_expert, specs[0], (0, 2)), (to_expert, specs[1], (0, 2)), acc, weights, maps_e, tile,
            to_expert.shape if last else None, "routed",
        )
        grads_e.append(got)
    back = lax.all_to_all(acc, "blk", 0, 0, tiled=True)

    near, far = [], []
    for rel, into in ((0, near), (2, far)):
        other = [moves.flip(a, 1) for a in grads_b[rel + 1]]
        into.extend(add(a, b) for a, b in zip(grads_b[rel], other))
    sums_b = [add(a, moves.flip(b.astype(BF16), 2)) for a, b in zip(near, far)]
    if moves.ring:
        total = moves.fold_ring(sums_b)
        own_b_grad = add(total[0], moves.swap(total[1].astype(BF16)))
    else:
        own_b_grad = moves.fold_whole(sums_b[0].astype(BF16))
    shared_in_grad, shared_out_t = from_tiles(own_b_grad, tile)

    totals_e = []
    for got in grads_e:
        if moves.ring:
            ring = moves.ring
            parts = [None] * ring
            for s in (1, 2, 3, 0):
                parts[s] = add(got[s], moves.swap(got[ring + s]))
            totals_e.append(moves.fold_ring(parts)[0])
        else:
            totals_e.append(moves.fold_whole(got[0]))
    split_e = [from_tiles(total, tile) for total in totals_e]
    expert_in_grad = jnp.concatenate([pair[0] for pair in split_e], axis=1)
    expert_out_t = jnp.concatenate([pair[1] for pair in split_e], axis=1)

    slot_rows = (n_blk // 2, moves.slots, moves.rows)
    block_out, grad_residual, grad_mod_two, grad_router, out_keep, out_send, grad_mixed = call(
        functools.partial(middle_kernel, micro, n_blk, moves),
        [
            shaped((count, D), BF16),
            shaped((count, D), F32),
            shaped((micro, 4, D), F32),
            shaped((LANES, D), F32),
            shaped(slot_rows + (width_o,), BF16),
            shaped(slot_rows + (width_o,), BF16),
            shaped((n_blk, count, part), BF16),
        ],
        "middle",
        in_specs=[smem()] + [vmem()] * 14,
        scratch_shapes=[pltpu.VMEM((count, D), BF16), pltpu.VMEM((n_blk, D, width_o), BF16)],
    )(
        info, back, routes_2d, slots, probs, shared_val, shared_grad, residual, attended, mixed, normed_two,
        mod, out_full, router_t, given,
    )

    def fold_blocks(keep, send_part):
        total = add(keep, moves.flip(send_part, 1))
        total = add(total[0], moves.flip(total[1].astype(BF16), 2))
        if not moves.ring:
            return moves.fold_whole(total.astype(BF16))
        ring = moves.ring
        total = add(total[:ring], moves.swap(total[ring:].astype(BF16)))
        return moves.fold_ring([total[s] for s in range(ring)])

    out_grad = fold_blocks(out_keep, out_send)

    grad_mixed = lax.all_to_all(grad_mixed, "blk", 0, 0, tiled=True)
    grad_projected = call(
        attend_back_kernel,
        shaped((n_blk, count, 3 * part), BF16),
        "attend_back",
        grid=(micro,),
        in_specs=[by_micro(3 * part), by_micro(part)],
        out_specs=by_micro(3 * part),
    )(projected, grad_mixed)
    arrived = lax.all_to_all(grad_projected, "blk", 0, 0, tiled=True)
    qkv_keep, qkv_send, blocks = qkv_grads(moves, info, arrived, normed_one, slot_rows, width_q)
    qkv_grad = fold_blocks(qkv_keep, qkv_send)
    tokens_grad, grad_mod_one = call(
        functools.partial(tokens_grad_kernel, micro, n_blk),
        [shaped((count, D), F32), shaped((micro, 2, D), F32)],
        "tokens_grad",
    )(blocks, qkv_w, tokens_2d, mod, grad_residual)

    grad_mod = jnp.concatenate([grad_mod_one, grad_mod_two], axis=1).reshape(micro, n_blk, wide)
    payload = jnp.concatenate(
        [
            jnp.broadcast_to(
                grad_mod.transpose(1, 0, 2).reshape(1, n_blk, micro * wide), (n_dp, n_blk, micro * wide)
            ),
            grad_router[:n_blk].reshape(n_blk, n_dp, shard).transpose(1, 0, 2),
        ],
        axis=2,
    ).reshape(n_dp * n_blk, -1)
    arrived = lax.all_to_all(payload, ("dp", "blk"), 0, 0, tiled=True).reshape(n_dp, n_blk, -1)
    item_mod = jnp.sum(arrived[:, :, : micro * wide], axis=1).reshape(n_dp * micro, wide)
    ada_grad = jnp.dot(
        cond.reshape(n_dp * micro, shard).astype(F32).T, item_mod, precision=lax.Precision.HIGHEST
    )
    router_grad = jnp.sum(arrived[:, :, micro * wide :], axis=(0, 1))[:, None]

    return (
        block_out.reshape(tokens.shape),
        tokens_grad.reshape(tokens.shape),
        ada_grad,
        qkv_grad,
        out_grad,
        router_grad,
        shared_in_grad,
        shared_out_t.T,
        expert_in_grad[None],
        expert_out_t.T[None],
    )


def qkv_grads(moves, info, arrived, normed_one, slot_rows, width):
    n_blk, count = arrived.shape[:2]

    def kernel(info, arrived, normed_one, keep, send, blocks, wide, held):
        qkv_grad_kernel(n_blk, moves, info, arrived, normed_one, keep, send, wide, blocks, held)

    return call(
        kernel,
        [
            shaped(slot_rows + (width,), BF16),
            shaped(slot_rows + (width,), BF16),
            shaped((n_blk, count, width), BF16),
        ],
        "qkv_grad",
        in_specs=[smem(), vmem(), vmem()],
        scratch_shapes=[pltpu.VMEM((count, 3 * D), BF16), pltpu.VMEM((D, width), BF16)],
    )(info, arrived, normed_one)


def solution(mesh):
    moves = Moves(mesh)
    in_specs = (
        P(None, "dp", "blk", None),
        P(None, "dp"),
        P(None, "dp", "blk", None),
        P("dp", "blk"),
        P("dp", "blk"),
        P("dp", "blk"),
        P("dp", "blk"),
        P("dp", "blk"),
        P("blk", "dp"),
        P("blk", "dp", None),
        P("blk", None, "dp"),
        P(None, "dp", "blk", None),
    )
    out_specs = (
        P(None, "dp", "blk", None),
        P(None, "dp", "blk", None),
        P("dp", "blk"),
        P("dp", "blk"),
        P("dp", "blk"),
        P("dp", "blk"),
        P("dp", "blk"),
        P("blk", "dp"),
        P("blk", "dp", None),
        P("blk", None, "dp"),
    )
    return jax.shard_map(
        functools.partial(on_device, moves),
        mesh=mesh,
        in_specs=in_specs,
        out_specs=out_specs,
        check_vma=False,
    )
```

```python
import functools
import math

import jax
import jax.numpy as jnp
from jax import lax
from jax.experimental import pallas as pl
from jax.experimental.pallas import tpu as pltpu
from jax.sharding import PartitionSpec as P

D = 768
HEADS = 12
HEAD_DIM = 64
TOP = 2
LANES = 128
F32 = jnp.float32
BF16 = jnp.bfloat16
NN = (((1,), (0,)), ((), ()))
NT = (((1,), (1,)), ((), ()))
TN = (((0,), (0,)), ((), ()))
EPS_NORM = 1e-06
GELU_C = math.sqrt(2.0 / math.pi)
GELU_A = 0.044715
VMEM_LIMIT = 60 * 1024 * 1024


def mm(left, right, dims=NN):
    return lax.dot_general(left, right, dims, preferred_element_type=F32)


def call(kernel, out_shape, name, **kwargs):
    return pl.pallas_call(
        kernel,
        out_shape=out_shape,
        name=name,
        compiler_params=pltpu.CompilerParams(vmem_limit_bytes=VMEM_LIMIT),
        cost_estimate=pl.CostEstimate(flops=0, bytes_accessed=0, transcendentals=0),
        **kwargs,
    )


def smem():
    return pl.BlockSpec(memory_space=pltpu.SMEM)


def vmem():
    return pl.BlockSpec(memory_space=pltpu.VMEM)


def shaped(shape, dtype):
    return jax.ShapeDtypeStruct(shape, dtype)


class Moves:
    def __init__(self, mesh):
        self.n_dp, self.n_blk = mesh.shape["dp"], mesh.shape["blk"]
        self.ring = 4 if self.n_dp == 8 else 0
        self.rows = D // self.n_dp if self.ring else D
        self.slots = 8 if self.ring else 1

    def info(self):
        dp, blk = lax.axis_index("dp"), lax.axis_index("blk")
        if self.ring:
            z, x = dp // 2, dp % 2
            offs = [
                (2 * ((z + self.ring - step) % self.ring) + (x ^ flip)) * self.rows
                for flip in range(2)
                for step in range(self.ring)
            ]
        else:
            offs = [jnp.zeros((), jnp.int32)]
        return jnp.stack(offs + [blk]).astype(jnp.int32)

    def rotate(self, array, steps=1):
        pairs = [(d, (d + 2 * steps) % self.n_dp) for d in range(self.n_dp)]
        return lax.ppermute(array, "dp", pairs)

    def swap(self, array):
        return lax.ppermute(array, "dp", [(d, d ^ 1) for d in range(self.n_dp)])

    def flip(self, array, bit):
        return lax.ppermute(array, "blk", [(b, b ^ bit) for b in range(self.n_blk)])

    def whole(self, shard):
        return lax.all_gather(shard, "dp", axis=0, tiled=True)[None]

    def fold_whole(self, part):
        return lax.psum_scatter(part, "dp", scatter_dimension=0, tiled=True).astype(F32)


def together(*arrays):
    return lax.optimization_barrier(arrays)


def after(value, wait):
    return lax.optimization_barrier((value, wait))[0]


def add(left, right):
    return left.astype(F32) + right.astype(F32)


def normed(rows):
    mean = jnp.mean(rows, axis=-1, keepdims=True)
    centered = rows - mean
    var = jnp.mean(centered * centered, axis=-1, keepdims=True)
    inverse = lax.rsqrt(var + EPS_NORM)
    return centered * inverse, inverse


def norm_back(hat, inverse, grad_hat):
    mean_grad = jnp.mean(grad_hat, axis=-1, keepdims=True)
    mean_both = jnp.mean(grad_hat * hat, axis=-1, keepdims=True)
    return inverse * (grad_hat - mean_grad - hat * mean_both)


def column_sum(rows):
    return jnp.sum(rows, axis=0, keepdims=True)


def place_slots(moves, info, refs, maps, out, start, width):
    for ref, slots in zip(refs, maps):
        for k, j in enumerate(slots):
            at = pl.ds(pl.multiple_of(info[j], moves.rows), moves.rows)
            out[at, :] = ref[k, :, start : start + width]


def take_slots(moves, info, source, refs, maps, start):
    width = source.shape[1]
    for ref, slots in zip(refs, maps):
        for k, j in enumerate(slots):
            at = pl.ds(pl.multiple_of(info[j], moves.rows), moves.rows)
            ref[k, :, start : start + width] = source[at, :]


def qkv_kernel(moves, micro, maps, info, *refs):
    n_blk = moves.n_blk
    tokens, mod, refs = refs[:n_blk], refs[n_blk], refs[n_blk + 1 :]
    weights, refs = refs[: len(maps)], refs[len(maps) :]
    normed_out, weight_out, out_half, kept, near, far, out_w = refs
    length = tokens[0].shape[0] // micro
    part = D // n_blk
    own = info[moves.slots]
    place_slots(moves, info, weights, maps, weight_out, 0, 3 * part)
    place_slots(moves, info, weights, maps, out_w, 3 * part, part)
    half = D // 2
    for i in range(2):
        out_half[:, i * part : (i + 1) * part] = out_w[i * half : (i + 1) * half, :]
    for rel in range(n_blk):
        block = own ^ rel
        for m in range(micro):
            rows = slice(m * length, (m + 1) * length)
            hat, _ = normed(tokens[rel][rows, :].astype(F32))
            values = hat * (1.0 + mod[m, 1:2, :]) + mod[m, 0:1, :]
            normed_out[block, rows, :] = values.astype(BF16)
        projected = mm(normed_out[block], weight_out[...])
        first, last = projected[:, :part], projected[:, 2 * part :]
        even = own % 2 == 0
        groups = (
            (kept, jnp.where(even, first, last)),
            (near, projected[:, part : 2 * part]),
            (far, jnp.where(even, last, first)),
        )
        for out, group in groups:
            for m in range(micro):
                out[block, :, m * part : (m + 1) * part] = group[
                    m * length : (m + 1) * length
                ].astype(BF16)


def by_source(own, kept, near, far, out):
    out[own] = kept[...]
    out[own ^ 1] = near[...]
    out[own ^ 2] = far[...]


def head_rows(ref, source, start):
    block = ref[source, :, :, start : start + HEAD_DIM]
    return block.reshape(block.shape[0] * block.shape[1], HEAD_DIM)


def softmax_rows(query, key):
    scores = mm(query, key, NT) * (1.0 / math.sqrt(HEAD_DIM))
    raised = jnp.exp(scores - jnp.max(scores, axis=-1, keepdims=True))
    return raised / jnp.sum(raised, axis=-1, keepdims=True)


def attend_kernel(moves, micro, info, kept, near, far, out, projected):
    n_blk, own = moves.n_blk, info[moves.slots]
    part = D // n_blk
    length = out.shape[1]
    by_source(own, kept, near, far, projected)
    for start in range(0, micro * part, HEAD_DIM):
        query, key, value = (
            head_rows(projected, (i * n_blk + own) // 3, start) for i in range(3)
        )
        probs = softmax_rows(query, key).astype(BF16)
        mixed = mm(probs, value).astype(BF16)
        out[:, :, start : start + HEAD_DIM] = mixed.reshape(n_blk, length, HEAD_DIM)


def attend_back_kernel(moves, micro, info, kept, near, far, grad_mixed, kept_out, near_out, far_out, projected, out):
    n_blk, own = moves.n_blk, info[moves.slots]
    part = D // n_blk
    length = grad_mixed.shape[1]
    scale = 1.0 / math.sqrt(HEAD_DIM)
    by_source(own, kept, near, far, projected)
    for start in range(0, micro * part, HEAD_DIM):
        query, key, value = (
            head_rows(projected, (i * n_blk + own) // 3, start) for i in range(3)
        )
        block = grad_mixed[:, :, start : start + HEAD_DIM]
        grad = block.reshape(n_blk * length, HEAD_DIM)
        probs = softmax_rows(query, key)
        grad_probs = mm(grad, value, NT)
        inner = jnp.sum(probs * grad_probs, axis=-1, keepdims=True)
        grad_scores = (probs * (grad_probs - inner)).astype(BF16)
        grads = (
            mm(grad_scores, key) * scale,
            mm(grad_scores, query, TN) * scale,
            mm(probs.astype(BF16), grad, TN),
        )
        for i, part_grad in enumerate(grads):
            out[(i * n_blk + own) // 3, :, :, start : start + HEAD_DIM] = part_grad.astype(
                BF16
            ).reshape(n_blk, length, HEAD_DIM)
    kept_out[...] = out[own]
    near_out[...] = out[own ^ 1]
    far_out[...] = out[own ^ 2]


def thirds(values):
    first = values.astype(BF16)
    rest = values - first.astype(F32)
    second = rest.astype(BF16)
    return first, second, (rest - second.astype(F32)).astype(BF16)


def lane_thirds(values, count):
    parts = [third[:, :count] for third in thirds(values)]
    parts.append(jnp.zeros((values.shape[0], LANES - 3 * count), BF16))
    return jnp.concatenate(parts, axis=1)


def from_thirds(lanes, count):
    lanes = lanes.astype(F32)
    return lanes[:, :count] + lanes[:, count : 2 * count] + lanes[:, 2 * count : 3 * count]


def residual_kernel(moves, micro, info, mixed_in, tokens, mod, router, routes, *refs):
    n_blk, own = moves.n_blk, info[moves.slots]
    out_weights, refs = refs[:n_blk], refs[n_blk:]
    mixed, attended, residual, normed_two, probs, payload, parts = refs
    part, half = D // n_blk, D // 2
    length = tokens.shape[0] // micro
    for h in range(n_blk):
        for m in range(micro):
            mixed[m * length : (m + 1) * length, h * part : (h + 1) * part] = mixed_in[
                h, :, m * part : (m + 1) * part
            ]
    left, right = mixed[:, :half], mixed[:, half:]
    for rel in range(n_blk):
        weight = out_weights[rel]
        parts[own ^ rel] = mm(left, weight[:, :part]) + mm(right, weight[:, part:])
    for b in range(n_blk):
        attended[:, b * part : (b + 1) * part] = parts[b]
    for m in range(micro):
        rows = slice(m * length, (m + 1) * length)
        stream = tokens[rows, :].astype(F32) + mod[m, 2:3, :] * attended[rows, :]
        residual[rows, :] = stream
        hat, _ = normed(stream)
        two = (hat * (1.0 + mod[m, 4:5, :]) + mod[m, 3:4, :]).astype(BF16)
        normed_two[rows, :] = two
        payload[rows, :D] = two
    logits = mm(normed_two[...], router[...], NT)
    lanes = lax.broadcasted_iota(jnp.int32, logits.shape, 1)
    picks = [lanes == routes[:, k : k + 1] for k in range(TOP)]
    chosen = [jnp.sum(jnp.where(p, logits, 0.0), axis=-1, keepdims=True) for p in picks]
    top = functools.reduce(jnp.maximum, chosen)
    raised = [jnp.exp(value - top) for value in chosen]
    total = functools.reduce(jnp.add, raised)
    gates = functools.reduce(
        jnp.add, [jnp.where(p, value / total, 0.0) for p, value in zip(picks, raised)]
    )
    probs[...] = gates
    payload[:, D:] = lane_thirds(gates, n_blk)


def expert_step(info, moves, maps, tile, rows, grads, totals, weights, outs, scratch):
    w_in, w_out, g_in, g_out = scratch
    place_slots(moves, info, weights, maps, w_in, 0, tile)
    place_slots(moves, info, weights, maps, w_out, tile, tile)
    pre = mm(rows, w_in[...])
    squared = pre * pre
    bend = jnp.tanh(GELU_C * pre * (1.0 + GELU_A * squared))
    half = 0.5 * (1.0 + bend)
    act = (pre * half).astype(BF16)
    slope = half + 0.5 * pre * (1.0 - bend * bend) * (GELU_C * (1.0 + 3.0 * GELU_A * squared))
    totals[0][...] += mm(act, w_out[...], NT)
    grad_pre = (mm(grads, w_out[...]) * slope).astype(BF16)
    totals[1][...] += mm(grad_pre, w_in[...], NT)
    g_in[...] = mm(rows, grad_pre, TN).astype(BF16)
    g_out[...] = mm(grads, act, TN).astype(BF16)
    take_slots(moves, info, g_in, outs, maps, 0)
    take_slots(moves, info, g_out, outs, maps, tile)


def own_lanes(values, own, count):
    lanes = lax.broadcasted_iota(jnp.int32, values.shape, 1)
    mine = jnp.logical_and(lanes % count == own, lanes < 3 * count)
    return jnp.sum(jnp.where(mine, values.astype(F32), 0.0), axis=-1, keepdims=True)


def routed_kernel(moves, maps, tile, first, last, info, *refs):
    refs = list(refs)

    def pop(count):
        taken = refs[:count]
        del refs[:count]
        return taken

    n_blk, own = moves.n_blk, info[moves.slots]
    payload, gradients, mod = (pop(n_blk), pop(n_blk), pop(1)[0]) if first else ([], [], None)
    given = [] if first else pop(4)
    weights = pop(len(maps))
    hold, all_grads, rows, grads = pop(4) if first else [None] * 2 + given[:2]
    results = pop(2)
    outs = pop(len(maps))
    scratch = pop(4)
    totals = pop(2) if last else results
    step = pl.program_id(0)

    @pl.when(step == 0)
    def _():
        for i, total in enumerate(totals):
            total[...] = jnp.zeros_like(total) if first else given[2 + i][...]

    if first:

        @pl.when(step == 0)
        def _():
            all_count = hold.shape[1]
            micro = mod.shape[0]
            count = payload[0].shape[0]
            length = count // micro
            for rel in range(n_blk):
                for m in range(micro):
                    mixed = gradients[rel][m * length : (m + 1) * length, :].astype(F32) * mod[m, 5:6, :]
                    start = rel * count + m * length
                    all_grads[start : start + length, :] = mixed.astype(BF16)
            gates = jnp.concatenate([ref[:, D:] for ref in payload])
            column = own_lanes(gates, own, n_blk)
            named = jnp.broadcast_to((column > 0.0).astype(F32), (all_count, LANES))
            row = named.T[:8, :]
            ranks = row
            lanes = lax.broadcasted_iota(jnp.int32, row.shape, 1)
            shift = 1
            while shift < all_count:
                ranks = ranks + jnp.where(lanes >= shift, pltpu.roll(ranks, shift, 1), 0.0)
                shift *= 2
            places = (ranks * row - 1.0)[:1, :].astype(jnp.int32)
            index = lax.broadcasted_iota(jnp.int32, hold.shape, 0)
            hold[...] = (index == places).astype(BF16)
            slot_gate = own_lanes(mm(hold[...], gates), own, n_blk)
            rows[...] = mm(hold[...], jnp.concatenate([ref[:, :D] for ref in payload])).astype(BF16)
            picked = mm(hold[...], all_grads[...])
            grads[...] = (slot_gate * picked).astype(BF16)

    expert_step(info, moves, maps, tile, rows[...], grads[...], totals, weights, outs, scratch)

    if last:

        @pl.when(step == pl.num_programs(0) - 1)
        def _():
            for result, total in zip(results, totals):
                result[...] = total[...].astype(BF16)


def shared_kernel(moves, maps, tile, info, *refs):
    n_blk, own = moves.n_blk, info[moves.slots]
    payload, refs = refs[:n_blk], refs[n_blk:]
    (grads, hold, values, backs), refs = refs[:4], refs[4:]
    weights, refs = refs[: len(maps)], refs[len(maps) :]
    (keep, send), outs, refs = refs[:2], refs[2 : 2 + len(maps)], refs[2 + len(maps) :]
    rows, totals, scratch = refs[0], refs[1:3], refs[3:]
    count = payload[0].shape[0]

    @pl.when(pl.program_id(0) == 0)
    def _():
        for rel in range(n_blk):
            at = slice(rel * count, (rel + 1) * count)
            rows[at, :] = payload[rel][:, :D]
        for total in totals:
            total[...] = jnp.zeros_like(total)

    expert_step(info, moves, maps, tile, rows[...], grads[...], totals, weights, outs, scratch)

    @pl.when(pl.program_id(0) == pl.num_programs(0) - 1)
    def _():
        for rel in range(n_blk):
            at = slice(rel * count, (rel + 1) * count)
            target = (send if rel % 2 else keep).at[rel // 2]
            here = hold[:, at]
            routed = mm(here, values[...], TN)
            gate = own_lanes(payload[rel][:, D:], own, n_blk)
            target[:, :D] = (totals[0][at, :] + gate * routed).astype(BF16)
            target[:, D : 2 * D] = (totals[1][at, :] + mm(here, backs[...], TN)).astype(BF16)
            inner = jnp.sum(grads[at, :].astype(F32) * routed, axis=-1, keepdims=True)
            lanes = lax.broadcasted_iota(jnp.int32, (count, LANES), 1)
            target[:, 2 * D :] = lane_thirds(jnp.where(lanes == own, inner, 0.0), n_blk)


def middle_kernel(
    moves, micro, info, near, far, probs, residual, attended, mixed, normed_two, mod, router, cotangent, *refs
):
    n_blk, own = moves.n_blk, info[moves.slots]
    out_weights, refs = refs[:n_blk], refs[n_blk:]
    block_out, grad_residual, grad_mod, grad_router, keep, send, grad_mixed, grad_attended, wide = refs[:9]
    blocks = refs[9]
    part, half = D // n_blk, D // 2
    length = residual.shape[0] // micro
    given = cotangent[...].astype(F32)
    mixture = near[:, :D].astype(F32) + far[:, :D].astype(F32)
    gates = probs[:, :n_blk]
    inner = from_thirds(near[:, 2 * D :], n_blk) + from_thirds(far[:, 2 * D :], n_blk)
    chosen = gates * (inner - jnp.sum(gates * inner, axis=-1, keepdims=True))
    grad_logits = jnp.concatenate(
        [chosen, jnp.zeros((chosen.shape[0], LANES - n_blk), F32)], axis=1
    ).astype(BF16)
    grad_router[...] = mm(grad_logits, normed_two[...], TN)
    grad_two = (
        near[:, D : 2 * D].astype(F32)
        + far[:, D : 2 * D].astype(F32)
        + mm(grad_logits, router[...])
    )
    for m in range(micro):
        rows = slice(m * length, (m + 1) * length)
        block_out[rows, :] = (residual[rows, :] + mod[m, 5:6, :] * mixture[rows]).astype(BF16)
        grad_mod[m, 3:4, :] = column_sum(given[rows] * mixture[rows])
        hat, inverse = normed(residual[rows, :])
        mine = grad_two[rows]
        grad_mod[m, 1:2, :] = column_sum(mine)
        grad_mod[m, 2:3, :] = column_sum(mine * hat)
        total = given[rows] + norm_back(hat, inverse, mine * (1.0 + mod[m, 4:5, :]))
        grad_residual[rows, :] = total
        grad_mod[m, 0:1, :] = column_sum(total * attended[rows, :])
        grad_attended[rows, :] = (total * mod[m, 2:3, :]).astype(BF16)
    for b in range(n_blk):
        blocks[b] = grad_attended[:, b * part : (b + 1) * part]
    left, right = 0.0, 0.0
    for rel in range(n_blk):
        weight, grad = out_weights[rel], blocks[own ^ rel]
        left = left + mm(grad, weight[:, :part], NT)
        right = right + mm(grad, weight[:, part:], NT)
    back_mixed = jnp.concatenate([left, right], axis=1).astype(BF16)
    for h in range(n_blk):
        for m in range(micro):
            grad_mixed[h, :, m * part : (m + 1) * part] = back_mixed[
                m * length : (m + 1) * length, h * part : (h + 1) * part
            ]
    all_mixed = mixed[...]
    for rel in range(n_blk):
        wide[...] = mm(all_mixed, blocks[own ^ rel], TN).astype(BF16)
        target = (send if rel % 2 else keep).at[rel // 2]
        groups = target.shape[0]
        for j in range(moves.slots):
            at = pl.ds(pl.multiple_of(info[j], moves.rows), moves.rows)
            start = j // groups * part
            target[j % groups, :, start : start + part] = wide[at, :]


def qkv_grad_kernel(moves, micro, maps, info, kept, near, far, normed_one, weight, *refs):
    n_blk, own = moves.n_blk, info[moves.slots]
    tokens, mod, refs = refs[:n_blk], refs[n_blk], refs[n_blk + 1 :]
    outs, refs = refs[: len(maps)], refs[len(maps) :]
    keep, send, grad_mod, arrived, blocks, wide = refs
    by_source(own, kept, near, far, arrived)
    part = D // n_blk
    length = arrived.shape[2]
    count = micro * length
    for j in range(3):
        source = (3 * own + j) % n_blk
        for b in range(n_blk):
            for m in range(micro):
                blocks[b, m * length : (m + 1) * length, j * part : (j + 1) * part] = arrived[
                    source, b, :, m * part : (m + 1) * part
                ]
    every = blocks[...].reshape(n_blk * count, 3 * part)
    wide[...] = mm(normed_one[...].reshape(n_blk * count, D), every, TN).astype(BF16)
    take_slots(moves, info, wide, outs, maps, 0)
    sums = [[0.0, 0.0] for _ in range(micro)]
    for rel in range(n_blk):
        back = mm(blocks[own ^ rel], weight[...], NT)
        target = send if rel % 2 else keep
        target[rel // 2] = back.astype(BF16)
        for m in range(micro):
            rows = slice(m * length, (m + 1) * length)
            hat, _ = normed(tokens[rel][rows, :].astype(F32))
            sums[m][0] += column_sum(back[rows])
            sums[m][1] += column_sum(back[rows] * hat)
    for m in range(micro):
        for i in range(2):
            grad_mod[m, i : i + 1, :] = sums[m][i]


def tokens_grad_kernel(micro, near, far, tokens, mod, grad_residual, out):
    grad_one = near[...].astype(F32) + far[...].astype(F32)
    length = tokens.shape[0] // micro
    for m in range(micro):
        rows = slice(m * length, (m + 1) * length)
        hat, inverse = normed(tokens[rows, :].astype(F32))
        own = grad_one[rows]
        out[rows, :] = grad_residual[rows, :] + norm_back(hat, inverse, own * (1.0 + mod[m, 1:2, :]))


def by_tile(left, right, tile):
    parts = []
    for start in range(0, left.shape[1], tile):
        parts += [left[:, start : start + tile], right[:, start : start + tile]]
    return jnp.concatenate(parts, axis=1)


def from_tiles(packed, tile):
    parts = [
        [array[:, start : start + tile] for array in packed for start in range(first, array.shape[1], 2 * tile)]
        for first in (0, tile)
    ]
    return [jnp.concatenate(part, axis=1) for part in parts]


def weight_specs(arrays, tile):
    return [
        pl.BlockSpec((a.shape[0], a.shape[1], 2 * tile), lambda j: (0, 0, j)) for a in arrays
    ]


def held(shape):
    return pl.BlockSpec(shape, lambda j: (0,) * len(shape))


def on_device(moves, tokens, timesteps, routes, ada, qkv, out_w, router, shared_in, shared_out, expert_in, expert_out, cotangent):
    micro, _, length, _ = tokens.shape
    count = micro * length
    n_dp, n_blk, ring = moves.n_dp, moves.n_blk, moves.ring
    experts = n_blk
    capacity = length * TOP // experts + max(2, length // 32)
    room = -(-n_blk * micro * capacity // 16) * 16
    shard = D // n_dp
    part = D // n_blk
    info = moves.info()
    dp_at = lax.axis_index("dp")
    rotate, swap, flip = moves.rotate, moves.swap, moves.flip

    tokens_2d = tokens.reshape(count, D)
    given = cotangent.reshape(count, D)
    routes_2d = routes.reshape(count, TOP)

    pack_a = jnp.concatenate([qkv, out_w], axis=1)
    tile = shared_in.shape[1]
    pack_b = by_tile(shared_in, shared_out.T, tile)
    ff = expert_in.shape[2]
    chunk = ff // 2
    e_out = expert_out[0].T
    pack_0, pack_1 = (
        by_tile(expert_in[0][:, c : c + chunk], e_out[:, c : c + chunk], tile)[None]
        for c in range(0, ff, chunk)
    )


    half = D // 2
    column = jnp.arange(D)
    frequency = jnp.exp(-math.log(10000.0) * (column % half).astype(F32) / half)
    angles = timesteps.astype(F32) * frequency
    cond = jax.nn.silu(jnp.where(column < half, jnp.cos(angles), jnp.sin(angles))).astype(BF16)
    cond = cond.reshape(micro, n_dp, shard).transpose(1, 0, 2)
    cond = lax.all_to_all(cond, "dp", 0, 0, tiled=True)
    if ring:
        maps_a = [[0, 1, 2, 3], [4, 5, 6, 7]]
        maps_b = [[s, ring + s] for s in range(ring)]
        maps_e = [[j] for j in range(moves.slots)]
        cond, pack_a, pack_0, tokens_2d = together(cond, pack_a, pack_0, tokens_2d)
        a1, a2, a3 = rotate(pack_a, 1), rotate(pack_a, 2), rotate(pack_a, -1)
        e0_x0 = swap(pack_0)
    else:
        weights_a, maps_a = [moves.whole(pack_a)], [[0]]

    wide = ada.shape[1]
    partial_mod = jnp.einsum("dmr,rc->dmc", cond, ada, preferred_element_type=F32)
    payload = jnp.concatenate(
        [
            partial_mod.reshape(n_dp, micro * wide),
            jnp.broadcast_to(router[:, 0].astype(F32)[None], (n_dp, shard)),
        ],
        axis=1,
    )
    arrived = lax.all_to_all(payload, "dp", 0, 0, tiled=True)
    far_tokens = flip(tokens_2d, 2)
    if ring:
        arrived, far_tokens, e0_x0, a1, a2, a3, pack_0, given = together(
            arrived, far_tokens, e0_x0, a1, a2, a3, pack_0, given
        )
        held_a = jnp.stack([pack_a, a1, a2, a3])
        weights_a = [held_a, swap(held_a)]
        e0_1 = rotate(pack_0, 1)
    tokens_all = [tokens_2d, flip(tokens_2d, 1), far_tokens, flip(far_tokens, 1)]
    own_mod = jnp.sum(arrived[:, : micro * wide], axis=0)
    own_mod = jnp.concatenate([own_mod, arrived[:, micro * wide :].reshape(D)])
    gathered = lax.all_gather(own_mod, "blk", axis=0)
    if ring:
        gathered, weights_a, tokens_all, given, e0_1, pack_0 = together(
            gathered, weights_a, tokens_all, given, e0_1, pack_0
        )
        e0_3, e0_x1 = rotate(pack_0, -1), swap(e0_1)
    near_given, far_given = flip(given, 1), flip(given, 2)
    mod = gathered[:, : micro * wide].reshape(n_blk, micro, wide)
    mod = mod.transpose(1, 0, 2).reshape(micro, 6, D)
    router_t = jnp.pad(gathered[:, micro * wide :].astype(BF16), ((0, LANES - n_blk), (0, 0)))

    group = shaped((n_blk, length, micro * part), BF16)
    normed_one, qkv_w, out_half, kept, near, far = call(
        functools.partial(qkv_kernel, moves, micro, maps_a),
        [
            shaped((n_blk, count, D), BF16),
            shaped((D, 3 * part), BF16),
            shaped((D // 2, 2 * part), BF16),
            group,
            group,
            group,
        ],
        "qkv",
        in_specs=[smem()] + [vmem()] * (n_blk + 1 + len(weights_a)),
        scratch_shapes=[pltpu.VMEM((D, part), BF16)],
    )(info, *tokens_all, mod, *weights_a)
    if ring:
        near, far, out_half, far_given, near_given, e0_1, e0_3, e0_x1, pack_1 = together(
            near, far, out_half, far_given, near_given, e0_1, e0_3, e0_x1, pack_1
        )
        e0_2, e0_x3 = rotate(e0_1, 1), swap(e0_3)
    near, far = flip(near, 1), flip(far, 2)
    far_out = flip(out_half, 2)
    if ring:
        near, far, out_half, far_out, far_given, e0_2, e0_x3, pack_1, pack_b = together(
            near, far, out_half, far_out, far_given, e0_2, e0_x3, pack_1, pack_b
        )
        e0_x2, b_x, e1_1 = swap(e0_2), swap(pack_b), rotate(pack_1, 1)
    projected = (kept, near, far)
    out_weights = [out_half, flip(out_half, 1), far_out, flip(far_out, 1)]

    from_all = pltpu.VMEM((n_blk, n_blk, length, micro * part), BF16)
    mixed_out = call(
        functools.partial(attend_kernel, moves, micro),
        group,
        "attend",
        in_specs=[smem()] + [vmem()] * 3,
        scratch_shapes=[from_all],
    )(info, *projected)
    mixed_in = lax.all_to_all(mixed_out, "blk", 0, 0, tiled=True)
    if ring:
        mixed_in, out_weights, e0_x2, b_x, e1_1, pack_b, pack_1, far_given = together(
            mixed_in, out_weights, e0_x2, b_x, e1_1, pack_b, pack_1, far_given
        )
        both = jnp.stack([pack_b, b_x])
        e1_2, e1_3 = rotate(e1_1, 1), rotate(pack_1, -1)
        e1_x1, e1_x0 = swap(e1_1), swap(pack_1)
    given_all = [given, near_given, far_given, flip(far_given, 1)]
    columns = D + LANES
    mixed, attended, residual, normed_two, probs, payload = call(
        functools.partial(residual_kernel, moves, micro),
        [
            shaped((count, D), BF16),
            shaped((count, D), F32),
            shaped((count, D), F32),
            shaped((count, D), BF16),
            shaped((count, LANES), F32),
            shaped((count, columns), BF16),
        ],
        "residual",
        in_specs=[smem()] + [vmem()] * (5 + n_blk),
        scratch_shapes=[pltpu.VMEM((n_blk, count, part), F32)],
    )(info, mixed_in, tokens_2d, mod, router_t, routes_2d, *out_weights)
    payloads = [payload, flip(payload, 1), flip(payload, 2)]
    if ring:
        payloads, given_all, e1_2, e1_3, e1_x1, e1_x0, both = together(
            payloads, given_all, e1_2, e1_3, e1_x1, e1_x0, both
        )
        e1_x2, e1_x3 = swap(e1_2), swap(e1_3)
        b_1, b_3 = rotate(both, 1), rotate(both, -1)
    payloads.append(flip(payloads[2], 1))
    if ring:
        weights_e = [
            [pack_0, e0_1, e0_2, e0_3, e0_x0, e0_x1, e0_x2, e0_x3],
            [pack_1, e1_1, e1_2, e1_3, e1_x0, e1_x1, None, None],
        ]
    else:
        weights_b, maps_b = [moves.whole(pack_b)], [[0]]
        weights_e, maps_e = [[moves.whole(pack[0])] for pack in (pack_0, pack_1)], [[0]]

    all_count = n_blk * count
    pay_specs = [held((count, columns))] * n_blk
    tiles = [pltpu.VMEM((D, tile), BF16) for _ in range(4)]
    pair = [((room, D), BF16)] * 2
    totals = [((room, D), F32)] * 2

    def routed_part(c, operands, weights):
        first, last = c == 0, c == 1
        in_specs = [held(operand.shape) for operand in operands]
        results = [((room, all_count), BF16), ((all_count, D), BF16)] + pair if first else []
        results = results + (pair if last else totals)
        got = call(
            functools.partial(routed_kernel, moves, maps_e, tile, first, last),
            [shaped(*r) for r in results] + [shaped(w.shape, BF16) for w in weights],
            "routed",
            grid=(weights[0].shape[2] // (2 * tile),),
            in_specs=[smem()] + in_specs + weight_specs(weights, tile),
            out_specs=[held(shape) for shape, _ in results] + weight_specs(weights, tile),
            scratch_shapes=tiles + ([pltpu.VMEM((room, D), F32)] * 2 if last else []),
        )(info, *operands, *weights)
        return got[: len(results)], got[len(results) :]

    state, grads_0 = routed_part(0, [*payloads, *given_all, mod], weights_e[0])
    if ring:
        state, grads_0, b_1, b_3, e1_x2, e1_x3 = together(
            state, grads_0, b_1, b_3, e1_x2, e1_x3
        )
        weights_e[1][6:] = [e1_x2, e1_x3]
        b_2 = rotate(b_1, 1)
        x0_2 = swap(grads_0[ring + 2])
    hold, all_grads, *state = state
    state, grads_1 = routed_part(1, state, weights_e[1])
    if ring:
        state, grads_1, b_2, x0_2, grads_0 = together(state, grads_1, b_2, x0_2, grads_0)
        weights_b = [both, b_1, b_2, b_3]
        two_0 = rotate(add(grads_0[2], x0_2).astype(BF16), 1)
        x0_3 = swap(grads_0[ring + 3])
    keep, send, *grads_b = call(
        functools.partial(shared_kernel, moves, maps_b, tile),
        [shaped((2, count, 2 * D + LANES), BF16)] * 2 + [shaped(w.shape, BF16) for w in weights_b],
        "shared",
        grid=(1,),
        in_specs=[smem()]
        + pay_specs
        + [held((all_count, D)), held((room, all_count))]
        + [held((room, D))] * 2
        + weight_specs(weights_b, tile),
        out_specs=[held((2, count, 2 * D + LANES))] * 2 + weight_specs(weights_b, tile),
        scratch_shapes=[pltpu.VMEM((all_count, D), BF16)]
        + [pltpu.VMEM((all_count, D), F32)] * 2
        + tiles,
    )(info, *payloads, all_grads, hold, *state, *weights_b)

    if ring:
        keep, send, grads_b, two_0, x0_3, grads_0, grads_1 = together(
            keep, send, grads_b, two_0, x0_3, grads_0, grads_1
        )
        three_0 = rotate((add(grads_0[3], x0_3) + two_0.astype(F32)).astype(BF16), 1)
        x0_1 = swap(grads_0[ring + 1])
    total = add(keep, flip(send, 1)).astype(BF16)
    near, far = total[0], total[1]
    if ring:
        near, far, three_0, x0_1, grads_0, grads_b = together(
            near, far, three_0, x0_1, grads_0, grads_b
        )
        two_b, x0_0 = rotate(grads_b[2], 1), swap(grads_0[ring])
    far = flip(far, 2)
    if ring:
        near, far, two_b, x0_0, grads_0, grads_1, grads_b = together(
            near, far, two_b, x0_0, grads_0, grads_1, grads_b
        )
        one_0 = rotate(add(grads_0[1], x0_1).astype(BF16), -1)
        x1_2 = swap(grads_1[ring + 2])

    halves = 2 if ring else 1
    out_rows = (2, moves.slots // halves, moves.rows, halves * part)
    block_out, grad_residual, grad_mod_two, grad_router, out_keep, out_send, grad_mixed = call(
        functools.partial(middle_kernel, moves, micro),
        [
            shaped((count, D), BF16),
            shaped((count, D), F32),
            shaped((micro, 4, D), F32),
            shaped((LANES, D), F32),
            shaped(out_rows, BF16),
            shaped(out_rows, BF16),
            group,
        ],
        "middle",
        in_specs=[smem()] + [vmem()] * (10 + n_blk),
        scratch_shapes=[
            pltpu.VMEM((count, D), BF16),
            pltpu.VMEM((D, part), BF16),
            pltpu.VMEM((n_blk, count, part), BF16),
        ],
    )(
        info, near, far, probs, residual, attended, mixed, normed_two, mod, router_t, given, *out_weights,
    )

    if ring:
        grad_mixed, one_0, x1_2, grads_1, grads_b = together(
            grad_mixed, one_0, x1_2, grads_1, grads_b
        )
        one_b, x1_3 = rotate(grads_b[1], -1), swap(grads_1[ring + 3])
    grad_mixed = lax.all_to_all(grad_mixed, "blk", 0, 0, tiled=True)
    if ring:
        grad_mixed, one_b, x1_3, grads_1, grads_b, out_keep, out_send = together(
            grad_mixed, one_b, x1_3, grads_1, grads_b, out_keep, out_send
        )
        sum_0 = add(grads_0[0], x0_0) + add(three_0, one_0)
        two_1 = rotate(add(grads_1[2], x1_2).astype(BF16), 1)
        x1_1 = swap(grads_1[ring + 1])
    out_sums = add(out_keep, flip(out_send, 1)).astype(BF16)
    kept, near, far = call(
        functools.partial(attend_back_kernel, moves, micro),
        [group] * 3,
        "attend_back",
        in_specs=[smem()] + [vmem()] * 4,
        scratch_shapes=[from_all, from_all],
    )(info, *projected, grad_mixed)
    if ring:
        near, far, two_1, x1_1, out_sums, grads_1, grads_b = together(
            near, far, two_1, x1_1, out_sums, grads_1, grads_b
        )
        three_b = rotate(add(grads_b[3], two_b).astype(BF16), 1)
        x1_0 = swap(grads_1[ring])
    near, far = flip(near, 1), flip(far, 2)
    out_parts = add(out_sums[0], flip(out_sums[1], 2)).astype(BF16)
    if ring:
        near, far, out_parts, three_b, x1_0, grads_1, grads_b = together(
            near, far, out_parts, three_b, x1_0, grads_1, grads_b
        )
        three_1 = rotate((add(grads_1[3], x1_3) + two_1.astype(F32)).astype(BF16), 1)
        sum_b = add(grads_b[0], one_b) + three_b.astype(F32)
        b_across = swap(sum_b[1].astype(BF16))
        out_across = swap(out_parts[:, :, part:])
    got = call(
        functools.partial(qkv_grad_kernel, moves, micro, maps_a),
        [shaped(w.shape[:2] + (3 * part,), BF16) for w in weights_a]
        + [shaped((2, count, D), BF16)] * 2
        + [shaped((micro, 2, D), F32)],
        "qkv_grad",
        in_specs=[smem()] + [vmem()] * (6 + n_blk),
        scratch_shapes=[
            from_all,
            pltpu.VMEM((n_blk, count, 3 * part), BF16),
            pltpu.VMEM((D, 3 * part), BF16),
        ],
    )(info, kept, near, far, normed_one, qkv_w, *tokens_all, mod)
    qkv_parts, (one_keep, one_send, grad_mod_one) = got[:-3], got[-3:]
    if ring:
        qkv_parts, one_keep, one_send, grad_mod_one, three_1, b_across, out_across, out_parts, grads_1 = together(
            qkv_parts, one_keep, one_send, grad_mod_one, three_1, b_across, out_across, out_parts, grads_1
        )
        qkv_across = swap(qkv_parts[1])
        one_1 = rotate(add(grads_1[1], x1_1).astype(BF16), -1)
    one_sums = add(one_keep, flip(one_send, 1)).astype(BF16)

    grad_mod = jnp.concatenate([grad_mod_one, grad_mod_two], axis=1).reshape(micro, n_blk, wide)
    payload = jnp.concatenate(
        [
            jnp.broadcast_to(
                grad_mod.transpose(1, 0, 2).reshape(1, n_blk, micro * wide), (n_dp, n_blk, micro * wide)
            ),
            grad_router[:n_blk].reshape(n_blk, n_dp, shard).transpose(1, 0, 2),
        ],
        axis=2,
    ).reshape(n_dp * n_blk, -1)

    if ring:
        sums_b = add(sum_b[0], b_across)
        shared_in_grad, shared_out_t = from_tiles([sums_b], tile)
        own = add(out_parts[:, :, :part], out_across).astype(BF16)
        one_sums, qkv_across, one_1, payload, qkv_parts, own, shared_in_grad, shared_out_t = together(
            one_sums, qkv_across, one_1, payload, qkv_parts, own, shared_in_grad, shared_out_t
        )
        mine = add(qkv_parts[0], qkv_across).astype(BF16)
        qkv_2, qkv_1, qkv_3 = rotate(mine[2], 2), rotate(mine[1], -1), rotate(mine[3], 1)
        out_1, out_2, out_3 = rotate(own[1], -1), rotate(own[2], 2), rotate(own[3], 1)
    near, far = one_sums[0], flip(one_sums[1], 2)
    arrived = lax.all_to_all(payload, ("dp", "blk"), 0, 0, tiled=True)
    arrived = arrived.reshape(n_dp, n_blk, -1)
    item_mod = jnp.sum(arrived[:, :, : micro * wide], axis=1).reshape(n_dp * micro, wide)
    ada_grad = jnp.dot(
        cond.reshape(n_dp * micro, shard).astype(F32).T, item_mod, precision=lax.Precision.HIGHEST
    )
    router_grad = jnp.sum(arrived[:, :, micro * wide :], axis=(0, 1))[:, None]
    if ring:
        sum_1 = add(grads_1[0], x1_0) + add(three_1, one_1)
        expert_in_grad, expert_out_t = from_tiles([sum_0[0], sum_1[0]], tile)
        shared_out_grad, expert_out_grad = shared_out_t.T, expert_out_t.T
        near, far, out_1, out_2, out_3, qkv_1, qkv_2, qkv_3, ada_grad, router_grad, expert_in_grad, expert_out_grad = together(
            near, far, out_1, out_2, out_3, qkv_1, qkv_2, qkv_3, ada_grad, router_grad, expert_in_grad, expert_out_grad
        )
        qkv_grad = add(mine[0], qkv_2) + add(qkv_1, qkv_3)
        out_grad = add(own[0], out_2) + add(out_1, out_3)
    else:
        sums_b = moves.fold_whole(grads_b[0][0])
        sums_e = [moves.fold_whole(got[0][0]) for got in (grads_0, grads_1)]
        shared_in_grad, shared_out_t = from_tiles([sums_b], tile)
        expert_in_grad, expert_out_t = from_tiles(sums_e, tile)
        shared_out_grad, expert_out_grad = shared_out_t.T, expert_out_t.T
        qkv_grad = moves.fold_whole(qkv_parts[0][0])
        out_grad = moves.fold_whole(out_parts[0])
    tokens_grad = call(
        functools.partial(tokens_grad_kernel, micro),
        shaped((count, D), F32),
        "tokens_grad",
    )(near, far, tokens_2d, mod, grad_residual)

    return (
        block_out.reshape(tokens.shape),
        tokens_grad.reshape(tokens.shape),
        ada_grad,
        qkv_grad,
        out_grad,
        router_grad,
        shared_in_grad,
        shared_out_grad,
        expert_in_grad[None],
        expert_out_grad[None],
    )


def solution(mesh):
    moves = Moves(mesh)
    in_specs = (
        P(None, "dp", "blk", None),
        P(None, "dp"),
        P(None, "dp", "blk", None),
        P("dp", "blk"),
        P("dp", "blk"),
        P("dp", "blk"),
        P("dp", "blk"),
        P("dp", "blk"),
        P("blk", "dp"),
        P("blk", "dp", None),
        P("blk", None, "dp"),
        P(None, "dp", "blk", None),
    )
    out_specs = (
        P(None, "dp", "blk", None),
        P(None, "dp", "blk", None),
        P("dp", "blk"),
        P("dp", "blk"),
        P("dp", "blk"),
        P("dp", "blk"),
        P("dp", "blk"),
        P("blk", "dp"),
        P("blk", "dp", None),
        P("blk", None, "dp"),
    )
    return jax.shard_map(
        functools.partial(on_device, moves),
        mesh=mesh,
        in_specs=in_specs,
        out_specs=out_specs,
        check_vma=False,
    )
```

```python
import copy
import functools
import math

import jax
import jax.numpy as jnp
from jax import lax
from jax.experimental import pallas as pl
from jax.experimental.pallas import tpu as pltpu
from jax.sharding import PartitionSpec as P

D = 768
HEADS = 12
HEAD_DIM = 64
TOP = 2
LANES = 128
F32 = jnp.float32
BF16 = jnp.bfloat16
NN = (((1,), (0,)), ((), ()))
NT = (((1,), (1,)), ((), ()))
TN = (((0,), (0,)), ((), ()))
EPS_NORM = 1e-06
GELU_C = math.sqrt(2.0 / math.pi)
GELU_A = 0.044715
VMEM_MIB = {
    "qkv": 10,
    "attend": 10,
    "residual": 10,
    "pick": 12,
    "routed": 24,
    "shared": 28,
    "back": 8,
    "middle": 10,
    "attend_back": 14,
    "mixture": 10,
    "qkv_grad": 14,
    "tokens_grad": 8,
    "block_out": 8,
}


def mm(left, right, dims=NN):
    return lax.dot_general(left, right, dims, preferred_element_type=F32)


def call(kernel, out_shape, name, vmem_mib=None, **kwargs):
    def run(*operands):
        if "grid" not in kwargs:
            kwargs.setdefault("in_specs", [vmem()] * len(operands))
            kwargs["out_specs"] = jax.tree.map(lambda _: vmem(), out_shape)
        limit = (vmem_mib or VMEM_MIB[name]) * 1024 * 1024
        return pl.pallas_call(
            kernel,
            out_shape=out_shape,
            name=name,
            compiler_params=pltpu.CompilerParams(vmem_limit_bytes=limit),
            **kwargs,
        )(*operands)

    return run


def smem():
    return pl.BlockSpec(memory_space=pltpu.SMEM)


def vmem():
    return pl.BlockSpec(memory_space=pltpu.VMEM)


def shaped(shape, dtype):
    return jax.ShapeDtypeStruct(shape, dtype)


class Moves:
    def __init__(self, mesh):
        self.n_dp, self.n_blk = mesh.shape["dp"], mesh.shape["blk"]
        self.ring = 4 if self.n_dp == 8 else 0
        self.rows = D // self.n_dp if self.ring else D
        self.slots = 8 if self.ring else 1

    def info(self):
        dp, blk = lax.axis_index("dp"), lax.axis_index("blk")
        if self.ring:
            z, x = dp // 2, dp % 2
            offs = [
                (2 * ((z + self.ring - step) % self.ring) + (x ^ flip)) * self.rows
                for flip in range(2)
                for step in range(self.ring)
            ]
        else:
            offs = [jnp.zeros((), jnp.int32)]
        return jnp.stack(offs + [blk]).astype(jnp.int32)

    def rotate(self, array, steps=1):
        pairs = [(d, (d + 2 * steps) % self.n_dp) for d in range(self.n_dp)]
        return lax.ppermute(array, "dp", pairs)

    def swap(self, array):
        return lax.ppermute(array, "dp", [(d, d ^ 1) for d in range(self.n_dp)])

    def flip(self, array, bit):
        return lax.ppermute(array, "blk", [(b, b ^ bit) for b in range(self.n_blk)])

    def whole_rows(self):
        rows = copy.copy(self)
        rows.rows, rows.slots = D, 1
        return rows

    def whole(self, shard):
        return lax.all_gather(shard, "dp", axis=0, tiled=True)[None]

    def fold_whole(self, part):
        return lax.psum_scatter(part, "dp", scatter_dimension=0, tiled=True).astype(F32)


def together(*arrays):
    return lax.optimization_barrier(arrays)


def after(value, wait):
    return lax.optimization_barrier((value, wait))[0]


def add(left, right):
    return left.astype(F32) + right.astype(F32)


def normed(rows):
    mean = jnp.mean(rows, axis=-1, keepdims=True)
    centered = rows - mean
    var = jnp.mean(centered * centered, axis=-1, keepdims=True)
    inverse = lax.rsqrt(var + EPS_NORM)
    return centered * inverse, inverse


def norm_back(hat, inverse, grad_hat):
    mean_grad = jnp.mean(grad_hat, axis=-1, keepdims=True)
    mean_both = jnp.mean(grad_hat * hat, axis=-1, keepdims=True)
    return inverse * (grad_hat - mean_grad - hat * mean_both)


def column_sum(rows):
    return jnp.sum(rows, axis=0, keepdims=True)


def place_slots(moves, info, refs, maps, out, start, width):
    if not isinstance(start, int):
        start = pl.multiple_of(start, LANES)
    for ref, slots in zip(refs, maps):
        for k, j in enumerate(slots):
            at = pl.ds(pl.multiple_of(info[j], moves.rows), moves.rows)
            out[at, :] = ref[k, :, pl.ds(start, width)]


def take_slots(moves, info, source, refs, maps, start, before=None):
    width = source.shape[1]
    if not isinstance(start, int):
        start = pl.multiple_of(start, LANES)
    columns = pl.ds(start, width)
    for i, (ref, slots) in enumerate(zip(refs, maps)):
        for k, j in enumerate(slots):
            at = pl.ds(pl.multiple_of(info[j], moves.rows), moves.rows)
            if before:
                total = source[at, :].astype(F32) + before[i][k, :, columns].astype(F32)
                ref[k, :, columns] = total.astype(BF16)
            else:
                ref[k, :, columns] = source[at, :]


def qkv_kernel(moves, micro, maps, info, *refs):
    n_blk = moves.n_blk
    tokens, mod, refs = refs[:n_blk], refs[n_blk], refs[n_blk + 1 :]
    weights, refs = refs[: len(maps)], refs[len(maps) :]
    normed_out, weight_out, out_half, kept, near, far, out_w = refs
    length = tokens[0].shape[0] // micro
    part = D // n_blk
    own = info[moves.slots]
    place_slots(moves, info, weights, maps, weight_out, 0, 3 * part)
    place_slots(moves, info, weights, maps, out_w, 3 * part, part)
    half = D // 2
    for i in range(2):
        out_half[:, i * part : (i + 1) * part] = out_w[i * half : (i + 1) * half, :]
    for rel in range(n_blk):
        block = own ^ rel
        for m in range(micro):
            rows = slice(m * length, (m + 1) * length)
            hat, _ = normed(tokens[rel][rows, :].astype(F32))
            values = hat * (1.0 + mod[m, 1:2, :]) + mod[m, 0:1, :]
            normed_out[block, rows, :] = values.astype(BF16)
        projected = mm(normed_out[block], weight_out[...])
        first, last = projected[:, :part], projected[:, 2 * part :]
        even = own % 2 == 0
        groups = (
            (kept, jnp.where(even, first, last)),
            (near, projected[:, part : 2 * part]),
            (far, jnp.where(even, last, first)),
        )
        for out, group in groups:
            for m in range(micro):
                out[block, :, m * part : (m + 1) * part] = group[
                    m * length : (m + 1) * length
                ].astype(BF16)


def by_source(own, kept, near, far, out):
    out[own] = kept[...]
    out[own ^ 1] = near[...]
    out[own ^ 2] = far[...]


def head_rows(ref, source, start):
    block = ref[source, :, :, start : start + HEAD_DIM]
    return block.reshape(block.shape[0] * block.shape[1], HEAD_DIM)


SCORE_SCALE = 1.0 / math.sqrt(HEAD_DIM)


def head_parts(moves, info, projected, start):
    n_blk, own = moves.n_blk, info[moves.slots]
    query, key, value = (
        head_rows(projected, (i * n_blk + own) // 3, start) for i in range(3)
    )
    return query * jnp.asarray(SCORE_SCALE, BF16), key, value


def softmax_rows(query, key):
    scores = mm(query, key, NT)
    raised = jnp.exp(scores - jnp.max(scores, axis=-1, keepdims=True))
    return raised, 1.0 / jnp.sum(raised, axis=-1, keepdims=True)


def attend_kernel(moves, info, kept, near, far, out, projected):
    n_blk, length, columns = out.shape
    by_source(info[moves.slots], kept, near, far, projected)
    for start in range(0, columns, HEAD_DIM):
        query, key, value = head_parts(moves, info, projected, start)
        raised, inverse = softmax_rows(query, key)
        mixed = mm((raised * inverse).astype(BF16), value).astype(BF16)
        out[:, :, start : start + HEAD_DIM] = mixed.reshape(n_blk, length, HEAD_DIM)


def attend_back_kernel(
    moves, info, kept, near, far, grad_mixed, kept_out, near_out, far_out, projected, out
):
    n_blk, own = moves.n_blk, info[moves.slots]
    _, length, columns = grad_mixed.shape
    by_source(own, kept, near, far, projected)
    for start in range(0, columns, HEAD_DIM):
        query, key, value = head_parts(moves, info, projected, start)
        grad = grad_mixed[:, :, start : start + HEAD_DIM].reshape(n_blk * length, HEAD_DIM)
        raised, inverse = softmax_rows(query, key)
        probs = raised * inverse
        grad_probs = mm(grad, value, NT)
        inner = jnp.sum(probs * grad_probs, axis=-1, keepdims=True)
        grad_scores = (probs * (grad_probs - inner)).astype(BF16)
        grads = (
            mm(grad_scores, key) * SCORE_SCALE,
            mm(grad_scores, query, TN),
            mm(probs.astype(BF16), grad, TN),
        )
        for i, part_grad in enumerate(grads):
            out[(i * n_blk + own) // 3, :, :, start : start + HEAD_DIM] = part_grad.astype(
                BF16
            ).reshape(n_blk, length, HEAD_DIM)
    kept_out[...] = out[own]
    near_out[...] = out[own ^ 1]
    far_out[...] = out[own ^ 2]


def thirds(values):
    first = values.astype(BF16)
    rest = values - first.astype(F32)
    second = rest.astype(BF16)
    return first, second, (rest - second.astype(F32)).astype(BF16)


def lane_thirds(values, count):
    parts = [third[:, :count] for third in thirds(values)]
    parts.append(jnp.zeros((values.shape[0], LANES - 3 * count), BF16))
    return jnp.concatenate(parts, axis=1)


def from_thirds(lanes, count):
    lanes = lanes.astype(F32)
    return lanes[:, :count] + lanes[:, count : 2 * count] + lanes[:, 2 * count : 3 * count]


def residual_kernel(moves, micro, info, mixed_in, tokens, mod, router, routes, *refs):
    n_blk, own = moves.n_blk, info[moves.slots]
    out_weights, refs = refs[:n_blk], refs[n_blk:]
    mixed, attended, residual, normed_two, probs, payload, parts = refs
    part, half = D // n_blk, D // 2
    length = tokens.shape[0] // micro
    for h in range(n_blk):
        for m in range(micro):
            mixed[m * length : (m + 1) * length, h * part : (h + 1) * part] = mixed_in[
                h, :, m * part : (m + 1) * part
            ]
    left, right = mixed[:, :half], mixed[:, half:]
    for rel in range(n_blk):
        weight = out_weights[rel]
        parts[own ^ rel] = mm(left, weight[:, :part]) + mm(right, weight[:, part:])
    for b in range(n_blk):
        attended[:, b * part : (b + 1) * part] = parts[b]
    for m in range(micro):
        rows = slice(m * length, (m + 1) * length)
        stream = tokens[rows, :].astype(F32) + mod[m, 2:3, :] * attended[rows, :]
        residual[rows, :] = stream
        hat, _ = normed(stream)
        two = (hat * (1.0 + mod[m, 4:5, :]) + mod[m, 3:4, :]).astype(BF16)
        normed_two[rows, :] = two
        payload[rows, :D] = two
    logits = mm(normed_two[...], router[...], NT)
    lanes = lax.broadcasted_iota(jnp.int32, logits.shape, 1)
    picks = [lanes == routes[:, k : k + 1] for k in range(TOP)]
    chosen = [jnp.sum(jnp.where(p, logits, 0.0), axis=-1, keepdims=True) for p in picks]
    top = functools.reduce(jnp.maximum, chosen)
    raised = [jnp.exp(value - top) for value in chosen]
    total = functools.reduce(jnp.add, raised)
    gates = functools.reduce(
        jnp.add, [jnp.where(p, value / total, 0.0) for p, value in zip(picks, raised)]
    )
    probs[...] = gates
    payload[:, D:] = lane_thirds(gates, n_blk)


def expert_step(
    info, moves, maps, out_maps, tile, rows, grads, totals, weights, outs, scratch, base=0, before=None
):
    w_in, w_out, g_in, g_out = scratch
    place_slots(moves, info, weights, maps, w_in, base, tile)
    place_slots(moves, info, weights, maps, w_out, base + tile, tile)
    pre = mm(rows, w_in[...])
    squared = pre * pre
    bend = jnp.tanh(GELU_C * pre * (1.0 + GELU_A * squared))
    half = 0.5 * (1.0 + bend)
    act = (pre * half).astype(BF16)
    slope = half + 0.5 * pre * (1.0 - bend * bend) * (GELU_C * (1.0 + 3.0 * GELU_A * squared))
    totals[0][...] += mm(act, w_out[...], NT)
    grad_pre = (mm(grads, w_out[...]) * slope).astype(BF16)
    totals[1][...] += mm(grad_pre, w_in[...], NT)
    g_in[...] = mm(rows, grad_pre, TN).astype(BF16)
    g_out[...] = mm(grads, act, TN).astype(BF16)
    take_slots(moves, info, g_in, outs, out_maps, base, before)
    take_slots(moves, info, g_out, outs, out_maps, base + tile, before)


def own_lanes(values, own, count):
    lanes = lax.broadcasted_iota(jnp.int32, values.shape, 1)
    mine = jnp.logical_and(lanes % count == own, lanes < 3 * count)
    return jnp.sum(jnp.where(mine, values.astype(F32), 0.0), axis=-1, keepdims=True)


def pick_kernel(moves, info, *refs):
    n_blk, own = moves.n_blk, info[moves.slots]
    payload, gradients, mod, refs = refs[:n_blk], refs[n_blk : 2 * n_blk], refs[2 * n_blk], refs[2 * n_blk + 1 :]
    all_grads, hold, rows = refs
    count, micro = payload[0].shape[0], mod.shape[0]
    length = count // micro
    for rel in range(n_blk):
        for m in range(micro):
            mixed = gradients[rel][m * length : (m + 1) * length, :].astype(F32) * mod[m, 5:6, :]
            start = rel * count + m * length
            all_grads[start : start + length, :] = mixed.astype(BF16)
    gates = jnp.concatenate([ref[:, D:] for ref in payload])
    column = own_lanes(gates, own, n_blk)
    all_count = n_blk * count
    named = jnp.broadcast_to((column > 0.0).astype(F32), (all_count, LANES))
    row = named.T[:8, :]
    ranks = row
    lanes = lax.broadcasted_iota(jnp.int32, row.shape, 1)
    shift = 1
    while shift < all_count:
        ranks = ranks + jnp.where(lanes >= shift, pltpu.roll(ranks, shift, 1), 0.0)
        shift *= 2
    places = (ranks * row - 1.0)[:1, :].astype(jnp.int32)
    index = lax.broadcasted_iota(jnp.int32, hold.shape, 0)
    hold[...] = (index == places).astype(BF16)
    slot_gate = own_lanes(mm(hold[...], gates), own, n_blk)
    rows[:, :D] = mm(hold[...], jnp.concatenate([ref[:, :D] for ref in payload])).astype(BF16)
    rows[:, D:] = (slot_gate * mm(hold[...], all_grads[...])).astype(BF16)


def shared_kernel(moves, maps, out_maps, tile, info, *refs):
    n_blk = moves.n_blk
    payload, grads, refs = refs[:n_blk], refs[n_blk], refs[n_blk + 1 :]
    weights, refs = refs[: len(maps)], refs[len(maps) :]
    results, outs, refs = refs[:2], refs[2 : 2 + len(out_maps)], refs[2 + len(out_maps) :]
    rows, totals, scratch = refs[0], refs[1:3], refs[3:]
    count = payload[0].shape[0]
    for rel in range(n_blk):
        rows[rel * count : (rel + 1) * count, :] = payload[rel][:, :D]
    for total in totals:
        total[...] = jnp.zeros_like(total)
    expert_step(
        info, moves, maps, out_maps, tile, rows[...], grads[...], totals, weights, outs, scratch
    )
    for result, total in zip(results, totals):
        result[...] = total[...].astype(BF16)


def routed_kernel(moves, maps, out_maps, tile, whole, other, info, given, *refs):
    n_blk, own = moves.n_blk, info[moves.slots]
    weights, refs = refs[: len(maps)], refs[len(maps) :]
    before, refs = (refs[: len(out_maps)], refs[len(out_maps) :]) if other else ([], refs)
    results, refs = (refs[:2], refs[2:]) if other else (refs[:3], refs[3:])
    outs, refs = refs[: len(out_maps)], refs[len(out_maps) :]
    totals, scratch = refs[:2], refs[2:]
    step = pl.program_id(0)

    @pl.when(step == 0)
    def _():
        for total in totals:
            total[...] = jnp.zeros_like(total)

    base = step * 2 * tile if whole else 0
    expert_step(
        info, moves, maps, out_maps, tile, given[:, :D], given[:, D:], totals, weights, outs, scratch, base, before
    )

    @pl.when(step == pl.num_programs(0) - 1)
    def _():
        value, back = totals[0][...], totals[1][...]
        inner = jnp.sum(given[:, D:].astype(F32) * value, axis=-1, keepdims=True)
        lanes = lax.broadcasted_iota(jnp.int32, (value.shape[0], LANES), 1)
        inner = jnp.where(lanes == own, inner, 0.0)
        if other:
            results[0][...] = value.astype(BF16)
            results[1][:, :D] = back.astype(BF16)
            results[1][:, D:] = lane_thirds(inner, n_blk)
        else:
            results[0][...], results[1][...], results[2][...] = value, back, inner


def back_kernel(moves, info, hold, shared, back, inner, *refs):
    n_blk, own = moves.n_blk, info[moves.slots]
    *other, keep, send = refs
    total, product = back[...], inner[...]
    if other:
        total = total + other[0][:, :D].astype(F32)
        more = own_lanes(other[0][:, D:], own, n_blk)
        lanes = lax.broadcasted_iota(jnp.int32, product.shape, 1)
        product = product + jnp.where(lanes == own, more, 0.0)
    total, product = total.astype(BF16), lane_thirds(product, n_blk)
    count = keep.shape[1]
    for rel in range(n_blk):
        at = slice(rel * count, (rel + 1) * count)
        target = (send if rel % 2 else keep).at[rel // 2]
        here = hold[:, at]
        target[:, :D] = (shared[at, :].astype(F32) + mm(here, total, TN)).astype(BF16)
        target[:, D:] = mm(here, product, TN).astype(BF16)


def mixture_kernel(moves, info, hold, shared, value, mod, *refs):
    n_blk, own, micro = moves.n_blk, info[moves.slots], mod.shape[0]
    payload, gradients, refs = refs[:n_blk], refs[n_blk : 2 * n_blk], refs[2 * n_blk :]
    *other, keep, send, grad_gate = refs
    total = value[...]
    if other:
        total = total + other[0][...].astype(F32)
    total = total.astype(BF16)
    count = keep.shape[1]
    length = count // micro
    sums = [0.0] * micro
    for rel in range(n_blk):
        at = slice(rel * count, (rel + 1) * count)
        target = (send if rel % 2 else keep).at[rel // 2]
        gate = own_lanes(payload[rel][:, D:], own, n_blk)
        mixture = shared[at, :].astype(F32) + gate * mm(hold[:, at], total, TN)
        target[...] = mixture.astype(BF16)
        product = mixture * gradients[rel][...].astype(F32)
        for m in range(micro):
            sums[m] = sums[m] + column_sum(product[m * length : (m + 1) * length])
    for m in range(micro):
        grad_gate[m] = sums[m]


def middle_kernel(
    moves, micro, info, near, far, probs, residual, attended, mixed, normed_two, mod, router, cotangent, *refs
):
    n_blk, own = moves.n_blk, info[moves.slots]
    out_weights, refs = refs[:n_blk], refs[n_blk:]
    grad_residual, grad_mod, grad_router, keep, send, grad_mixed, grad_attended, wide, blocks = refs
    part, half = D // n_blk, D // 2
    length = residual.shape[0] // micro
    given = cotangent[...].astype(F32)
    gates = probs[:, :n_blk]
    inner = from_thirds(near[:, D:], n_blk) + from_thirds(far[:, D:], n_blk)
    chosen = inner - gates * jnp.sum(inner, axis=-1, keepdims=True)
    grad_logits = jnp.concatenate(
        [chosen, jnp.zeros((chosen.shape[0], LANES - n_blk), F32)], axis=1
    ).astype(BF16)
    grad_router[...] = mm(grad_logits, normed_two[...], TN)
    grad_two = (
        near[:, :D].astype(F32)
        + far[:, :D].astype(F32)
        + mm(grad_logits, router[...])
    )
    for m in range(micro):
        rows = slice(m * length, (m + 1) * length)
        hat, inverse = normed(residual[rows, :])
        mine = grad_two[rows]
        grad_mod[m, 1:2, :] = column_sum(mine)
        grad_mod[m, 2:3, :] = column_sum(mine * hat)
        total = given[rows] + norm_back(hat, inverse, mine * (1.0 + mod[m, 4:5, :]))
        grad_residual[rows, :] = total
        grad_mod[m, 0:1, :] = column_sum(total * attended[rows, :])
        grad_attended[rows, :] = (total * mod[m, 2:3, :]).astype(BF16)
    for b in range(n_blk):
        blocks[b] = grad_attended[:, b * part : (b + 1) * part]
    left, right = 0.0, 0.0
    for rel in range(n_blk):
        weight, grad = out_weights[rel], blocks[own ^ rel]
        left = left + mm(grad, weight[:, :part], NT)
        right = right + mm(grad, weight[:, part:], NT)
    back_mixed = jnp.concatenate([left, right], axis=1).astype(BF16)
    for h in range(n_blk):
        for m in range(micro):
            grad_mixed[h, :, m * part : (m + 1) * part] = back_mixed[
                m * length : (m + 1) * length, h * part : (h + 1) * part
            ]
    all_mixed = mixed[...]
    for rel in range(n_blk):
        wide[...] = mm(all_mixed, blocks[own ^ rel], TN).astype(BF16)
        target = (send if rel % 2 else keep).at[rel // 2]
        groups = target.shape[0]
        for j in range(moves.slots):
            at = pl.ds(pl.multiple_of(info[j], moves.rows), moves.rows)
            start = j // groups * part
            target[j % groups, :, start : start + part] = wide[at, :]


def block_out_kernel(micro, near, far, residual, mod, block_out):
    mixture = near[...].astype(F32) + far[...].astype(F32)
    length = residual.shape[0] // micro
    for m in range(micro):
        rows = slice(m * length, (m + 1) * length)
        block_out[rows, :] = (residual[rows, :] + mod[m, 5:6, :] * mixture[rows]).astype(BF16)


def qkv_grad_kernel(moves, micro, maps, info, kept, near, far, out_near, out_far, normed_one, weight, *refs):
    n_blk, own = moves.n_blk, info[moves.slots]
    tokens, mod, refs = refs[:n_blk], refs[n_blk], refs[n_blk + 1 :]
    outs, refs = refs[: len(maps)], refs[len(maps) :]
    keep, send, grad_mod, arrived, blocks, wide = refs
    by_source(own, kept, near, far, arrived)
    part = D // n_blk
    length = arrived.shape[2]
    count = micro * length
    for j in range(3):
        source = (3 * own + j) % n_blk
        for b in range(n_blk):
            for m in range(micro):
                blocks[b, m * length : (m + 1) * length, j * part : (j + 1) * part] = arrived[
                    source, b, :, m * part : (m + 1) * part
                ]
    every = blocks[...].reshape(n_blk * count, 3 * part)
    wide[...] = mm(normed_one[...].reshape(n_blk * count, D), every, TN).astype(BF16)
    take_slots(moves, info, wide, outs, maps, 0)
    out_grad = (out_near[...].astype(F32) + out_far[...].astype(F32)).astype(BF16)
    groups = out_near.shape[0]
    for ref, slots in zip(outs, maps):
        for k, j in enumerate(slots):
            start = j // groups * part
            ref[k, :, 3 * part :] = out_grad[j % groups, :, start : start + part]
    sums = [[0.0, 0.0] for _ in range(micro)]
    for rel in range(n_blk):
        back = mm(blocks[own ^ rel], weight[...], NT)
        target = send if rel % 2 else keep
        target[rel // 2] = back.astype(BF16)
        for m in range(micro):
            rows = slice(m * length, (m + 1) * length)
            hat, _ = normed(tokens[rel][rows, :].astype(F32))
            sums[m][0] += column_sum(back[rows])
            sums[m][1] += column_sum(back[rows] * hat)
    for m in range(micro):
        for i in range(2):
            grad_mod[m, i : i + 1, :] = sums[m][i]


def tokens_grad_kernel(micro, near, far, tokens, mod, grad_residual, out):
    grad_one = near[...].astype(F32) + far[...].astype(F32)
    length = tokens.shape[0] // micro
    for m in range(micro):
        rows = slice(m * length, (m + 1) * length)
        hat, inverse = normed(tokens[rows, :].astype(F32))
        own = grad_one[rows]
        out[rows, :] = grad_residual[rows, :] + norm_back(hat, inverse, own * (1.0 + mod[m, 1:2, :]))


def by_tile(left, right, tile):
    parts = []
    for start in range(0, left.shape[1], tile):
        parts += [left[:, start : start + tile], right[:, start : start + tile]]
    return jnp.concatenate(parts, axis=1)


def from_tiles(packed, tile):
    parts = [
        [array[:, start : start + tile] for array in packed for start in range(first, array.shape[1], 2 * tile)]
        for first in (0, tile)
    ]
    return [jnp.concatenate(part, axis=1) for part in parts]


def block_specs(parts, tile):
    return [
        pl.BlockSpec((a.shape[0], a.shape[1], 2 * tile), lambda j, first=first: (0, 0, first + j))
        for a, first in parts
    ]


def held(shape):
    return pl.BlockSpec(shape, lambda j: (0,) * len(shape))


def on_device(moves, tokens, timesteps, routes, ada, qkv, out_w, router, shared_in, shared_out, expert_in, expert_out, cotangent):
    micro, _, length, _ = tokens.shape
    count = micro * length
    n_dp, n_blk, ring = moves.n_dp, moves.n_blk, moves.ring
    experts = n_blk
    capacity = length * TOP // experts + max(2, length // 32)
    room = -(-n_blk * micro * capacity // 16) * 16
    shard = D // n_dp
    part = D // n_blk
    info = moves.info()
    dp_at = lax.axis_index("dp")
    rotate, swap, flip = moves.rotate, moves.swap, moves.flip

    tokens_2d = tokens.reshape(count, D)
    given = cotangent.reshape(count, D)
    routes_2d = routes.reshape(count, TOP)

    pack_a = jnp.concatenate([qkv, out_w], axis=1)
    tile = shared_in.shape[1]
    pack_b = by_tile(shared_in, shared_out.T, tile)
    ff = expert_in.shape[2]
    e_out = expert_out[0].T
    shares = 2 if ring else 1
    first_half, last_half = (
        by_tile(expert_in[0][:, c : c + ff // 2], e_out[:, c : c + ff // 2], tile)
        for c in (0, ff // 2)
    )
    side = dp_at % 2 == 0


    half = D // 2
    column = jnp.arange(D)
    frequency = jnp.exp(-math.log(10000.0) * (column % half).astype(F32) / half)
    angles = timesteps.astype(F32) * frequency
    cond = jax.nn.silu(jnp.where(column < half, jnp.cos(angles), jnp.sin(angles))).astype(BF16)
    cond = cond.reshape(micro, n_dp, shard).transpose(1, 0, 2)
    cond = lax.all_to_all(cond, "dp", 0, 0, tiled=True)
    if ring:
        maps_a = [[0, 1, 2, 3], [4, 5, 6, 7]]
        cond, pack_a, pack_b, first_half, last_half, tokens_2d, given = together(
            cond, pack_a, pack_b, first_half, last_half, tokens_2d, given
        )
        a1, a2, a3 = rotate(pack_a, 1), rotate(pack_a, 2), rotate(pack_a, -1)
        e_own = jnp.where(side, first_half, last_half)
        e_across = swap(jnp.where(side, last_half, first_half))
    else:
        weights_a, maps_a = [moves.whole(pack_a)], [[0]]

    wide = ada.shape[1]
    partial_mod = jnp.einsum("dmr,rc->dmc", cond, ada, preferred_element_type=F32)
    payload = jnp.concatenate(
        [
            partial_mod.reshape(n_dp, micro * wide),
            jnp.broadcast_to(router[:, 0].astype(F32)[None], (n_dp, shard)),
        ],
        axis=1,
    )
    arrived = lax.all_to_all(payload, "dp", 0, 0, tiled=True)
    far_tokens = flip(tokens_2d, 2)
    if ring:
        arrived, far_tokens, e_own, e_across, a1, a2, a3, given = together(
            arrived, far_tokens, e_own, e_across, a1, a2, a3, given
        )
        held_a = jnp.stack([pack_a, a1, a2, a3])
        weights_a = [held_a, swap(held_a)]
        pack_0 = jnp.stack([e_own, e_across])
        pack_1 = rotate(pack_0, 1)
    tokens_all = [tokens_2d, flip(tokens_2d, 1), far_tokens, flip(far_tokens, 1)]
    own_mod = jnp.sum(arrived[:, : micro * wide], axis=0)
    own_mod = jnp.concatenate([own_mod, arrived[:, micro * wide :].reshape(D)])
    gathered = lax.all_gather(own_mod, "blk", axis=0)
    if ring:
        gathered, weights_a, tokens_all, given = together(gathered, weights_a, tokens_all, given)
    near_given, far_given = flip(given, 1), flip(given, 2)
    mod = gathered[:, : micro * wide].reshape(n_blk, micro, wide)
    mod = mod.transpose(1, 0, 2).reshape(micro, 6, D)
    router_t = jnp.pad(gathered[:, micro * wide :].astype(BF16), ((0, LANES - n_blk), (0, 0)))

    group = shaped((n_blk, length, micro * part), BF16)
    normed_one, qkv_w, out_half, kept, near, far = call(
        functools.partial(qkv_kernel, moves, micro, maps_a),
        [
            shaped((n_blk, count, D), BF16),
            shaped((D, 3 * part), BF16),
            shaped((D // 2, 2 * part), BF16),
            group,
            group,
            group,
        ],
        "qkv",
        in_specs=[smem()] + [vmem()] * (n_blk + 1 + len(weights_a)),
        scratch_shapes=[pltpu.VMEM((D, part), BF16)],
    )(info, *tokens_all, mod, *weights_a)
    if ring:
        near, far, out_half, far_given, near_given, pack_0, pack_1 = together(
            near, far, out_half, far_given, near_given, pack_0, pack_1
        )
        pack_2 = rotate(pack_1, 1)
        b_0 = pack_b[None]
        b_1, b_x0 = rotate(b_0, 1), swap(b_0)
    near, far = flip(near, 1), flip(far, 2)
    if ring:
        near, far, out_half = together(near, far, out_half)
    projected = (kept, near, far)
    out_weights = [out_half] + [flip(out_half, bits) for bits in range(1, n_blk)]

    from_all = pltpu.VMEM((n_blk, n_blk, length, micro * part), BF16)
    mixed_out = call(
        functools.partial(attend_kernel, moves),
        group,
        "attend",
        in_specs=[smem()] + [vmem()] * 3,
        scratch_shapes=[from_all],
    )(info, *projected)
    mixed_in = lax.all_to_all(mixed_out, "blk", 0, 0, tiled=True)
    if ring:
        mixed_in, out_weights, pack_2, b_1, b_x0, far_given = together(
            mixed_in, out_weights, pack_2, b_1, b_x0, far_given
        )
    given_all = [given, near_given, far_given, flip(far_given, 1)]
    if ring:
        pack_3 = rotate(pack_2, 1)
        b_2, b_3 = rotate(b_1, 1), rotate(b_0, -1)
        b_x1 = swap(b_1)
    columns = D + LANES
    mixed, attended, residual, normed_two, probs, payload = call(
        functools.partial(residual_kernel, moves, micro),
        [
            shaped((count, D), BF16),
            shaped((count, D), F32),
            shaped((count, D), F32),
            shaped((count, D), BF16),
            shaped((count, LANES), F32),
            shaped((count, columns), BF16),
        ],
        "residual",
        in_specs=[smem()] + [vmem()] * (5 + n_blk),
        scratch_shapes=[pltpu.VMEM((n_blk, count, part), F32)],
    )(info, mixed_in, tokens_2d, mod, router_t, routes_2d, *out_weights)
    payloads = [payload, flip(payload, 1), flip(payload, 2)]
    if ring:
        payloads, given_all, b_x1 = together(payloads, given_all, b_x1)
    payloads.append(flip(payloads[2], 1))
    all_count = n_blk * count
    all_grads, hold, rows = call(
        functools.partial(pick_kernel, moves),
        [shaped((all_count, D), BF16), shaped((room, all_count), BF16), shaped((room, 2 * D), BF16)],
        "pick",
        in_specs=[smem()] + [vmem()] * (2 * n_blk + 1),
    )(info, *payloads, *given_all, mod)

    if ring:
        rows, hold, all_grads, pack_3 = together(rows, hold, all_grads, pack_3)
        rows_across = swap(rows)
        parts_e = [(p, 0) for p in (pack_0, pack_1, pack_2, pack_3)]
        maps_e = [[s, ring + s] for s in range(ring)]
        maps_b = [[0], [1], [2], [3], [4], [5], [6, 7]]
        out_maps_b = [[0, 1, 2, 3], [4, 5, 6, 7]]
    else:
        parts_e = [(moves.whole(jnp.concatenate([first_half, last_half], axis=1)), 0)]
        parts_b = [(moves.whole(pack_b), 0)]
        maps_e, maps_b, out_maps_b = [[0]], [[0]], [[0]]
    tiles = [pltpu.VMEM((D, tile), BF16) for _ in range(4)]
    steps = ff // tile // shares

    def routed_part(other, given_rows, parts, before):
        results = [((room, D), F32)] * 2 + [((room, LANES), F32)]
        if other:
            results = [((room, D), BF16), ((room, columns), BF16)]
        if ring:
            weight_specs = [vmem()] * len(parts)
            out_specs = [vmem()] * (len(results) + len(maps_e))
        else:
            weight_specs = block_specs(parts, tile)
            out_specs = [held(shape) for shape, _ in results] + weight_specs
        got = call(
            functools.partial(routed_kernel, moves, maps_e, maps_e, tile, bool(ring), other),
            [shaped(*r) for r in results]
            + [shaped((len(m), moves.rows, 2 * tile * steps), BF16) for m in maps_e],
            "routed",
            vmem_mib=None if ring else 48,
            grid=(steps,),
            in_specs=[smem(), vmem()] + weight_specs + [vmem()] * len(before),
            out_specs=out_specs,
            scratch_shapes=[pltpu.VMEM((room, D), F32)] * 2 + tiles,
        )(info, given_rows, *[a for a, _ in parts], *before)
        return got[: len(results)], got[len(results) :]

    (value, back, inner), got_e = routed_part(False, rows, parts_e, [])
    other_value, other_back = [], []
    if ring:
        got_e, rows_across, b_2, b_3 = together(got_e, rows_across, b_2, b_3)
        b_x23 = swap(jnp.concatenate([b_2, b_3]))
        (send_value, send_back), got_e = routed_part(True, rows_across, parts_e, got_e)
        got_e, value, back, send_value, send_back, all_grads, b_x23 = together(
            got_e, value, back, send_value, send_back, all_grads, b_x23
        )
        other_back = [swap(send_back)]
        e_two, e_one = rotate(got_e[2], 1), rotate(got_e[1], -1)
        parts_b = [(b, 0) for b in (b_0, b_1, b_2, b_3, b_x0, b_x1, b_x23)]
    slot_shape = (moves.rows, 2 * tile)
    got_b = call(
        functools.partial(shared_kernel, moves, maps_b, out_maps_b, tile),
        [shaped((all_count, D), BF16)] * 2
        + [shaped((len(m),) + slot_shape, BF16) for m in out_maps_b],
        "shared",
        in_specs=[smem()] + [vmem()] * (n_blk + 1 + len(parts_b)),
        scratch_shapes=[pltpu.VMEM((all_count, D), BF16)]
        + [pltpu.VMEM((all_count, D), F32)] * 2
        + tiles,
    )(info, *payloads, all_grads, *[a for a, _ in parts_b])
    shared, own_b, other_b = got_b[:2], got_b[2], got_b[-1]
    if ring:
        other_back, e_two, send_value, shared, own_b, other_b, got_e = together(
            other_back, e_two, send_value, shared, own_b, other_b, got_e
        )
        other_value = [swap(send_value)]
    keep, send = call(
        functools.partial(back_kernel, moves),
        [shaped((2, count, columns), BF16)] * 2,
        "back",
        in_specs=[smem()] + [vmem()] * (4 + len(other_back)),
    )(info, hold, shared[1], back, inner, *other_back)

    total = add(keep, flip(send, 1)).astype(BF16)
    near, far = total[0], flip(total[1], 2)
    if ring:
        near, far, other_b, got_e, e_two = together(near, far, other_b, got_e, e_two)
        across_b = swap(other_b)
        e_three = rotate(add(got_e[3], e_two).astype(BF16), 1)

    halves = 2 if ring else 1
    out_rows = (2, moves.slots // halves, moves.rows, halves * part)
    grad_residual, grad_mod_two, grad_router, out_keep, out_send, grad_mixed = call(
        functools.partial(middle_kernel, moves, micro),
        [
            shaped((count, D), F32),
            shaped((micro, 3, D), F32),
            shaped((LANES, D), F32),
            shaped(out_rows, BF16),
            shaped(out_rows, BF16),
            group,
        ],
        "middle",
        in_specs=[smem()] + [vmem()] * (10 + n_blk),
        scratch_shapes=[
            pltpu.VMEM((count, D), BF16),
            pltpu.VMEM((D, part), BF16),
            pltpu.VMEM((n_blk, count, part), BF16),
        ],
    )(
        info, near, far, probs, residual, attended, mixed, normed_two, mod, router_t, given, *out_weights,
    )

    if ring:
        grad_mixed, out_send, e_one, other_value = together(
            grad_mixed, out_send, e_one, other_value
        )
    grad_mixed = lax.all_to_all(grad_mixed, "blk", 0, 0, tiled=True)
    out_sums = add(out_keep, flip(out_send, 1)).astype(BF16)
    if ring:
        grad_mixed, out_sums = together(grad_mixed, out_sums)
    out_far = flip(out_sums[1], 2)
    kept, near, far = call(
        functools.partial(attend_back_kernel, moves),
        [group] * 3,
        "attend_back",
        in_specs=[smem()] + [vmem()] * 4,
        scratch_shapes=[from_all, from_all],
    )(info, *projected, grad_mixed)
    if ring:
        near, far, out_far, e_three, across_b, own_b, got_e = together(
            near, far, out_far, e_three, across_b, own_b, got_e
        )
        total = add(got_e[0], e_one) + e_three.astype(F32)
        e_across = swap(total[1].astype(BF16))
        sums_b = add(own_b, across_b).astype(BF16)
        b_two, b_one = rotate(sums_b[2], 1), rotate(sums_b[1], -1)
    near, far = flip(near, 1), flip(far, 2)
    mix_keep, mix_send, grad_gate = call(
        functools.partial(mixture_kernel, moves),
        [shaped((2, count, D), BF16)] * 2 + [shaped((micro, 1, D), F32)],
        "mixture",
        in_specs=[smem()] + [vmem()] * (4 + 2 * n_blk + len(other_value)),
    )(info, hold, shared[0], value, mod, *payloads, *given_all, *other_value)
    if ring:
        near, far, mix_send, b_two, e_across, sums_b = together(
            near, far, mix_send, b_two, e_across, sums_b
        )
        b_three = rotate(add(sums_b[3], b_two).astype(BF16), 1)
    mix_total = add(mix_keep, flip(mix_send, 1)).astype(BF16)
    got = call(
        functools.partial(qkv_grad_kernel, moves, micro, maps_a),
        [shaped(w.shape, BF16) for w in weights_a]
        + [shaped((2, count, D), BF16)] * 2
        + [shaped((micro, 2, D), F32)],
        "qkv_grad",
        in_specs=[smem()] + [vmem()] * (8 + n_blk),
        scratch_shapes=[
            from_all,
            pltpu.VMEM((n_blk, count, 3 * part), BF16),
            pltpu.VMEM((D, 3 * part), BF16),
        ],
    )(info, kept, near, far, out_sums[0], out_far, normed_one, qkv_w, *tokens_all, mod)
    qkv_parts, (one_keep, one_send, grad_mod_one) = got[:-3], got[-3:]
    if ring:
        qkv_parts, one_keep, one_send, grad_mod_one, mix_total, b_one, sums_b = together(
            qkv_parts, one_keep, one_send, grad_mod_one, mix_total, b_one, sums_b
        )
        qkv_across = swap(qkv_parts[1])

    grad_mod = jnp.concatenate([grad_mod_one, grad_mod_two, grad_gate], axis=1)
    grad_mod = grad_mod.reshape(micro, n_blk, wide)
    payload = jnp.concatenate(
        [
            jnp.broadcast_to(
                grad_mod.transpose(1, 0, 2).reshape(1, n_blk, micro * wide), (n_dp, n_blk, micro * wide)
            ),
            grad_router[:n_blk].reshape(n_blk, n_dp, shard).transpose(1, 0, 2),
        ],
        axis=2,
    ).reshape(n_dp * n_blk, -1)
    one_sums = add(one_keep, flip(one_send, 1)).astype(BF16)
    if ring:
        one_sums, payload = together(one_sums, payload)
    arrived = lax.all_to_all(payload, ("dp", "blk"), 0, 0, tiled=True)
    near, far = one_sums[0], flip(one_sums[1], 2)

    if ring:
        e_mine, e_across = total[0], e_across.astype(F32)
        sums_e = [jnp.where(side, e_mine, e_across), jnp.where(side, e_across, e_mine)]
        expert_in_grad, expert_out_t = from_tiles(sums_e, tile)
        expert_out_grad = expert_out_t.T
        near, far, qkv_across, qkv_parts, mix_total, expert_in_grad, expert_out_grad, b_three, arrived = together(
            near, far, qkv_across, qkv_parts, mix_total, expert_in_grad, expert_out_grad, b_three, arrived
        )
        mine = add(qkv_parts[0], qkv_across).astype(BF16)
        qkv_2, qkv_1, qkv_3 = rotate(mine[2], 2), rotate(mine[1], -1), rotate(mine[3], 1)
        sums_b = add(sums_b[0], b_one) + b_three.astype(F32)
    else:
        sums_b = moves.fold_whole(own_b[0])
        expert_in_grad, expert_out_t = from_tiles([moves.fold_whole(got_e[0][0])], tile)
        expert_out_grad = expert_out_t.T
    mix_far = flip(mix_total[1], 2)
    tokens_grad = call(
        functools.partial(tokens_grad_kernel, micro),
        shaped((count, D), F32),
        "tokens_grad",
    )(near, far, tokens_2d, mod, grad_residual)
    shared_in_grad, shared_out_t = from_tiles([sums_b], tile)
    shared_out_grad = shared_out_t.T
    arrived = arrived.reshape(n_dp, n_blk, -1)
    item_mod = jnp.sum(arrived[:, :, : micro * wide], axis=1).reshape(n_dp * micro, wide)
    ada_grad = jnp.dot(
        cond.reshape(n_dp * micro, shard).astype(F32).T, item_mod, precision=lax.Precision.HIGHEST
    )
    router_grad = jnp.sum(arrived[:, :, micro * wide :], axis=(0, 1))[:, None]
    block_out = call(
        functools.partial(block_out_kernel, micro), shaped((count, D), BF16), "block_out"
    )(mix_total[0], mix_far, residual, mod)
    if ring:
        tokens_grad, block_out, qkv_1, qkv_2, qkv_3, ada_grad, router_grad, shared_in_grad, shared_out_grad = together(
            tokens_grad, block_out, qkv_1, qkv_2, qkv_3, ada_grad, router_grad, shared_in_grad, shared_out_grad
        )
        last = add(mine[0], qkv_2) + add(qkv_1, qkv_3)
    else:
        last = moves.fold_whole(qkv_parts[0][0])
    qkv_grad, out_grad = last[:, : 3 * part], last[:, 3 * part :]
    return (
        block_out.reshape(tokens.shape),
        tokens_grad.reshape(tokens.shape),
        ada_grad,
        qkv_grad,
        out_grad,
        router_grad,
        shared_in_grad,
        shared_out_grad,
        expert_in_grad[None],
        expert_out_grad[None],
    )


def solution(mesh):
    moves = Moves(mesh)
    in_specs = (
        P(None, "dp", "blk", None),
        P(None, "dp"),
        P(None, "dp", "blk", None),
        P("dp", "blk"),
        P("dp", "blk"),
        P("dp", "blk"),
        P("dp", "blk"),
        P("dp", "blk"),
        P("blk", "dp"),
        P("blk", "dp", None),
        P("blk", None, "dp"),
        P(None, "dp", "blk", None),
    )
    out_specs = (
        P(None, "dp", "blk", None),
        P(None, "dp", "blk", None),
        P("dp", "blk"),
        P("dp", "blk"),
        P("dp", "blk"),
        P("dp", "blk"),
        P("dp", "blk"),
        P("blk", "dp"),
        P("blk", "dp", None),
        P("blk", None, "dp"),
    )
    return jax.shard_map(
        functools.partial(on_device, moves),
        mesh=mesh,
        in_specs=in_specs,
        out_specs=out_specs,
        check_vma=False,
    )
```

```python
import copy
import functools
import math

import jax
import jax.numpy as jnp
from jax import lax
from jax.experimental import pallas as pl
from jax.experimental.pallas import tpu as pltpu
from jax.sharding import PartitionSpec as P

D = 768
HEADS = 12
HEAD_DIM = 64
TOP = 2
LANES = 128
F32 = jnp.float32
BF16 = jnp.bfloat16
NN = (((1,), (0,)), ((), ()))
NT = (((1,), (1,)), ((), ()))
TN = (((0,), (0,)), ((), ()))
EPS_NORM = 1e-06
GELU_C = math.sqrt(2.0 / math.pi)
GELU_A = 0.044715
VMEM_MIB = {
    "out_weight": 4,
    "shared_sum": 4,
    "slot_sum": 4,
    "last_sum": 4,
    "qkv": 10,
    "attend": 10,
    "residual": 10,
    "pick": 12,
    "routed": 24,
    "shared": 28,
    "back": 8,
    "middle": 10,
    "attend_back": 14,
    "mixture": 10,
    "qkv_grad": 14,
    "tokens_grad": 8,
    "block_out": 8,
}


def mm(left, right, dims=NN):
    return lax.dot_general(left, right, dims, preferred_element_type=F32)


def call(kernel, out_shape, name, vmem_mib=None, **kwargs):
    def run(*operands):
        if "grid" not in kwargs:
            kwargs.setdefault("in_specs", [vmem()] * len(operands))
            kwargs["out_specs"] = jax.tree.map(lambda _: vmem(), out_shape)
        limit = (vmem_mib or VMEM_MIB[name]) * 1024 * 1024
        return pl.pallas_call(
            kernel,
            out_shape=out_shape,
            name=name,
            compiler_params=pltpu.CompilerParams(vmem_limit_bytes=limit),
            **kwargs,
        )(*operands)

    return run


def smem():
    return pl.BlockSpec(memory_space=pltpu.SMEM)


def vmem():
    return pl.BlockSpec(memory_space=pltpu.VMEM)


def shaped(shape, dtype):
    return jax.ShapeDtypeStruct(shape, dtype)


class Moves:
    def __init__(self, mesh):
        self.n_dp, self.n_blk = mesh.shape["dp"], mesh.shape["blk"]
        self.ring = 4 if self.n_dp == 8 else 0
        self.rows = D // self.n_dp if self.ring else D
        self.slots = 8 if self.ring else 1

    def info(self):
        dp, blk = lax.axis_index("dp"), lax.axis_index("blk")
        if self.ring:
            z, x = dp // 2, dp % 2
            offs = [
                (2 * ((z + self.ring - step) % self.ring) + (x ^ flip)) * self.rows
                for flip in range(2)
                for step in range(self.ring)
            ]
        else:
            offs = [jnp.zeros((), jnp.int32)]
        return jnp.stack(offs + [blk]).astype(jnp.int32)

    def rotate(self, array, steps=1):
        pairs = [(d, (d + 2 * steps) % self.n_dp) for d in range(self.n_dp)]
        return lax.ppermute(array, "dp", pairs)

    def swap(self, array):
        return lax.ppermute(array, "dp", [(d, d ^ 1) for d in range(self.n_dp)])

    def flip(self, array, bit):
        return lax.ppermute(array, "blk", [(b, b ^ bit) for b in range(self.n_blk)])

    def whole_rows(self):
        rows = copy.copy(self)
        rows.rows, rows.slots = D, 1
        return rows

    def whole(self, shard):
        return lax.all_gather(shard, "dp", axis=0, tiled=True)[None]

    def fold_whole(self, part):
        return lax.psum_scatter(part, "dp", scatter_dimension=0, tiled=True).astype(F32)


def together(*arrays):
    return lax.optimization_barrier(arrays)


def after(value, wait):
    return lax.optimization_barrier((value, wait))[0]


def add(left, right):
    return left.astype(F32) + right.astype(F32)


def normed(rows):
    mean = jnp.mean(rows, axis=-1, keepdims=True)
    centered = rows - mean
    var = jnp.mean(centered * centered, axis=-1, keepdims=True)
    inverse = lax.rsqrt(var + EPS_NORM)
    return centered * inverse, inverse


def norm_back(hat, inverse, grad_hat):
    mean_grad = jnp.mean(grad_hat, axis=-1, keepdims=True)
    mean_both = jnp.mean(grad_hat * hat, axis=-1, keepdims=True)
    return inverse * (grad_hat - mean_grad - hat * mean_both)


def column_sum(rows):
    return jnp.sum(rows, axis=0, keepdims=True)


def place_slots(moves, info, refs, maps, out, start, width):
    if not isinstance(start, int):
        start = pl.multiple_of(start, LANES)
    for ref, slots in zip(refs, maps):
        for k, j in enumerate(slots):
            at = pl.ds(pl.multiple_of(info[j], moves.rows), moves.rows)
            out[at, :] = ref[k, :, pl.ds(start, width)]


def take_slots(moves, info, source, refs, maps, start, before=None):
    width = source.shape[1]
    if not isinstance(start, int):
        start = pl.multiple_of(start, LANES)
    columns = pl.ds(start, width)
    for i, (ref, slots) in enumerate(zip(refs, maps)):
        for k, j in enumerate(slots):
            at = pl.ds(pl.multiple_of(info[j], moves.rows), moves.rows)
            if before:
                total = source[at, :].astype(F32) + before[i][k, :, columns].astype(F32)
                ref[k, :, columns] = total.astype(BF16)
            else:
                ref[k, :, columns] = source[at, :]


def out_weight_kernel(moves, maps, info, *refs):
    weights, (out, held) = refs[: len(maps)], refs[len(maps) :]
    part, half = held.shape[1], D // 2
    place_slots(moves, info, weights, maps, held, 3 * part, part)
    for i in range(2):
        out[:, i * part : (i + 1) * part] = held[i * half : (i + 1) * half, :]


def qkv_kernel(moves, micro, maps, info, *refs):
    n_blk = moves.n_blk
    tokens, mod, refs = refs[:n_blk], refs[n_blk], refs[n_blk + 1 :]
    weights, refs = refs[: len(maps)], refs[len(maps) :]
    normed_out, weight_out, kept, near, far = refs
    length = tokens[0].shape[0] // micro
    part = D // n_blk
    own = info[moves.slots]
    place_slots(moves, info, weights, maps, weight_out, 0, 3 * part)
    for rel in range(n_blk):
        block = own ^ rel
        for m in range(micro):
            rows = slice(m * length, (m + 1) * length)
            hat, _ = normed(tokens[rel][rows, :].astype(F32))
            values = hat * (1.0 + mod[m, 1:2, :]) + mod[m, 0:1, :]
            normed_out[block, rows, :] = values.astype(BF16)
        projected = mm(normed_out[block], weight_out[...])
        first, last = projected[:, :part], projected[:, 2 * part :]
        even = own % 2 == 0
        groups = (
            (kept, jnp.where(even, first, last)),
            (near, projected[:, part : 2 * part]),
            (far, jnp.where(even, last, first)),
        )
        for out, group in groups:
            for m in range(micro):
                out[block, :, m * part : (m + 1) * part] = group[
                    m * length : (m + 1) * length
                ].astype(BF16)


def by_source(own, kept, near, far, out):
    out[own] = kept[...]
    out[own ^ 1] = near[...]
    out[own ^ 2] = far[...]


def head_rows(ref, source, start):
    block = ref[source, :, :, start : start + HEAD_DIM]
    return block.reshape(block.shape[0] * block.shape[1], HEAD_DIM)


SCORE_SCALE = 1.0 / math.sqrt(HEAD_DIM)


def head_parts(moves, info, projected, start):
    n_blk, own = moves.n_blk, info[moves.slots]
    query, key, value = (
        head_rows(projected, (i * n_blk + own) // 3, start) for i in range(3)
    )
    return query * jnp.asarray(SCORE_SCALE, BF16), key, value


def softmax_rows(query, key):
    scores = mm(query, key, NT)
    raised = jnp.exp(scores - jnp.max(scores, axis=-1, keepdims=True))
    return raised, 1.0 / jnp.sum(raised, axis=-1, keepdims=True)


def attend_kernel(moves, info, kept, near, far, out, projected):
    n_blk, length, columns = out.shape
    by_source(info[moves.slots], kept, near, far, projected)
    for start in range(0, columns, HEAD_DIM):
        query, key, value = head_parts(moves, info, projected, start)
        raised, inverse = softmax_rows(query, key)
        mixed = mm((raised * inverse).astype(BF16), value).astype(BF16)
        out[:, :, start : start + HEAD_DIM] = mixed.reshape(n_blk, length, HEAD_DIM)


def attend_back_kernel(
    moves, info, kept, near, far, grad_mixed, kept_out, near_out, far_out, projected, out
):
    n_blk, own = moves.n_blk, info[moves.slots]
    _, length, columns = grad_mixed.shape
    by_source(own, kept, near, far, projected)
    for start in range(0, columns, HEAD_DIM):
        query, key, value = head_parts(moves, info, projected, start)
        grad = grad_mixed[:, :, start : start + HEAD_DIM].reshape(n_blk * length, HEAD_DIM)
        raised, inverse = softmax_rows(query, key)
        probs = raised * inverse
        grad_probs = mm(grad, value, NT)
        inner = jnp.sum(probs * grad_probs, axis=-1, keepdims=True)
        grad_scores = (probs * (grad_probs - inner)).astype(BF16)
        grads = (
            mm(grad_scores, key) * SCORE_SCALE,
            mm(grad_scores, query, TN),
            mm(probs.astype(BF16), grad, TN),
        )
        for i, part_grad in enumerate(grads):
            out[(i * n_blk + own) // 3, :, :, start : start + HEAD_DIM] = part_grad.astype(
                BF16
            ).reshape(n_blk, length, HEAD_DIM)
    kept_out[...] = out[own]
    near_out[...] = out[own ^ 1]
    far_out[...] = out[own ^ 2]


def thirds(values):
    first = values.astype(BF16)
    rest = values - first.astype(F32)
    second = rest.astype(BF16)
    return first, second, (rest - second.astype(F32)).astype(BF16)


def lane_thirds(values, count):
    parts = [third[:, :count] for third in thirds(values)]
    parts.append(jnp.zeros((values.shape[0], LANES - 3 * count), BF16))
    return jnp.concatenate(parts, axis=1)


def from_thirds(lanes, count):
    lanes = lanes.astype(F32)
    return lanes[:, :count] + lanes[:, count : 2 * count] + lanes[:, 2 * count : 3 * count]


def residual_kernel(moves, micro, info, mixed_in, tokens, mod, router, routes, *refs):
    n_blk, own = moves.n_blk, info[moves.slots]
    out_weights, refs = refs[:n_blk], refs[n_blk:]
    mixed, attended, residual, normed_two, probs, payload, parts = refs
    part, half = D // n_blk, D // 2
    length = tokens.shape[0] // micro
    for h in range(n_blk):
        for m in range(micro):
            mixed[m * length : (m + 1) * length, h * part : (h + 1) * part] = mixed_in[
                h, :, m * part : (m + 1) * part
            ]
    left, right = mixed[:, :half], mixed[:, half:]
    for rel in range(n_blk):
        weight = out_weights[rel]
        parts[own ^ rel] = mm(left, weight[:, :part]) + mm(right, weight[:, part:])
    for b in range(n_blk):
        attended[:, b * part : (b + 1) * part] = parts[b]
    for m in range(micro):
        rows = slice(m * length, (m + 1) * length)
        stream = tokens[rows, :].astype(F32) + mod[m, 2:3, :] * attended[rows, :]
        residual[rows, :] = stream
        hat, _ = normed(stream)
        two = (hat * (1.0 + mod[m, 4:5, :]) + mod[m, 3:4, :]).astype(BF16)
        normed_two[rows, :] = two
        payload[rows, :D] = two
    logits = mm(normed_two[...], router[...], NT)
    lanes = lax.broadcasted_iota(jnp.int32, logits.shape, 1)
    picks = [lanes == routes[:, k : k + 1] for k in range(TOP)]
    chosen = [jnp.sum(jnp.where(p, logits, 0.0), axis=-1, keepdims=True) for p in picks]
    top = functools.reduce(jnp.maximum, chosen)
    raised = [jnp.exp(value - top) for value in chosen]
    total = functools.reduce(jnp.add, raised)
    gates = functools.reduce(
        jnp.add, [jnp.where(p, value / total, 0.0) for p, value in zip(picks, raised)]
    )
    probs[...] = gates
    payload[:, D:] = lane_thirds(gates, n_blk)


def expert_step(
    info, moves, maps, out_maps, tile, rows, grads, totals, weights, outs, scratch, base=0, before=None
):
    w_in, w_out, g_in, g_out = scratch
    place_slots(moves, info, weights, maps, w_in, base, tile)
    place_slots(moves, info, weights, maps, w_out, base + tile, tile)
    pre = mm(rows, w_in[...])
    squared = pre * pre
    bend = jnp.tanh(GELU_C * pre * (1.0 + GELU_A * squared))
    half = 0.5 * (1.0 + bend)
    act = (pre * half).astype(BF16)
    slope = half + 0.5 * pre * (1.0 - bend * bend) * (GELU_C * (1.0 + 3.0 * GELU_A * squared))
    totals[0][...] += mm(act, w_out[...], NT)
    grad_pre = (mm(grads, w_out[...]) * slope).astype(BF16)
    totals[1][...] += mm(grad_pre, w_in[...], NT)
    g_in[...] = mm(rows, grad_pre, TN).astype(BF16)
    g_out[...] = mm(grads, act, TN).astype(BF16)
    take_slots(moves, info, g_in, outs, out_maps, base, before)
    take_slots(moves, info, g_out, outs, out_maps, base + tile, before)


def own_lanes(values, own, count):
    lanes = lax.broadcasted_iota(jnp.int32, values.shape, 1)
    mine = jnp.logical_and(lanes % count == own, lanes < 3 * count)
    return jnp.sum(jnp.where(mine, values.astype(F32), 0.0), axis=-1, keepdims=True)


def pick_kernel(moves, info, *refs):
    n_blk, own = moves.n_blk, info[moves.slots]
    payload, gradients, mod, refs = refs[:n_blk], refs[n_blk : 2 * n_blk], refs[2 * n_blk], refs[2 * n_blk + 1 :]
    all_grads, hold_t, rows, hold = refs
    count, micro = payload[0].shape[0], mod.shape[0]
    length = count // micro
    for rel in range(n_blk):
        for m in range(micro):
            mixed = gradients[rel][m * length : (m + 1) * length, :].astype(F32) * mod[m, 5:6, :]
            start = rel * count + m * length
            all_grads[start : start + length, :] = mixed.astype(BF16)
    gates = jnp.concatenate([ref[:, D:] for ref in payload])
    column = own_lanes(gates, own, n_blk)
    all_count = n_blk * count
    named = jnp.broadcast_to((column > 0.0).astype(F32), (all_count, LANES))
    row = named.T[:8, :]
    ranks = row
    lanes = lax.broadcasted_iota(jnp.int32, row.shape, 1)
    shift = 1
    while shift < all_count:
        ranks = ranks + jnp.where(lanes >= shift, pltpu.roll(ranks, shift, 1), 0.0)
        shift *= 2
    places = ranks * row - 1.0
    index = lax.broadcasted_iota(jnp.int32, hold.shape, 0)
    hold[...] = (index == places[:1, :].astype(jnp.int32)).astype(BF16)
    places = jnp.broadcast_to(places[:1, :], (LANES, all_count)).T[:, :1].astype(jnp.int32)
    index = lax.broadcasted_iota(jnp.int32, hold_t.shape, 1)
    hold_t[...] = (index == places).astype(BF16)
    slot_gate = own_lanes(mm(hold[...], gates), own, n_blk)
    rows[:, :D] = mm(hold[...], jnp.concatenate([ref[:, :D] for ref in payload])).astype(BF16)
    rows[:, D:] = (slot_gate * mm(hold[...], all_grads[...])).astype(BF16)


def shared_kernel(moves, maps, out_maps, tile, info, *refs):
    n_blk = moves.n_blk
    payload, grads, refs = refs[:n_blk], refs[n_blk], refs[n_blk + 1 :]
    weights, refs = refs[: len(maps)], refs[len(maps) :]
    results, outs, refs = refs[:2], refs[2 : 2 + len(out_maps)], refs[2 + len(out_maps) :]
    rows, totals, scratch = refs[0], refs[1:3], refs[3:]
    count = payload[0].shape[0]
    for rel in range(n_blk):
        rows[rel * count : (rel + 1) * count, :] = payload[rel][:, :D]
    for total in totals:
        total[...] = jnp.zeros_like(total)
    expert_step(
        info, moves, maps, out_maps, tile, rows[...], grads[...], totals, weights, outs, scratch
    )
    for result, total in zip(results, totals):
        result[...] = total[...].astype(BF16)


def routed_kernel(moves, maps, out_maps, tile, whole, unrolled, other, info, given, *refs):
    n_blk, own = moves.n_blk, info[moves.slots]
    weights, refs = refs[: len(maps)], refs[len(maps) :]
    before, refs = (refs[: len(out_maps)], refs[len(out_maps) :]) if other else ([], refs)
    results, refs = (refs[:2], refs[2:]) if other else (refs[:3], refs[3:])
    outs, refs = refs[: len(out_maps)], refs[len(out_maps) :]
    totals, scratch = refs[:2], refs[2:]

    def clear():
        for total in totals:
            total[...] = jnp.zeros_like(total)

    def one_tile(base):
        expert_step(
            info, moves, maps, out_maps, tile, given[:, :D], given[:, D:], totals, weights, outs, scratch, base, before
        )

    def finish():
        value, back = totals[0][...], totals[1][...]
        inner = jnp.sum(given[:, D:].astype(F32) * value, axis=-1, keepdims=True)
        lanes = lax.broadcasted_iota(jnp.int32, (value.shape[0], LANES), 1)
        inner = jnp.where(lanes == own, inner, 0.0)
        if other:
            results[0][...] = value.astype(BF16)
            results[1][:, :D] = back.astype(BF16)
            results[1][:, D:] = lane_thirds(inner, n_blk)
        else:
            results[0][...], results[1][...], results[2][...] = value, back, inner

    if unrolled:
        clear()
        for step in range(unrolled):
            one_tile(step * 2 * tile)
        finish()
    else:
        step = pl.program_id(0)
        pl.when(step == 0)(clear)
        one_tile(step * 2 * tile if whole else 0)
        pl.when(step == pl.num_programs(0) - 1)(finish)


def back_kernel(moves, info, hold, shared, back, inner, *refs):
    n_blk, own = moves.n_blk, info[moves.slots]
    *other, keep, send = refs
    total, product = back[...], inner[...]
    if other:
        total = total + other[0][:, :D].astype(F32)
        more = own_lanes(other[0][:, D:], own, n_blk)
        lanes = lax.broadcasted_iota(jnp.int32, product.shape, 1)
        product = product + jnp.where(lanes == own, more, 0.0)
    total, product = total.astype(BF16), lane_thirds(product, n_blk)
    count = keep.shape[1]
    for rel in range(n_blk):
        at = slice(rel * count, (rel + 1) * count)
        target = (send if rel % 2 else keep).at[rel // 2]
        here = hold[at, :]
        target[:, :D] = (shared[at, :].astype(F32) + mm(here, total)).astype(BF16)
        target[:, D:] = mm(here, product).astype(BF16)


def mixture_kernel(moves, info, hold, shared, value, mod, *refs):
    n_blk, own, micro = moves.n_blk, info[moves.slots], mod.shape[0]
    payload, gradients, refs = refs[:n_blk], refs[n_blk : 2 * n_blk], refs[2 * n_blk :]
    *other, keep, send, grad_gate = refs
    total = value[...]
    if other:
        total = total + other[0][...].astype(F32)
    total = total.astype(BF16)
    count = keep.shape[1]
    length = count // micro
    sums = [0.0] * micro
    for rel in range(n_blk):
        at = slice(rel * count, (rel + 1) * count)
        target = (send if rel % 2 else keep).at[rel // 2]
        gate = own_lanes(payload[rel][:, D:], own, n_blk)
        mixture = shared[at, :].astype(F32) + gate * mm(hold[at, :], total)
        target[...] = mixture.astype(BF16)
        product = mixture * gradients[rel][...].astype(F32)
        for m in range(micro):
            sums[m] = sums[m] + column_sum(product[m * length : (m + 1) * length])
    for m in range(micro):
        grad_gate[m] = sums[m]


def middle_kernel(
    moves, micro, info, near, far, probs, residual, attended, mixed, normed_two, mod, router, cotangent, *refs
):
    n_blk, own = moves.n_blk, info[moves.slots]
    out_weights, refs = refs[:n_blk], refs[n_blk:]
    grad_residual, grad_mod, grad_router, keep, send, grad_mixed, grad_attended, wide, blocks = refs
    part, half = D // n_blk, D // 2
    length = residual.shape[0] // micro
    given = cotangent[...].astype(F32)
    gates = probs[:, :n_blk]
    inner = from_thirds(near[:, D:], n_blk) + from_thirds(far[:, D:], n_blk)
    chosen = inner - gates * jnp.sum(inner, axis=-1, keepdims=True)
    grad_logits = jnp.concatenate(
        [chosen, jnp.zeros((chosen.shape[0], LANES - n_blk), F32)], axis=1
    ).astype(BF16)
    grad_router[...] = mm(grad_logits, normed_two[...], TN)
    grad_two = (
        near[:, :D].astype(F32)
        + far[:, :D].astype(F32)
        + mm(grad_logits, router[...])
    )
    for m in range(micro):
        rows = slice(m * length, (m + 1) * length)
        hat, inverse = normed(residual[rows, :])
        mine = grad_two[rows]
        grad_mod[m, 1:2, :] = column_sum(mine)
        grad_mod[m, 2:3, :] = column_sum(mine * hat)
        total = given[rows] + norm_back(hat, inverse, mine * (1.0 + mod[m, 4:5, :]))
        grad_residual[rows, :] = total
        grad_mod[m, 0:1, :] = column_sum(total * attended[rows, :])
        grad_attended[rows, :] = (total * mod[m, 2:3, :]).astype(BF16)
    for b in range(n_blk):
        blocks[b] = grad_attended[:, b * part : (b + 1) * part]
    left, right = 0.0, 0.0
    for rel in range(n_blk):
        weight, grad = out_weights[rel], blocks[own ^ rel]
        left = left + mm(grad, weight[:, :part], NT)
        right = right + mm(grad, weight[:, part:], NT)
    back_mixed = jnp.concatenate([left, right], axis=1).astype(BF16)
    for h in range(n_blk):
        for m in range(micro):
            grad_mixed[h, :, m * part : (m + 1) * part] = back_mixed[
                m * length : (m + 1) * length, h * part : (h + 1) * part
            ]
    all_mixed = mixed[...]
    for rel in range(n_blk):
        wide[...] = mm(all_mixed, blocks[own ^ rel], TN).astype(BF16)
        target = (send if rel % 2 else keep).at[rel // 2]
        groups = target.shape[0]
        for j in range(moves.slots):
            at = pl.ds(pl.multiple_of(info[j], moves.rows), moves.rows)
            start = j // groups * part
            target[j % groups, :, start : start + part] = wide[at, :]


def sum_kernel(count, left, right, *outs):
    for i in range(count):
        outs[i][0] = (left[i].astype(F32) + right[i].astype(F32)).astype(outs[i].dtype)


def last_kernel(first, second, third, fourth, left, right):
    total = first[0] + second[0].astype(F32) + third[0].astype(F32) + fourth[0].astype(F32)
    left[...] = total[:, : left.shape[1]]
    right[...] = total[:, left.shape[1] :]


def block_out_kernel(micro, near, far, residual, mod, block_out):
    mixture = near[...].astype(F32) + far[...].astype(F32)
    length = residual.shape[0] // micro
    for m in range(micro):
        rows = slice(m * length, (m + 1) * length)
        block_out[rows, :] = (residual[rows, :] + mod[m, 5:6, :] * mixture[rows]).astype(BF16)


def qkv_grad_kernel(moves, micro, maps, info, kept, near, far, out_near, out_far, normed_one, weight, *refs):
    n_blk, own = moves.n_blk, info[moves.slots]
    tokens, mod, refs = refs[:n_blk], refs[n_blk], refs[n_blk + 1 :]
    outs, refs = refs[: len(maps)], refs[len(maps) :]
    keep, send, grad_mod, arrived, blocks, wide = refs
    by_source(own, kept, near, far, arrived)
    part = D // n_blk
    length = arrived.shape[2]
    count = micro * length
    for j in range(3):
        source = (3 * own + j) % n_blk
        for b in range(n_blk):
            for m in range(micro):
                blocks[b, m * length : (m + 1) * length, j * part : (j + 1) * part] = arrived[
                    source, b, :, m * part : (m + 1) * part
                ]
    every = blocks[...].reshape(n_blk * count, 3 * part)
    wide[...] = mm(normed_one[...].reshape(n_blk * count, D), every, TN).astype(BF16)
    take_slots(moves, info, wide, outs, maps, 0)
    out_grad = (out_near[...].astype(F32) + out_far[...].astype(F32)).astype(BF16)
    groups = out_near.shape[0]
    for ref, slots in zip(outs, maps):
        for k, j in enumerate(slots):
            start = j // groups * part
            ref[k, :, 3 * part :] = out_grad[j % groups, :, start : start + part]
    sums = [[0.0, 0.0] for _ in range(micro)]
    for rel in range(n_blk):
        back = mm(blocks[own ^ rel], weight[...], NT)
        target = send if rel % 2 else keep
        target[rel // 2] = back.astype(BF16)
        for m in range(micro):
            rows = slice(m * length, (m + 1) * length)
            hat, _ = normed(tokens[rel][rows, :].astype(F32))
            sums[m][0] += column_sum(back[rows])
            sums[m][1] += column_sum(back[rows] * hat)
    for m in range(micro):
        for i in range(2):
            grad_mod[m, i : i + 1, :] = sums[m][i]


def tokens_grad_kernel(micro, near, far, tokens, mod, grad_residual, out):
    grad_one = near[...].astype(F32) + far[...].astype(F32)
    length = tokens.shape[0] // micro
    for m in range(micro):
        rows = slice(m * length, (m + 1) * length)
        hat, inverse = normed(tokens[rows, :].astype(F32))
        own = grad_one[rows]
        out[rows, :] = grad_residual[rows, :] + norm_back(hat, inverse, own * (1.0 + mod[m, 1:2, :]))


def by_tile(left, right, tile):
    parts = []
    for start in range(0, left.shape[1], tile):
        parts += [left[:, start : start + tile], right[:, start : start + tile]]
    return jnp.concatenate(parts, axis=1)


def from_tiles(packed, tile):
    parts = [
        [array[:, start : start + tile] for array in packed for start in range(first, array.shape[1], 2 * tile)]
        for first in (0, tile)
    ]
    return [jnp.concatenate(part, axis=1) for part in parts]


def block_specs(parts, tile):
    return [
        pl.BlockSpec((a.shape[0], a.shape[1], 2 * tile), lambda j, first=first: (0, 0, first + j))
        for a, first in parts
    ]


def held(shape):
    return pl.BlockSpec(shape, lambda j: (0,) * len(shape))


def on_device(moves, tokens, timesteps, routes, ada, qkv, out_w, router, shared_in, shared_out, expert_in, expert_out, cotangent):
    micro, _, length, _ = tokens.shape
    count = micro * length
    n_dp, n_blk, ring = moves.n_dp, moves.n_blk, moves.ring
    experts = n_blk
    capacity = length * TOP // experts + max(2, length // 32)
    room = -(-n_blk * micro * capacity // 16) * 16
    shard = D // n_dp
    part = D // n_blk
    info = moves.info()
    dp_at = lax.axis_index("dp")
    rotate, swap, flip = moves.rotate, moves.swap, moves.flip

    tokens_2d = tokens.reshape(count, D)
    given = cotangent.reshape(count, D)
    routes_2d = routes.reshape(count, TOP)

    pack_a = jnp.concatenate([qkv, out_w], axis=1)
    tile = shared_in.shape[1]
    pack_b = by_tile(shared_in, shared_out.T, tile)
    ff = expert_in.shape[2]
    e_out = expert_out[0].T
    shares = 2 if ring else 1
    first_half, last_half = (
        by_tile(expert_in[0][:, c : c + ff // 2], e_out[:, c : c + ff // 2], tile)
        for c in (0, ff // 2)
    )
    side = dp_at % 2 == 0


    half = D // 2
    column = jnp.arange(D)
    frequency = jnp.exp(-math.log(10000.0) * (column % half).astype(F32) / half)
    angles = timesteps.astype(F32) * frequency
    cond = jax.nn.silu(jnp.where(column < half, jnp.cos(angles), jnp.sin(angles))).astype(BF16)
    cond = cond.reshape(micro, n_dp, shard).transpose(1, 0, 2)
    cond = lax.all_to_all(cond, "dp", 0, 0, tiled=True)
    if ring:
        maps_a = [[0, 1, 2, 3], [4, 5, 6, 7]]
        cond, pack_a, pack_b, first_half, last_half, tokens_2d, given = together(
            cond, pack_a, pack_b, first_half, last_half, tokens_2d, given
        )
        a1, a2, a3 = rotate(pack_a, 1), rotate(pack_a, 2), rotate(pack_a, -1)
        e_own = jnp.where(side, first_half, last_half)
        e_across = swap(jnp.where(side, last_half, first_half))
    else:
        weights_a, maps_a = [moves.whole(pack_a)], [[0]]

    wide = ada.shape[1]
    partial_mod = jnp.einsum("dmr,rc->dmc", cond, ada, preferred_element_type=F32)
    payload = jnp.concatenate(
        [
            partial_mod.reshape(n_dp, micro * wide),
            jnp.broadcast_to(router[:, 0].astype(F32)[None], (n_dp, shard)),
        ],
        axis=1,
    )
    arrived = lax.all_to_all(payload, "dp", 0, 0, tiled=True)
    far_tokens = flip(tokens_2d, 2)
    if ring:
        arrived, far_tokens, e_own, e_across, a1, a2, a3, given = together(
            arrived, far_tokens, e_own, e_across, a1, a2, a3, given
        )
        held_a = jnp.stack([pack_a, a1, a2, a3])
        weights_a = [held_a, swap(held_a)]
        pack_0 = jnp.stack([e_own, e_across])
        pack_1 = rotate(pack_0, 1)
    tokens_all = [tokens_2d, flip(tokens_2d, 1), far_tokens, flip(far_tokens, 1)]
    own_mod = jnp.sum(arrived[:, : micro * wide], axis=0)
    own_mod = jnp.concatenate([own_mod, arrived[:, micro * wide :].reshape(D)])
    gathered = lax.all_gather(own_mod, "blk", axis=0)
    if ring:
        gathered, weights_a, tokens_all, given = together(gathered, weights_a, tokens_all, given)
    near_given = flip(given, 1)
    mod = gathered[:, : micro * wide].reshape(n_blk, micro, wide)
    mod = mod.transpose(1, 0, 2).reshape(micro, 6, D)
    router_t = jnp.pad(gathered[:, micro * wide :].astype(BF16), ((0, LANES - n_blk), (0, 0)))

    group = shaped((n_blk, length, micro * part), BF16)
    out_half = call(
        functools.partial(out_weight_kernel, moves, maps_a),
        shaped((D // 2, 2 * part), BF16),
        "out_weight",
        in_specs=[smem()] + [vmem()] * len(weights_a),
        scratch_shapes=[pltpu.VMEM((D, part), BF16)],
    )(info, *weights_a)
    out_weights = [out_half, flip(out_half, 1), flip(out_half, 2)]
    normed_one, qkv_w, kept, near, far = call(
        functools.partial(qkv_kernel, moves, micro, maps_a),
        [shaped((n_blk, count, D), BF16), shaped((D, 3 * part), BF16), group, group, group],
        "qkv",
        in_specs=[smem()] + [vmem()] * (n_blk + 1 + len(weights_a)),
    )(info, *tokens_all, mod, *weights_a)
    if ring:
        near, far, out_weights, near_given, given, pack_0, pack_1 = together(
            near, far, out_weights, near_given, given, pack_0, pack_1
        )
        pack_2 = rotate(pack_1, 1)
        b_across = swap(pack_b)
    near, far = flip(near, 1), flip(far, 2)
    out_weights.append(flip(out_weights[2], 1))
    if ring:
        near, far, out_weights, b_across, given = together(near, far, out_weights, b_across, given)
    projected = (kept, near, far)
    far_given = flip(given, 2)

    from_all = pltpu.VMEM((n_blk, n_blk, length, micro * part), BF16)
    mixed_out = call(
        functools.partial(attend_kernel, moves),
        group,
        "attend",
        in_specs=[smem()] + [vmem()] * 3,
        scratch_shapes=[from_all],
    )(info, *projected)
    mixed_in = lax.all_to_all(mixed_out, "blk", 0, 0, tiled=True)
    if ring:
        mixed_in, out_weights, pack_2, far_given = together(
            mixed_in, out_weights, pack_2, far_given
        )
        b_0 = jnp.stack([pack_b, b_across])
    given_all = [given, near_given, far_given, flip(far_given, 1)]
    if ring:
        pack_3 = rotate(pack_2, 1)
    columns = D + LANES
    mixed, attended, residual, normed_two, probs, payload = call(
        functools.partial(residual_kernel, moves, micro),
        [
            shaped((count, D), BF16),
            shaped((count, D), F32),
            shaped((count, D), F32),
            shaped((count, D), BF16),
            shaped((count, LANES), F32),
            shaped((count, columns), BF16),
        ],
        "residual",
        in_specs=[smem()] + [vmem()] * (5 + n_blk),
        scratch_shapes=[pltpu.VMEM((n_blk, count, part), F32)],
    )(info, mixed_in, tokens_2d, mod, router_t, routes_2d, *out_weights)
    payloads = [payload, flip(payload, 1), flip(payload, 2)]
    if ring:
        payloads, given_all, b_0 = together(payloads, given_all, b_0)
    payloads.append(flip(payloads[2], 1))
    all_count = n_blk * count
    all_grads, hold, rows = call(
        functools.partial(pick_kernel, moves),
        [shaped((all_count, D), BF16), shaped((all_count, room), BF16), shaped((room, 2 * D), BF16)],
        "pick",
        scratch_shapes=[pltpu.VMEM((room, all_count), BF16)],
        in_specs=[smem()] + [vmem()] * (2 * n_blk + 1),
    )(info, *payloads, *given_all, mod)

    if ring:
        rows, hold, all_grads, pack_3 = together(rows, hold, all_grads, pack_3)
        rows_across = swap(rows)
        b_1, b_2, b_3 = rotate(b_0, 1), rotate(b_0, 2), rotate(b_0, -1)
        parts_e = [(p, 0) for p in (pack_0, pack_1, pack_2, pack_3)]
        maps_e = [[s, ring + s] for s in range(ring)]
        maps_b = maps_e
        out_maps_b = [[0, 1, 2, 3], [4, 5, 6, 7]]
    else:
        parts_e = [(moves.whole(jnp.concatenate([first_half, last_half], axis=1)), 0)]
        parts_b = [(moves.whole(pack_b), 0)]
        maps_e, maps_b, out_maps_b = [[0]], [[0]], [[0]]
    tiles = [pltpu.VMEM((D, tile), BF16) for _ in range(4)]
    steps = ff // tile // shares

    def routed_part(other, given_rows, parts, before):
        results = [((room, D), F32)] * 2 + [((room, LANES), F32)]
        unrolled = steps if ring else 0
        if other:
            results = [((room, D), BF16), ((room, columns), BF16)]
        if ring:
            weight_specs = [vmem()] * len(parts)
            out_specs = [vmem()] * (len(results) + len(maps_e))
        else:
            weight_specs = block_specs(parts, tile)
            out_specs = [held(shape) for shape, _ in results] + weight_specs
        got = call(
            functools.partial(routed_kernel, moves, maps_e, maps_e, tile, bool(ring), unrolled, other),
            [shaped(*r) for r in results]
            + [shaped((len(m), moves.rows, 2 * tile * steps), BF16) for m in maps_e],
            "routed",
            vmem_mib=None if ring else 48,
            **({} if unrolled else {"grid": (steps,)}),
            in_specs=[smem(), vmem()] + weight_specs + [vmem()] * len(before),
            out_specs=out_specs,
            scratch_shapes=[pltpu.VMEM((room, D), F32)] * 2 + tiles,
        )(info, given_rows, *[a for a, _ in parts], *before)
        return got[: len(results)], got[len(results) :]

    (value, back, inner), got_e = routed_part(False, rows, parts_e, [])
    other_value, other_back = [], []
    if ring:
        got_e, rows_across, b_1 = together(got_e, rows_across, b_1)
        (send_value, send_back), got_e = routed_part(True, rows_across, parts_e, got_e)
        got_e, value, back, send_value, send_back, all_grads, b_2, b_3 = together(
            got_e, value, back, send_value, send_back, all_grads, b_2, b_3
        )
        other_back = [swap(send_back)]
        e_two, e_one = rotate(got_e[2], 1), rotate(got_e[1], -1)
        parts_b = [(b, 0) for b in (b_0, b_1, b_2, b_3)]
    slot_shape = (moves.rows, 2 * tile)
    got_b = call(
        functools.partial(shared_kernel, moves, maps_b, out_maps_b, tile),
        [shaped((all_count, D), BF16)] * 2
        + [shaped((len(m),) + slot_shape, BF16) for m in out_maps_b],
        "shared",
        in_specs=[smem()] + [vmem()] * (n_blk + 1 + len(parts_b)),
        scratch_shapes=[pltpu.VMEM((all_count, D), BF16)]
        + [pltpu.VMEM((all_count, D), F32)] * 2
        + tiles,
    )(info, *payloads, all_grads, *[a for a, _ in parts_b])
    shared, own_b, other_b = got_b[:2], got_b[2], got_b[-1]
    if ring:
        other_back, e_two, send_value, shared, own_b, other_b, got_e = together(
            other_back, e_two, send_value, shared, own_b, other_b, got_e
        )
        other_value = [swap(send_value)]
    keep, send = call(
        functools.partial(back_kernel, moves),
        [shaped((2, count, columns), BF16)] * 2,
        "back",
        in_specs=[smem()] + [vmem()] * (4 + len(other_back)),
    )(info, hold, shared[1], back, inner, *other_back)

    crossed = flip(send, 1)
    near, far = (add(keep[i], crossed[i]).astype(BF16) for i in range(2))
    far = flip(far, 2)
    if ring:
        near, far, other_b, got_e, e_two = together(near, far, other_b, got_e, e_two)
        across_b = swap(other_b)
        e_three = rotate(add(got_e[3], e_two).astype(BF16), 1)

    halves = 2 if ring else 1
    out_rows = (2, moves.slots // halves, moves.rows, halves * part)
    grad_residual, grad_mod_two, grad_router, out_keep, out_send, grad_mixed = call(
        functools.partial(middle_kernel, moves, micro),
        [
            shaped((count, D), F32),
            shaped((micro, 3, D), F32),
            shaped((LANES, D), F32),
            shaped(out_rows, BF16),
            shaped(out_rows, BF16),
            group,
        ],
        "middle",
        in_specs=[smem()] + [vmem()] * (10 + n_blk),
        scratch_shapes=[
            pltpu.VMEM((count, D), BF16),
            pltpu.VMEM((D, part), BF16),
            pltpu.VMEM((n_blk, count, part), BF16),
        ],
    )(
        info, near, far, probs, residual, attended, mixed, normed_two, mod, router_t, given, *out_weights,
    )

    if ring:
        grad_mixed, out_send, e_one, other_value = together(
            grad_mixed, out_send, e_one, other_value
        )
    grad_mixed = lax.all_to_all(grad_mixed, "blk", 0, 0, tiled=True)
    crossed = flip(out_send, 1)
    out_sums = [add(out_keep[i], crossed[i]).astype(BF16) for i in range(2)]
    mix_keep, mix_send, grad_gate = call(
        functools.partial(mixture_kernel, moves),
        [shaped((2, count, D), BF16)] * 2 + [shaped((micro, 1, D), F32)],
        "mixture",
        in_specs=[smem()] + [vmem()] * (4 + 2 * n_blk + len(other_value)),
    )(info, hold, shared[0], value, mod, *payloads, *given_all, *other_value)
    if ring:
        grad_mixed, out_sums, mix_send, across_b, own_b = together(
            grad_mixed, out_sums, mix_send, across_b, own_b
        )
        sums_b = call(
            functools.partial(sum_kernel, ring),
            [shaped((1,) + slot_shape, BF16) for _ in range(ring)],
            "shared_sum",
        )(own_b, across_b)
    out_far = flip(out_sums[1], 2)
    mix_crossed = flip(mix_send, 1)
    mix_total = [add(mix_keep[i], mix_crossed[i]).astype(BF16) for i in range(2)]
    kept, near, far = call(
        functools.partial(attend_back_kernel, moves),
        [group] * 3,
        "attend_back",
        in_specs=[smem()] + [vmem()] * 4,
        scratch_shapes=[from_all, from_all],
    )(info, *projected, grad_mixed)
    if ring:
        near, far, out_far, e_three, got_e, mix_total, sums_b = together(
            near, far, out_far, e_three, got_e, mix_total, sums_b
        )
        e_across = swap((add(got_e[0][1], e_one[1]) + e_three[1].astype(F32)).astype(BF16))
        b_parts = [rotate(sums_b[s], steps) for s, steps in ((2, 2), (1, -1), (3, 1))]
    near, far = flip(near, 1), flip(far, 2)
    if ring:
        near, far, mix_total = together(near, far, mix_total)
    mix_far = flip(mix_total[1], 2)
    got = call(
        functools.partial(qkv_grad_kernel, moves, micro, maps_a),
        [shaped(w.shape, BF16) for w in weights_a]
        + [shaped((2, count, D), BF16)] * 2
        + [shaped((micro, 2, D), F32)],
        "qkv_grad",
        in_specs=[smem()] + [vmem()] * (8 + n_blk),
        scratch_shapes=[
            from_all,
            pltpu.VMEM((n_blk, count, 3 * part), BF16),
            pltpu.VMEM((D, 3 * part), BF16),
        ],
    )(info, kept, near, far, out_sums[0], out_far, normed_one, qkv_w, *tokens_all, mod)
    qkv_parts, (one_keep, one_send, grad_mod_one) = got[:-3], got[-3:]
    if ring:
        qkv_parts, one_keep, one_send, grad_mod_one, e_across, b_parts[0] = together(
            qkv_parts, one_keep, one_send, grad_mod_one, e_across, b_parts[0]
        )
        qkv_across = swap(qkv_parts[1])

    grad_mod = jnp.concatenate([grad_mod_one, grad_mod_two, grad_gate], axis=1)
    grad_mod = grad_mod.reshape(micro, n_blk, wide)
    payload = jnp.concatenate(
        [
            jnp.broadcast_to(
                grad_mod.transpose(1, 0, 2).reshape(1, n_blk, micro * wide), (n_dp, n_blk, micro * wide)
            ),
            grad_router[:n_blk].reshape(n_blk, n_dp, shard).transpose(1, 0, 2),
        ],
        axis=2,
    ).reshape(n_dp * n_blk, -1)
    crossed = flip(one_send, 1)
    one_near, one_far = (add(one_keep[i], crossed[i]).astype(BF16) for i in range(2))
    if ring:
        one_near, one_far, payload = together(one_near, one_far, payload)
    one_far = flip(one_far, 2)
    arrived = lax.all_to_all(payload, ("dp", "blk"), 0, 0, tiled=True)

    if ring:
        e_across = after(e_across, one_near).astype(F32)
        e_mine = add(got_e[0][0], e_one[0]) + e_three[0].astype(F32)
        sums_e = [jnp.where(side, e_mine, e_across), jnp.where(side, e_across, e_mine)]
        expert_in_grad, expert_out_t = from_tiles(sums_e, tile)
        expert_out_grad = expert_out_t.T
        one_near, one_far, qkv_across, qkv_parts, mix_far, expert_in_grad, expert_out_grad, b_parts, sums_b, arrived = together(
            one_near, one_far, qkv_across, qkv_parts, mix_far, expert_in_grad, expert_out_grad, b_parts, sums_b, arrived
        )
        mine = call(
            functools.partial(sum_kernel, ring),
            [shaped((1,) + qkv_across.shape[1:], BF16 if s else F32) for s in range(ring)],
            "slot_sum",
        )(qkv_parts[0], qkv_across)
        qkv_2, qkv_1, qkv_3 = (rotate(mine[s], steps) for s, steps in ((2, 2), (1, -1), (3, 1)))
        sums_b = (add(sums_b[0], b_parts[0]) + add(b_parts[1], b_parts[2]))[0]
    else:
        sums_b = moves.fold_whole(own_b[0])
        expert_in_grad, expert_out_t = from_tiles([moves.fold_whole(got_e[0][0])], tile)
        expert_out_grad = expert_out_t.T
    tokens_grad = call(
        functools.partial(tokens_grad_kernel, micro),
        shaped((count, D), F32),
        "tokens_grad",
    )(one_near, one_far, tokens_2d, mod, grad_residual)
    shared_in_grad, shared_out_t = from_tiles([sums_b], tile)
    shared_out_grad = shared_out_t.T
    arrived = arrived.reshape(n_dp, n_blk, -1)
    item_mod = jnp.sum(arrived[:, :, : micro * wide], axis=1).reshape(n_dp * micro, wide)
    ada_grad = jnp.dot(
        cond.reshape(n_dp * micro, shard).astype(F32).T, item_mod, precision=lax.Precision.HIGHEST
    )
    router_grad = jnp.sum(arrived[:, :, micro * wide :], axis=(0, 1))[:, None]
    block_out = call(
        functools.partial(block_out_kernel, micro), shaped((count, D), BF16), "block_out"
    )(mix_total[0], mix_far, residual, mod)
    if ring:
        tokens_grad, block_out, qkv_1, qkv_2, qkv_3, ada_grad, router_grad, shared_in_grad, shared_out_grad = together(
            tokens_grad, block_out, qkv_1, qkv_2, qkv_3, ada_grad, router_grad, shared_in_grad, shared_out_grad
        )
        qkv_grad, out_grad = call(
            last_kernel,
            [shaped((shard, 3 * part), F32), shaped((shard, part), F32)],
            "last_sum",
        )(mine[0], qkv_1, qkv_2, qkv_3)
    else:
        last = moves.fold_whole(qkv_parts[0][0])
        qkv_grad, out_grad = last[:, : 3 * part], last[:, 3 * part :]
    return (
        block_out.reshape(tokens.shape),
        tokens_grad.reshape(tokens.shape),
        ada_grad,
        qkv_grad,
        out_grad,
        router_grad,
        shared_in_grad,
        shared_out_grad,
        expert_in_grad[None],
        expert_out_grad[None],
    )


def solution(mesh):
    moves = Moves(mesh)
    in_specs = (
        P(None, "dp", "blk", None),
        P(None, "dp"),
        P(None, "dp", "blk", None),
        P("dp", "blk"),
        P("dp", "blk"),
        P("dp", "blk"),
        P("dp", "blk"),
        P("dp", "blk"),
        P("blk", "dp"),
        P("blk", "dp", None),
        P("blk", None, "dp"),
        P(None, "dp", "blk", None),
    )
    out_specs = (
        P(None, "dp", "blk", None),
        P(None, "dp", "blk", None),
        P("dp", "blk"),
        P("dp", "blk"),
        P("dp", "blk"),
        P("dp", "blk"),
        P("dp", "blk"),
        P("blk", "dp"),
        P("blk", "dp", None),
        P("blk", None, "dp"),
    )
    return jax.shard_map(
        functools.partial(on_device, moves),
        mesh=mesh,
        in_specs=in_specs,
        out_specs=out_specs,
        check_vma=False,
    )
```

```python
import copy
import functools
import math

import jax
import jax.numpy as jnp
from jax import lax
from jax.experimental import pallas as pl
from jax.experimental.pallas import tpu as pltpu
from jax.sharding import PartitionSpec as P

D = 768
HEADS = 12
HEAD_DIM = 64
TOP = 2
LANES = 128
F32 = jnp.float32
BF16 = jnp.bfloat16
NN = (((1,), (0,)), ((), ()))
NT = (((1,), (1,)), ((), ()))
TN = (((0,), (0,)), ((), ()))
EPS_NORM = 1e-06
GELU_C = math.sqrt(2.0 / math.pi)
GELU_A = 0.044715
VMEM_MIB = {
    "out_weight": 4,
    "shared_sum": 4,
    "slot_sum": 4,
    "last_sum": 4,
    "qkv": 10,
    "attend": 10,
    "residual": 10,
    "pick": 12,
    "routed": 24,
    "shared": 28,
    "back": 8,
    "middle": 10,
    "attend_back": 14,
    "mixture": 10,
    "qkv_grad": 14,
    "tokens_grad": 8,
    "block_out": 8,
}


def mm(left, right, dims=NN):
    return lax.dot_general(left, right, dims, preferred_element_type=F32)


def call(kernel, out_shape, name, vmem_mib=None, **kwargs):
    def run(*operands):
        if "grid" not in kwargs:
            kwargs.setdefault("in_specs", [vmem()] * len(operands))
            kwargs["out_specs"] = jax.tree.map(lambda _: vmem(), out_shape)
        limit = (vmem_mib or VMEM_MIB[name]) * 1024 * 1024
        return pl.pallas_call(
            kernel,
            out_shape=out_shape,
            name=name,
            compiler_params=pltpu.CompilerParams(vmem_limit_bytes=limit),
            **kwargs,
        )(*operands)

    return run


def smem():
    return pl.BlockSpec(memory_space=pltpu.SMEM)


def vmem():
    return pl.BlockSpec(memory_space=pltpu.VMEM)


def shaped(shape, dtype):
    return jax.ShapeDtypeStruct(shape, dtype)


class Moves:
    def __init__(self, mesh):
        self.n_dp, self.n_blk = mesh.shape["dp"], mesh.shape["blk"]
        self.ring = 4 if self.n_dp == 8 else 0
        self.rows = D // self.n_dp if self.ring else D
        self.slots = 8 if self.ring else 1

    def info(self):
        dp, blk = lax.axis_index("dp"), lax.axis_index("blk")
        if self.ring:
            z, x = dp // 2, dp % 2
            offs = [
                (2 * ((z + self.ring - step) % self.ring) + (x ^ flip)) * self.rows
                for flip in range(2)
                for step in range(self.ring)
            ]
        else:
            offs = [jnp.zeros((), jnp.int32)]
        return jnp.stack(offs + [blk]).astype(jnp.int32)

    def rotate(self, array, steps=1):
        pairs = [(d, (d + 2 * steps) % self.n_dp) for d in range(self.n_dp)]
        return lax.ppermute(array, "dp", pairs)

    def swap(self, array):
        return lax.ppermute(array, "dp", [(d, d ^ 1) for d in range(self.n_dp)])

    def flip(self, array, bit):
        return lax.ppermute(array, "blk", [(b, b ^ bit) for b in range(self.n_blk)])

    def whole_rows(self):
        rows = copy.copy(self)
        rows.rows, rows.slots = D, 1
        return rows

    def whole(self, shard):
        return lax.all_gather(shard, "dp", axis=0, tiled=True)[None]

    def fold_whole(self, part):
        return lax.psum_scatter(part, "dp", scatter_dimension=0, tiled=True).astype(F32)


def together(*arrays):
    return lax.optimization_barrier(arrays)


def after(value, wait):
    return lax.optimization_barrier((value, wait))[0]


def add(left, right):
    return left.astype(F32) + right.astype(F32)


def normed(rows):
    mean = jnp.mean(rows, axis=-1, keepdims=True)
    centered = rows - mean
    var = jnp.mean(centered * centered, axis=-1, keepdims=True)
    inverse = lax.rsqrt(var + EPS_NORM)
    return centered * inverse, inverse


def norm_back(hat, inverse, grad_hat):
    mean_grad = jnp.mean(grad_hat, axis=-1, keepdims=True)
    mean_both = jnp.mean(grad_hat * hat, axis=-1, keepdims=True)
    return inverse * (grad_hat - mean_grad - hat * mean_both)


def column_sum(rows):
    return jnp.sum(rows, axis=0, keepdims=True)


def place_slots(moves, info, refs, maps, out, start, width):
    if not isinstance(start, int):
        start = pl.multiple_of(start, LANES)
    for ref, slots in zip(refs, maps):
        for k, j in enumerate(slots):
            at = pl.ds(pl.multiple_of(info[j], moves.rows), moves.rows)
            out[at, :] = ref[k, :, pl.ds(start, width)]


def take_slots(moves, info, source, refs, maps, start, before=None):
    width = source.shape[1]
    if not isinstance(start, int):
        start = pl.multiple_of(start, LANES)
    columns = pl.ds(start, width)
    for i, (ref, slots) in enumerate(zip(refs, maps)):
        for k, j in enumerate(slots):
            at = pl.ds(pl.multiple_of(info[j], moves.rows), moves.rows)
            if before:
                total = source[at, :].astype(F32) + before[i][k, :, columns].astype(F32)
                ref[k, :, columns] = total.astype(BF16)
            else:
                ref[k, :, columns] = source[at, :]


def out_weight_kernel(moves, maps, info, *refs):
    weights, (out, held) = refs[: len(maps)], refs[len(maps) :]
    part, half = held.shape[1], D // 2
    place_slots(moves, info, weights, maps, held, 3 * part, part)
    for i in range(2):
        out[:, i * part : (i + 1) * part] = held[i * half : (i + 1) * half, :]


def qkv_kernel(moves, micro, maps, info, *refs):
    n_blk = moves.n_blk
    tokens, mod, refs = refs[:n_blk], refs[n_blk], refs[n_blk + 1 :]
    weights, refs = refs[: len(maps)], refs[len(maps) :]
    normed_out, weight_out, kept, near, far = refs
    length = tokens[0].shape[0] // micro
    part = D // n_blk
    own = info[moves.slots]
    place_slots(moves, info, weights, maps, weight_out, 0, 3 * part)
    for rel in range(n_blk):
        block = own ^ rel
        for m in range(micro):
            rows = slice(m * length, (m + 1) * length)
            hat, _ = normed(tokens[rel][rows, :].astype(F32))
            values = hat * (1.0 + mod[m, 1:2, :]) + mod[m, 0:1, :]
            normed_out[block, rows, :] = values.astype(BF16)
        projected = mm(normed_out[block], weight_out[...])
        first, last = projected[:, :part], projected[:, 2 * part :]
        even = own % 2 == 0
        groups = (
            (kept, jnp.where(even, first, last)),
            (near, projected[:, part : 2 * part]),
            (far, jnp.where(even, last, first)),
        )
        for out, group in groups:
            for m in range(micro):
                out[block, :, m * part : (m + 1) * part] = group[
                    m * length : (m + 1) * length
                ].astype(BF16)


def by_source(own, kept, near, far, out):
    out[own] = kept[...]
    out[own ^ 1] = near[...]
    out[own ^ 2] = far[...]


def head_rows(ref, source, start):
    block = ref[source, :, :, start : start + HEAD_DIM]
    return block.reshape(block.shape[0] * block.shape[1], HEAD_DIM)


SCORE_SCALE = 1.0 / math.sqrt(HEAD_DIM)


def head_parts(moves, info, projected, start):
    n_blk, own = moves.n_blk, info[moves.slots]
    query, key, value = (
        head_rows(projected, (i * n_blk + own) // 3, start) for i in range(3)
    )
    return query * jnp.asarray(SCORE_SCALE, BF16), key, value


def softmax_rows(query, key):
    scores = mm(query, key, NT)
    raised = jnp.exp(scores - jnp.max(scores, axis=-1, keepdims=True))
    return raised, 1.0 / jnp.sum(raised, axis=-1, keepdims=True)


def attend_kernel(moves, info, kept, near, far, out, projected):
    n_blk, length, columns = out.shape
    by_source(info[moves.slots], kept, near, far, projected)
    for start in range(0, columns, HEAD_DIM):
        query, key, value = head_parts(moves, info, projected, start)
        raised, inverse = softmax_rows(query, key)
        mixed = mm((raised * inverse).astype(BF16), value).astype(BF16)
        out[:, :, start : start + HEAD_DIM] = mixed.reshape(n_blk, length, HEAD_DIM)


def attend_back_kernel(
    moves, info, kept, near, far, grad_mixed, kept_out, near_out, far_out, projected, out
):
    n_blk, own = moves.n_blk, info[moves.slots]
    _, length, columns = grad_mixed.shape
    by_source(own, kept, near, far, projected)
    for start in range(0, columns, HEAD_DIM):
        query, key, value = head_parts(moves, info, projected, start)
        grad = grad_mixed[:, :, start : start + HEAD_DIM].reshape(n_blk * length, HEAD_DIM)
        raised, inverse = softmax_rows(query, key)
        probs = raised * inverse
        grad_probs = mm(grad, value, NT)
        inner = jnp.sum(probs * grad_probs, axis=-1, keepdims=True)
        grad_scores = (probs * (grad_probs - inner)).astype(BF16)
        grads = (
            mm(grad_scores, key) * SCORE_SCALE,
            mm(grad_scores, query, TN),
            mm(probs.astype(BF16), grad, TN),
        )
        for i, part_grad in enumerate(grads):
            out[(i * n_blk + own) // 3, :, :, start : start + HEAD_DIM] = part_grad.astype(
                BF16
            ).reshape(n_blk, length, HEAD_DIM)
    kept_out[...] = out[own]
    near_out[...] = out[own ^ 1]
    far_out[...] = out[own ^ 2]


def thirds(values):
    first = values.astype(BF16)
    rest = values - first.astype(F32)
    second = rest.astype(BF16)
    return first, second, (rest - second.astype(F32)).astype(BF16)


def lane_thirds(values, count):
    parts = [third[:, :count] for third in thirds(values)]
    parts.append(jnp.zeros((values.shape[0], LANES - 3 * count), BF16))
    return jnp.concatenate(parts, axis=1)


def from_thirds(lanes, count):
    lanes = lanes.astype(F32)
    return lanes[:, :count] + lanes[:, count : 2 * count] + lanes[:, 2 * count : 3 * count]


def residual_kernel(moves, micro, info, mixed_in, tokens, mod, router, routes, *refs):
    n_blk, own = moves.n_blk, info[moves.slots]
    out_weights, refs = refs[:n_blk], refs[n_blk:]
    mixed, attended, residual, normed_two, probs, payload, parts = refs
    part, half = D // n_blk, D // 2
    length = tokens.shape[0] // micro
    for h in range(n_blk):
        for m in range(micro):
            mixed[m * length : (m + 1) * length, h * part : (h + 1) * part] = mixed_in[
                h, :, m * part : (m + 1) * part
            ]
    left, right = mixed[:, :half], mixed[:, half:]
    for rel in range(n_blk):
        weight = out_weights[rel]
        parts[own ^ rel] = mm(left, weight[:, :part]) + mm(right, weight[:, part:])
    for b in range(n_blk):
        attended[:, b * part : (b + 1) * part] = parts[b]
    for m in range(micro):
        rows = slice(m * length, (m + 1) * length)
        stream = tokens[rows, :].astype(F32) + mod[m, 2:3, :] * attended[rows, :]
        residual[rows, :] = stream
        hat, _ = normed(stream)
        two = (hat * (1.0 + mod[m, 4:5, :]) + mod[m, 3:4, :]).astype(BF16)
        normed_two[rows, :] = two
        payload[rows, :D] = two
    logits = mm(normed_two[...], router[...], NT)
    lanes = lax.broadcasted_iota(jnp.int32, logits.shape, 1)
    picks = [lanes == routes[:, k : k + 1] for k in range(TOP)]
    chosen = [jnp.sum(jnp.where(p, logits, 0.0), axis=-1, keepdims=True) for p in picks]
    top = functools.reduce(jnp.maximum, chosen)
    raised = [jnp.exp(value - top) for value in chosen]
    total = functools.reduce(jnp.add, raised)
    gates = functools.reduce(
        jnp.add, [jnp.where(p, value / total, 0.0) for p, value in zip(picks, raised)]
    )
    probs[...] = gates
    payload[:, D:] = lane_thirds(gates, n_blk)


def expert_step(
    info, moves, maps, out_maps, tile, rows, grads, totals, weights, outs, scratch, base=0, before=None
):
    w_in, w_out, g_in, g_out = scratch
    place_slots(moves, info, weights, maps, w_in, base, tile)
    place_slots(moves, info, weights, maps, w_out, base + tile, tile)
    pre = mm(rows, w_in[...])
    squared = pre * pre
    bend = jnp.tanh(GELU_C * pre * (1.0 + GELU_A * squared))
    half = 0.5 * (1.0 + bend)
    act = (pre * half).astype(BF16)
    slope = half + 0.5 * pre * (1.0 - bend * bend) * (GELU_C * (1.0 + 3.0 * GELU_A * squared))
    totals[0][...] += mm(act, w_out[...], NT)
    grad_pre = (mm(grads, w_out[...]) * slope).astype(BF16)
    totals[1][...] += mm(grad_pre, w_in[...], NT)
    g_in[...] = mm(rows, grad_pre, TN).astype(BF16)
    g_out[...] = mm(grads, act, TN).astype(BF16)
    take_slots(moves, info, g_in, outs, out_maps, base, before)
    take_slots(moves, info, g_out, outs, out_maps, base + tile, before)


def own_lanes(values, own, count):
    lanes = lax.broadcasted_iota(jnp.int32, values.shape, 1)
    mine = jnp.logical_and(lanes % count == own, lanes < 3 * count)
    return jnp.sum(jnp.where(mine, values.astype(F32), 0.0), axis=-1, keepdims=True)


def pick_kernel(moves, info, *refs):
    n_blk, own = moves.n_blk, info[moves.slots]
    payload, gradients, mod, refs = refs[:n_blk], refs[n_blk : 2 * n_blk], refs[2 * n_blk], refs[2 * n_blk + 1 :]
    all_grads, hold_t, rows, hold = refs
    count, micro = payload[0].shape[0], mod.shape[0]
    length = count // micro
    for rel in range(n_blk):
        for m in range(micro):
            mixed = gradients[rel][m * length : (m + 1) * length, :].astype(F32) * mod[m, 5:6, :]
            start = rel * count + m * length
            all_grads[start : start + length, :] = mixed.astype(BF16)
    gates = jnp.concatenate([ref[:, D:] for ref in payload])
    column = own_lanes(gates, own, n_blk)
    all_count = n_blk * count
    named = jnp.broadcast_to((column > 0.0).astype(F32), (all_count, LANES))
    row = named.T[:8, :]
    ranks = row
    lanes = lax.broadcasted_iota(jnp.int32, row.shape, 1)
    shift = 1
    while shift < all_count:
        ranks = ranks + jnp.where(lanes >= shift, pltpu.roll(ranks, shift, 1), 0.0)
        shift *= 2
    places = ranks * row - 1.0
    index = lax.broadcasted_iota(jnp.int32, hold.shape, 0)
    hold[...] = (index == places[:1, :].astype(jnp.int32)).astype(BF16)
    places = jnp.broadcast_to(places[:1, :], (LANES, all_count)).T[:, :1].astype(jnp.int32)
    index = lax.broadcasted_iota(jnp.int32, hold_t.shape, 1)
    hold_t[...] = (index == places).astype(BF16)
    slot_gate = own_lanes(mm(hold[...], gates), own, n_blk)
    rows[:, :D] = mm(hold[...], jnp.concatenate([ref[:, :D] for ref in payload])).astype(BF16)
    rows[:, D:] = (slot_gate * mm(hold[...], all_grads[...])).astype(BF16)


def shared_kernel(moves, maps, out_maps, tile, info, *refs):
    n_blk = moves.n_blk
    payload, grads, refs = refs[:n_blk], refs[n_blk], refs[n_blk + 1 :]
    weights, refs = refs[: len(maps)], refs[len(maps) :]
    results, outs, refs = refs[:2], refs[2 : 2 + len(out_maps)], refs[2 + len(out_maps) :]
    rows, totals, scratch = refs[0], refs[1:3], refs[3:]
    count = payload[0].shape[0]
    for rel in range(n_blk):
        rows[rel * count : (rel + 1) * count, :] = payload[rel][:, :D]
    for total in totals:
        total[...] = jnp.zeros_like(total)
    expert_step(
        info, moves, maps, out_maps, tile, rows[...], grads[...], totals, weights, outs, scratch
    )
    for result, total in zip(results, totals):
        result[...] = total[...].astype(BF16)


def routed_kernel(moves, maps, out_maps, tile, whole, unrolled, other, info, given, *refs):
    n_blk, own = moves.n_blk, info[moves.slots]
    weights, refs = refs[: len(maps)], refs[len(maps) :]
    before, refs = (refs[: len(out_maps)], refs[len(out_maps) :]) if other else ([], refs)
    results, refs = (refs[:2], refs[2:]) if other else (refs[:3], refs[3:])
    outs, refs = refs[: len(out_maps)], refs[len(out_maps) :]
    totals, scratch = refs[:2], refs[2:]

    def clear():
        for total in totals:
            total[...] = jnp.zeros_like(total)

    def one_tile(base):
        expert_step(
            info, moves, maps, out_maps, tile, given[:, :D], given[:, D:], totals, weights, outs, scratch, base, before
        )

    def finish():
        value, back = totals[0][...], totals[1][...]
        inner = jnp.sum(given[:, D:].astype(F32) * value, axis=-1, keepdims=True)
        lanes = lax.broadcasted_iota(jnp.int32, (value.shape[0], LANES), 1)
        inner = jnp.where(lanes == own, inner, 0.0)
        if other:
            results[0][...] = value.astype(BF16)
            results[1][:, :D] = back.astype(BF16)
            results[1][:, D:] = lane_thirds(inner, n_blk)
        else:
            results[0][...], results[1][...], results[2][...] = value, back, inner

    if unrolled:
        clear()
        for step in range(unrolled):
            one_tile(step * 2 * tile)
        finish()
    else:
        step = pl.program_id(0)
        pl.when(step == 0)(clear)
        one_tile(step * 2 * tile if whole else 0)
        pl.when(step == pl.num_programs(0) - 1)(finish)


def back_kernel(moves, info, hold, shared, back, inner, *refs):
    n_blk, own = moves.n_blk, info[moves.slots]
    *other, keep, send = refs
    total, product = back[...], inner[...]
    if other:
        total = total + other[0][:, :D].astype(F32)
        more = own_lanes(other[0][:, D:], own, n_blk)
        lanes = lax.broadcasted_iota(jnp.int32, product.shape, 1)
        product = product + jnp.where(lanes == own, more, 0.0)
    total, product = total.astype(BF16), lane_thirds(product, n_blk)
    count = keep.shape[1]
    for rel in range(n_blk):
        at = slice(rel * count, (rel + 1) * count)
        target = (send if rel % 2 else keep).at[rel // 2]
        here = hold[at, :]
        target[:, :D] = (shared[at, :].astype(F32) + mm(here, total)).astype(BF16)
        target[:, D:] = mm(here, product).astype(BF16)


def mixture_kernel(moves, info, hold, shared, value, mod, *refs):
    n_blk, own, micro = moves.n_blk, info[moves.slots], mod.shape[0]
    payload, gradients, refs = refs[:n_blk], refs[n_blk : 2 * n_blk], refs[2 * n_blk :]
    *other, keep, send, grad_gate = refs
    total = value[...]
    if other:
        total = total + other[0][...].astype(F32)
    total = total.astype(BF16)
    count = keep.shape[1]
    length = count // micro
    sums = [0.0] * micro
    for rel in range(n_blk):
        at = slice(rel * count, (rel + 1) * count)
        target = (send if rel % 2 else keep).at[rel // 2]
        gate = own_lanes(payload[rel][:, D:], own, n_blk)
        mixture = shared[at, :].astype(F32) + gate * mm(hold[at, :], total)
        target[...] = mixture.astype(BF16)
        product = mixture * gradients[rel][...].astype(F32)
        for m in range(micro):
            sums[m] = sums[m] + column_sum(product[m * length : (m + 1) * length])
    for m in range(micro):
        grad_gate[m] = sums[m]


def middle_kernel(
    moves, micro, info, near, far, probs, residual, attended, mixed, normed_two, mod, router, cotangent, *refs
):
    n_blk, own = moves.n_blk, info[moves.slots]
    out_weights, refs = refs[:n_blk], refs[n_blk:]
    grad_residual, grad_mod, grad_router, keep, send, grad_mixed, grad_attended, wide, blocks = refs
    part, half = D // n_blk, D // 2
    length = residual.shape[0] // micro
    given = cotangent[...].astype(F32)
    gates = probs[:, :n_blk]
    inner = from_thirds(near[:, D:], n_blk) + from_thirds(far[:, D:], n_blk)
    chosen = inner - gates * jnp.sum(inner, axis=-1, keepdims=True)
    grad_logits = jnp.concatenate(
        [chosen, jnp.zeros((chosen.shape[0], LANES - n_blk), F32)], axis=1
    ).astype(BF16)
    grad_router[...] = mm(grad_logits, normed_two[...], TN)
    grad_two = (
        near[:, :D].astype(F32)
        + far[:, :D].astype(F32)
        + mm(grad_logits, router[...])
    )
    for m in range(micro):
        rows = slice(m * length, (m + 1) * length)
        hat, inverse = normed(residual[rows, :])
        mine = grad_two[rows]
        grad_mod[m, 1:2, :] = column_sum(mine)
        grad_mod[m, 2:3, :] = column_sum(mine * hat)
        total = given[rows] + norm_back(hat, inverse, mine * (1.0 + mod[m, 4:5, :]))
        grad_residual[rows, :] = total
        grad_mod[m, 0:1, :] = column_sum(total * attended[rows, :])
        grad_attended[rows, :] = (total * mod[m, 2:3, :]).astype(BF16)
    for b in range(n_blk):
        blocks[b] = grad_attended[:, b * part : (b + 1) * part]
    left, right = 0.0, 0.0
    for rel in range(n_blk):
        weight, grad = out_weights[rel], blocks[own ^ rel]
        left = left + mm(grad, weight[:, :part], NT)
        right = right + mm(grad, weight[:, part:], NT)
    back_mixed = jnp.concatenate([left, right], axis=1).astype(BF16)
    for h in range(n_blk):
        for m in range(micro):
            grad_mixed[h, :, m * part : (m + 1) * part] = back_mixed[
                m * length : (m + 1) * length, h * part : (h + 1) * part
            ]
    all_mixed = mixed[...]
    for rel in range(n_blk):
        wide[...] = mm(all_mixed, blocks[own ^ rel], TN).astype(BF16)
        target = (send if rel % 2 else keep).at[rel // 2]
        groups = target.shape[0]
        for j in range(moves.slots):
            at = pl.ds(pl.multiple_of(info[j], moves.rows), moves.rows)
            start = j // groups * part
            target[j % groups, :, start : start + part] = wide[at, :]


def sum_kernel(count, left, right, *outs):
    for i in range(count):
        outs[i][0] = (left[i].astype(F32) + right[i].astype(F32)).astype(outs[i].dtype)


def last_kernel(first, second, third, fourth, left, right):
    total = first[0] + second[0].astype(F32) + third[0].astype(F32) + fourth[0].astype(F32)
    left[...] = total[:, : left.shape[1]]
    right[...] = total[:, left.shape[1] :]


def block_out_kernel(micro, near, far, residual, mod, block_out):
    mixture = near[...].astype(F32) + far[...].astype(F32)
    length = residual.shape[0] // micro
    for m in range(micro):
        rows = slice(m * length, (m + 1) * length)
        block_out[rows, :] = (residual[rows, :] + mod[m, 5:6, :] * mixture[rows]).astype(BF16)


def qkv_grad_kernel(moves, micro, maps, info, kept, near, far, out_near, out_far, normed_one, weight, *refs):
    n_blk, own = moves.n_blk, info[moves.slots]
    tokens, mod, refs = refs[:n_blk], refs[n_blk], refs[n_blk + 1 :]
    outs, refs = refs[: len(maps)], refs[len(maps) :]
    keep, send, grad_mod, arrived, blocks, wide = refs
    by_source(own, kept, near, far, arrived)
    part = D // n_blk
    length = arrived.shape[2]
    count = micro * length
    for j in range(3):
        source = (3 * own + j) % n_blk
        for b in range(n_blk):
            for m in range(micro):
                blocks[b, m * length : (m + 1) * length, j * part : (j + 1) * part] = arrived[
                    source, b, :, m * part : (m + 1) * part
                ]
    every = blocks[...].reshape(n_blk * count, 3 * part)
    wide[...] = mm(normed_one[...].reshape(n_blk * count, D), every, TN).astype(BF16)
    take_slots(moves, info, wide, outs, maps, 0)
    out_grad = (out_near[...].astype(F32) + out_far[...].astype(F32)).astype(BF16)
    groups = out_near.shape[0]
    for ref, slots in zip(outs, maps):
        for k, j in enumerate(slots):
            start = j // groups * part
            ref[k, :, 3 * part :] = out_grad[j % groups, :, start : start + part]
    sums = [[0.0, 0.0] for _ in range(micro)]
    for rel in range(n_blk):
        back = mm(blocks[own ^ rel], weight[...], NT)
        target = send if rel % 2 else keep
        target[rel // 2] = back.astype(BF16)
        for m in range(micro):
            rows = slice(m * length, (m + 1) * length)
            hat, _ = normed(tokens[rel][rows, :].astype(F32))
            sums[m][0] += column_sum(back[rows])
            sums[m][1] += column_sum(back[rows] * hat)
    for m in range(micro):
        for i in range(2):
            grad_mod[m, i : i + 1, :] = sums[m][i]


def tokens_grad_kernel(micro, near, far, tokens, mod, grad_residual, out):
    grad_one = near[...].astype(F32) + far[...].astype(F32)
    length = tokens.shape[0] // micro
    for m in range(micro):
        rows = slice(m * length, (m + 1) * length)
        hat, inverse = normed(tokens[rows, :].astype(F32))
        own = grad_one[rows]
        out[rows, :] = grad_residual[rows, :] + norm_back(hat, inverse, own * (1.0 + mod[m, 1:2, :]))


def by_tile(left, right, tile):
    parts = []
    for start in range(0, left.shape[1], tile):
        parts += [left[:, start : start + tile], right[:, start : start + tile]]
    return jnp.concatenate(parts, axis=1)


def from_tiles(packed, tile):
    parts = [
        [array[:, start : start + tile] for array in packed for start in range(first, array.shape[1], 2 * tile)]
        for first in (0, tile)
    ]
    return [jnp.concatenate(part, axis=1) for part in parts]


def block_specs(parts, tile):
    return [
        pl.BlockSpec((a.shape[0], a.shape[1], 2 * tile), lambda j, first=first: (0, 0, first + j))
        for a, first in parts
    ]


def held(shape):
    return pl.BlockSpec(shape, lambda j: (0,) * len(shape))


def on_device(moves, tokens, timesteps, routes, ada, qkv, out_w, router, shared_in, shared_out, expert_in, expert_out, cotangent):
    micro, _, length, _ = tokens.shape
    count = micro * length
    n_dp, n_blk, ring = moves.n_dp, moves.n_blk, moves.ring
    experts = n_blk
    capacity = length * TOP // experts + max(2, length // 32)
    room = -(-n_blk * micro * capacity // 16) * 16
    shard = D // n_dp
    part = D // n_blk
    info = moves.info()
    dp_at = lax.axis_index("dp")
    rotate, swap, flip = moves.rotate, moves.swap, moves.flip

    tokens_2d = tokens.reshape(count, D)
    given = cotangent.reshape(count, D)
    routes_2d = routes.reshape(count, TOP)

    pack_a = jnp.concatenate([qkv, out_w], axis=1)
    tile = shared_in.shape[1]
    pack_b = by_tile(shared_in, shared_out.T, tile)
    ff = expert_in.shape[2]
    e_out = expert_out[0].T
    shares = 2 if ring else 1
    first_half, last_half = (
        by_tile(expert_in[0][:, c : c + ff // 2], e_out[:, c : c + ff // 2], tile)
        for c in (0, ff // 2)
    )
    side = dp_at % 2 == 0


    half = D // 2
    column = jnp.arange(D)
    frequency = jnp.exp(-math.log(10000.0) * (column % half).astype(F32) / half)
    angles = timesteps.astype(F32) * frequency
    cond = jax.nn.silu(jnp.where(column < half, jnp.cos(angles), jnp.sin(angles))).astype(BF16)
    cond = cond.reshape(micro, n_dp, shard).transpose(1, 0, 2)
    cond = lax.all_to_all(cond, "dp", 0, 0, tiled=True)
    if ring:
        maps_a = [[0, 1, 2, 3], [4, 5, 6, 7]]
        cond, pack_a, pack_b, first_half, last_half, tokens_2d, given = together(
            cond, pack_a, pack_b, first_half, last_half, tokens_2d, given
        )
        a1, a2, a3 = rotate(pack_a, 1), rotate(pack_a, 2), rotate(pack_a, -1)
        e_own = jnp.where(side, first_half, last_half)
        e_across = swap(jnp.where(side, last_half, first_half))
    else:
        weights_a, maps_a = [moves.whole(pack_a)], [[0]]

    wide = ada.shape[1]
    partial_mod = jnp.einsum("dmr,rc->dmc", cond, ada, preferred_element_type=F32)
    payload = jnp.concatenate(
        [
            partial_mod.reshape(n_dp, micro * wide),
            jnp.broadcast_to(router[:, 0].astype(F32)[None], (n_dp, shard)),
        ],
        axis=1,
    )
    arrived = lax.all_to_all(payload, "dp", 0, 0, tiled=True)
    far_tokens = flip(tokens_2d, 2)
    if ring:
        arrived, far_tokens, e_own, e_across, a1, a2, a3, given = together(
            arrived, far_tokens, e_own, e_across, a1, a2, a3, given
        )
        held_a = jnp.stack([pack_a, a1, a2, a3])
        weights_a = [held_a, swap(held_a)]
        pack_0 = jnp.stack([e_own, e_across])
        pack_1 = rotate(pack_0, 1)
    tokens_all = [tokens_2d, flip(tokens_2d, 1), far_tokens, flip(far_tokens, 1)]
    own_mod = jnp.sum(arrived[:, : micro * wide], axis=0)
    own_mod = jnp.concatenate([own_mod, arrived[:, micro * wide :].reshape(D)])
    gathered = lax.all_gather(own_mod, "blk", axis=0)
    if ring:
        gathered, weights_a, tokens_all, given = together(gathered, weights_a, tokens_all, given)
    near_given = flip(given, 1)
    mod = gathered[:, : micro * wide].reshape(n_blk, micro, wide)
    mod = mod.transpose(1, 0, 2).reshape(micro, 6, D)
    router_t = jnp.pad(gathered[:, micro * wide :].astype(BF16), ((0, LANES - n_blk), (0, 0)))

    group = shaped((n_blk, length, micro * part), BF16)
    out_half = call(
        functools.partial(out_weight_kernel, moves, maps_a),
        shaped((D // 2, 2 * part), BF16),
        "out_weight",
        in_specs=[smem()] + [vmem()] * len(weights_a),
        scratch_shapes=[pltpu.VMEM((D, part), BF16)],
    )(info, *weights_a)
    out_weights = [out_half, flip(out_half, 1), flip(out_half, 2)]
    normed_one, qkv_w, kept, near, far = call(
        functools.partial(qkv_kernel, moves, micro, maps_a),
        [shaped((n_blk, count, D), BF16), shaped((D, 3 * part), BF16), group, group, group],
        "qkv",
        in_specs=[smem()] + [vmem()] * (n_blk + 1 + len(weights_a)),
    )(info, *tokens_all, mod, *weights_a)
    if ring:
        near, far, out_weights, near_given, given, pack_0, pack_1 = together(
            near, far, out_weights, near_given, given, pack_0, pack_1
        )
        pack_2 = rotate(pack_1, 1)
        b_across = swap(pack_b)
    near, far = flip(near, 1), flip(far, 2)
    out_weights.append(flip(out_weights[2], 1))
    if ring:
        near, far, out_weights, b_across, given = together(near, far, out_weights, b_across, given)
    projected = (kept, near, far)
    far_given = flip(given, 2)

    from_all = pltpu.VMEM((n_blk, n_blk, length, micro * part), BF16)
    mixed_out = call(
        functools.partial(attend_kernel, moves),
        group,
        "attend",
        in_specs=[smem()] + [vmem()] * 3,
        scratch_shapes=[from_all],
    )(info, *projected)
    mixed_in = lax.all_to_all(mixed_out, "blk", 0, 0, tiled=True)
    if ring:
        mixed_in, out_weights, pack_2, far_given = together(
            mixed_in, out_weights, pack_2, far_given
        )
        b_0 = jnp.stack([pack_b, b_across])
    given_all = [given, near_given, far_given, flip(far_given, 1)]
    if ring:
        pack_3 = rotate(pack_2, 1)
    columns = D + LANES
    mixed, attended, residual, normed_two, probs, payload = call(
        functools.partial(residual_kernel, moves, micro),
        [
            shaped((count, D), BF16),
            shaped((count, D), F32),
            shaped((count, D), F32),
            shaped((count, D), BF16),
            shaped((count, LANES), F32),
            shaped((count, columns), BF16),
        ],
        "residual",
        in_specs=[smem()] + [vmem()] * (5 + n_blk),
        scratch_shapes=[pltpu.VMEM((n_blk, count, part), F32)],
    )(info, mixed_in, tokens_2d, mod, router_t, routes_2d, *out_weights)
    payloads = [payload, flip(payload, 1), flip(payload, 2)]
    if ring:
        payloads, given_all, b_0 = together(payloads, given_all, b_0)
    payloads.append(flip(payloads[2], 1))
    all_count = n_blk * count
    all_grads, hold, rows = call(
        functools.partial(pick_kernel, moves),
        [shaped((all_count, D), BF16), shaped((all_count, room), BF16), shaped((room, 2 * D), BF16)],
        "pick",
        scratch_shapes=[pltpu.VMEM((room, all_count), BF16)],
        in_specs=[smem()] + [vmem()] * (2 * n_blk + 1),
    )(info, *payloads, *given_all, mod)

    if ring:
        rows, hold, all_grads, pack_3 = together(rows, hold, all_grads, pack_3)
        rows_across = swap(rows)
        b_1, b_2, b_3 = rotate(b_0, 1), rotate(b_0, 2), rotate(b_0, -1)
        parts_e = [(p, 0) for p in (pack_0, pack_1, pack_2, pack_3)]
        maps_e = [[s, ring + s] for s in range(ring)]
        maps_b = maps_e
        out_maps_b = [[0, 1, 2, 3], [4, 5, 6, 7]]
    else:
        parts_e = [(moves.whole(jnp.concatenate([first_half, last_half], axis=1)), 0)]
        parts_b = [(moves.whole(pack_b), 0)]
        maps_e, maps_b, out_maps_b = [[0]], [[0]], [[0]]
    tiles = [pltpu.VMEM((D, tile), BF16) for _ in range(4)]
    steps = ff // tile // shares

    def routed_part(other, given_rows, parts, before):
        results = [((room, D), F32)] * 2 + [((room, LANES), F32)]
        unrolled = steps if ring else 0
        if other:
            results = [((room, D), BF16), ((room, columns), BF16)]
        if ring:
            weight_specs = [vmem()] * len(parts)
            out_specs = [vmem()] * (len(results) + len(maps_e))
        else:
            weight_specs = block_specs(parts, tile)
            out_specs = [held(shape) for shape, _ in results] + weight_specs
        got = call(
            functools.partial(routed_kernel, moves, maps_e, maps_e, tile, bool(ring), unrolled, other),
            [shaped(*r) for r in results]
            + [shaped((len(m), moves.rows, 2 * tile * steps), BF16) for m in maps_e],
            "routed",
            vmem_mib=None if ring else 48,
            **({} if unrolled else {"grid": (steps,)}),
            in_specs=[smem(), vmem()] + weight_specs + [vmem()] * len(before),
            out_specs=out_specs,
            scratch_shapes=[pltpu.VMEM((room, D), F32)] * 2 + tiles,
        )(info, given_rows, *[a for a, _ in parts], *before)
        return got[: len(results)], got[len(results) :]

    (value, back, inner), got_e = routed_part(False, rows, parts_e, [])
    other_value, other_back = [], []
    if ring:
        got_e, rows_across, b_1 = together(got_e, rows_across, b_1)
        (send_value, send_back), got_e = routed_part(True, rows_across, parts_e, got_e)
        got_e, value, back, send_value, send_back, all_grads, b_2, b_3 = together(
            got_e, value, back, send_value, send_back, all_grads, b_2, b_3
        )
        other_back = [swap(send_back)]
        e_two, e_one = rotate(got_e[2], 1), rotate(got_e[1], -1)
        parts_b = [(b, 0) for b in (b_0, b_1, b_2, b_3)]
    slot_shape = (moves.rows, 2 * tile)
    got_b = call(
        functools.partial(shared_kernel, moves, maps_b, out_maps_b, tile),
        [shaped((all_count, D), BF16)] * 2
        + [shaped((len(m),) + slot_shape, BF16) for m in out_maps_b],
        "shared",
        in_specs=[smem()] + [vmem()] * (n_blk + 1 + len(parts_b)),
        scratch_shapes=[pltpu.VMEM((all_count, D), BF16)]
        + [pltpu.VMEM((all_count, D), F32)] * 2
        + tiles,
    )(info, *payloads, all_grads, *[a for a, _ in parts_b])
    shared, own_b, other_b = got_b[:2], got_b[2], got_b[-1]
    if ring:
        other_back, e_two, send_value, shared, own_b, other_b, got_e = together(
            other_back, e_two, send_value, shared, own_b, other_b, got_e
        )
        other_value = [swap(send_value)]
    keep, send = call(
        functools.partial(back_kernel, moves),
        [shaped((2, count, columns), BF16)] * 2,
        "back",
        in_specs=[smem()] + [vmem()] * (4 + len(other_back)),
    )(info, hold, shared[1], back, inner, *other_back)

    crossed = flip(send, 1)
    near, far = (add(keep[i], crossed[i]).astype(BF16) for i in range(2))
    far = flip(far, 2)
    if ring:
        e_three = add(got_e[3], e_two).astype(BF16)
        near, far, other_b, e_three = together(near, far, other_b, e_three)
        across_b = swap(other_b)

    halves = 2 if ring else 1
    out_rows = (2, moves.slots // halves, moves.rows, halves * part)
    grad_residual, grad_mod_two, grad_router, out_keep, out_send, grad_mixed = call(
        functools.partial(middle_kernel, moves, micro),
        [
            shaped((count, D), F32),
            shaped((micro, 3, D), F32),
            shaped((LANES, D), F32),
            shaped(out_rows, BF16),
            shaped(out_rows, BF16),
            group,
        ],
        "middle",
        in_specs=[smem()] + [vmem()] * (10 + n_blk),
        scratch_shapes=[
            pltpu.VMEM((count, D), BF16),
            pltpu.VMEM((D, part), BF16),
            pltpu.VMEM((n_blk, count, part), BF16),
        ],
    )(
        info, near, far, probs, residual, attended, mixed, normed_two, mod, router_t, given, *out_weights,
    )

    if ring:
        grad_mixed, out_send, e_one, e_three, other_value = together(
            grad_mixed, out_send, e_one, e_three, other_value
        )
        e_three = rotate(e_three, 1)
    grad_mixed = lax.all_to_all(grad_mixed, "blk", 0, 0, tiled=True)
    crossed = flip(out_send, 1)
    out_sums = [add(out_keep[i], crossed[i]).astype(BF16) for i in range(2)]
    if ring:
        grad_mixed, out_sums, across_b, own_b = together(grad_mixed, out_sums, across_b, own_b)
        sums_b = call(
            functools.partial(sum_kernel, ring),
            [shaped((1,) + slot_shape, BF16) for _ in range(ring)],
            "shared_sum",
        )(own_b, across_b)
    out_far = flip(out_sums[1], 2)
    kept, near, far = call(
        functools.partial(attend_back_kernel, moves),
        [group] * 3,
        "attend_back",
        in_specs=[smem()] + [vmem()] * 4,
        scratch_shapes=[from_all, from_all],
    )(info, *projected, grad_mixed)
    if ring:
        near, far, out_far, e_three, got_e, sums_b, value, other_value = together(
            near, far, out_far, e_three, got_e, sums_b, value, other_value
        )
        e_across = swap((add(got_e[0][1], e_one[1]) + e_three[1].astype(F32)).astype(BF16))
        b_parts = [rotate(sums_b[s], steps) for s, steps in ((2, 2), (1, -1), (3, 1))]
    near, far = flip(near, 1), flip(far, 2)
    if ring:
        near, far, value, other_value = together(near, far, value, other_value)
    got = call(
        functools.partial(qkv_grad_kernel, moves, micro, maps_a),
        [shaped(w.shape, BF16) for w in weights_a]
        + [shaped((2, count, D), BF16)] * 2
        + [shaped((micro, 2, D), F32)],
        "qkv_grad",
        in_specs=[smem()] + [vmem()] * (8 + n_blk),
        scratch_shapes=[
            from_all,
            pltpu.VMEM((n_blk, count, 3 * part), BF16),
            pltpu.VMEM((D, 3 * part), BF16),
        ],
    )(info, kept, near, far, out_sums[0], out_far, normed_one, qkv_w, *tokens_all, mod)
    qkv_parts, (one_keep, one_send, grad_mod_one) = got[:-3], got[-3:]
    if ring:
        qkv_parts, one_keep, one_send, grad_mod_one, e_across, b_parts[0] = together(
            qkv_parts, one_keep, one_send, grad_mod_one, e_across, b_parts[0]
        )
        qkv_across = swap(qkv_parts[1])

    crossed = flip(one_send, 1)
    one_near, one_far = (add(one_keep[i], crossed[i]).astype(BF16) for i in range(2))
    if ring:
        one_near, one_far = together(one_near, one_far)
    one_far = flip(one_far, 2)
    if ring:
        e_across = after(e_across, one_near).astype(F32)
        e_mine = add(got_e[0][0], e_one[0]) + e_three[0].astype(F32)
        sums_e = [jnp.where(side, e_mine, e_across), jnp.where(side, e_across, e_mine)]
        expert_in_grad, expert_out_t = from_tiles(sums_e, tile)
        expert_out_grad = expert_out_t.T
        one_near, one_far, qkv_across, qkv_parts, expert_in_grad, expert_out_grad, b_parts, sums_b, value = together(
            one_near, one_far, qkv_across, qkv_parts, expert_in_grad, expert_out_grad, b_parts, sums_b, value
        )
        mine = call(
            functools.partial(sum_kernel, ring),
            [shaped((1,) + qkv_across.shape[1:], BF16 if s else F32) for s in range(ring)],
            "slot_sum",
        )(qkv_parts[0], qkv_across)
        qkv_2, qkv_1, qkv_3 = (rotate(mine[s], steps) for s, steps in ((2, 2), (1, -1), (3, 1)))
        sums_b = (add(sums_b[0], b_parts[0]) + add(b_parts[1], b_parts[2]))[0]
    else:
        sums_b = moves.fold_whole(own_b[0])
        expert_in_grad, expert_out_t = from_tiles([moves.fold_whole(got_e[0][0])], tile)
        expert_out_grad = expert_out_t.T
    mix_keep, mix_send, grad_gate = call(
        functools.partial(mixture_kernel, moves),
        [shaped((2, count, D), BF16)] * 2 + [shaped((micro, 1, D), F32)],
        "mixture",
        in_specs=[smem()] + [vmem()] * (4 + 2 * n_blk + len(other_value)),
    )(info, hold, shared[0], value, mod, *payloads, *given_all, *other_value)
    mix_crossed = flip(mix_send, 1)

    grad_mod = jnp.concatenate([grad_mod_one, grad_mod_two, grad_gate], axis=1)
    grad_mod = grad_mod.reshape(micro, n_blk, wide)
    payload = jnp.concatenate(
        [
            jnp.broadcast_to(
                grad_mod.transpose(1, 0, 2).reshape(1, n_blk, micro * wide), (n_dp, n_blk, micro * wide)
            ),
            grad_router[:n_blk].reshape(n_blk, n_dp, shard).transpose(1, 0, 2),
        ],
        axis=2,
    ).reshape(n_dp * n_blk, -1)
    arrived = lax.all_to_all(payload, ("dp", "blk"), 0, 0, tiled=True)

    mix_total = [add(mix_keep[i], mix_crossed[i]).astype(BF16) for i in range(2)]
    mix_far = flip(mix_total[1], 2)
    tokens_grad = call(
        functools.partial(tokens_grad_kernel, micro),
        shaped((count, D), F32),
        "tokens_grad",
    )(one_near, one_far, tokens_2d, mod, grad_residual)
    shared_in_grad, shared_out_t = from_tiles([sums_b], tile)
    shared_out_grad = shared_out_t.T
    arrived = arrived.reshape(n_dp, n_blk, -1)
    item_mod = jnp.sum(arrived[:, :, : micro * wide], axis=1).reshape(n_dp * micro, wide)
    ada_grad = jnp.dot(
        cond.reshape(n_dp * micro, shard).astype(F32).T, item_mod, precision=lax.Precision.HIGHEST
    )
    router_grad = jnp.sum(arrived[:, :, micro * wide :], axis=(0, 1))[:, None]
    block_out = call(
        functools.partial(block_out_kernel, micro), shaped((count, D), BF16), "block_out"
    )(mix_total[0], mix_far, residual, mod)
    if ring:
        tokens_grad, block_out, qkv_1, qkv_2, qkv_3, ada_grad, router_grad, shared_in_grad, shared_out_grad = together(
            tokens_grad, block_out, qkv_1, qkv_2, qkv_3, ada_grad, router_grad, shared_in_grad, shared_out_grad
        )
        qkv_grad, out_grad = call(
            last_kernel,
            [shaped((shard, 3 * part), F32), shaped((shard, part), F32)],
            "last_sum",
        )(mine[0], qkv_1, qkv_2, qkv_3)
    else:
        last = moves.fold_whole(qkv_parts[0][0])
        qkv_grad, out_grad = last[:, : 3 * part], last[:, 3 * part :]
    return (
        block_out.reshape(tokens.shape),
        tokens_grad.reshape(tokens.shape),
        ada_grad,
        qkv_grad,
        out_grad,
        router_grad,
        shared_in_grad,
        shared_out_grad,
        expert_in_grad[None],
        expert_out_grad[None],
    )


def solution(mesh):
    moves = Moves(mesh)
    in_specs = (
        P(None, "dp", "blk", None),
        P(None, "dp"),
        P(None, "dp", "blk", None),
        P("dp", "blk"),
        P("dp", "blk"),
        P("dp", "blk"),
        P("dp", "blk"),
        P("dp", "blk"),
        P("blk", "dp"),
        P("blk", "dp", None),
        P("blk", None, "dp"),
        P(None, "dp", "blk", None),
    )
    out_specs = (
        P(None, "dp", "blk", None),
        P(None, "dp", "blk", None),
        P("dp", "blk"),
        P("dp", "blk"),
        P("dp", "blk"),
        P("dp", "blk"),
        P("dp", "blk"),
        P("blk", "dp"),
        P("blk", "dp", None),
        P("blk", None, "dp"),
    )
    return jax.shard_map(
        functools.partial(on_device, moves),
        mesh=mesh,
        in_specs=in_specs,
        out_specs=out_specs,
        check_vma=False,
    )
```
